256 devices in a mesh: grp: 8 (over z_hi, core), shard: 32 (over y, x, z_lo).
Axes of the slice: x: 4, y: 4, z: 8 (z_hi: 4, z_lo: 2; z = z_hi * 2 + z_lo), core: 2. Of those that a mesh axis runs over, the one named last changes fastest.
Arguments:
- embeddings: bfloat16 [262144, 768], P(('grp', 'shard')), may hold values from -0.26 to 0.26
- centers: bfloat16 [2048, 768], P('shard'), may hold values from -0.26 to 0.26
- assignment: int32 [262144, 1], P(('grp', 'shard')), may hold values from 0 to 2047, as said below
Outputs:
- old_min: float32 [262144], P(('grp', 'shard'))
- refined_centers: float32 [2048, 768], P('shard')
- new_min: float32 [262144], P(('grp', 'shard'))
The draws below stay inside these ranges and needn't reach their ends.
Inputs may be any that keep to these rules, and one draw needn't show every extreme that they name: `assignment`: every cluster is named by at least one row; cluster k belongs to the index of shard that holds centers[k]; the rows of one device name clusters belonging to any one index of shard at least 16 and at most 64 times, and in every group one index of shard is named 64 times by the rows of each device of that group.
All inputs are finite; a program needn't handle non-finite values.
Results may differ from the reference program's by a relative error of at most 0.0003.
Values may be sent and summed in bfloat16 or wider, within the bound.
No kernel may reach another device: no remote copies, remote signals or barrier semaphores. Data moves between devices by JAX's collectives and lax.ppermute only.
A program may use at most 64 MiB of HBM per device.

```python
import math
import jax
import jax.numpy as jnp
from jax import lax

D = 768
K = 2048
ROW_DEV = 1024
ROWS = 262144
N_GRP = 8
N_SHARD = 32


def owner_layout(key):
    key = jax.random.fold_in(key, 101)
    keys = jax.random.split(key, 6)
    devices_all = N_GRP * N_SHARD
    most = 2 * ROW_DEV // N_SHARD
    fewest = ROW_DEV // (2 * N_SHARD)
    extra = ROW_DEV - most - (N_SHARD - 1) * fewest
    owned = K // N_SHARD
    group_full = jax.random.randint(keys[0], (N_GRP,), 0, N_SHARD).astype(jnp.int32)
    full = jnp.repeat(group_full, N_SHARD)
    others = jnp.arange(N_SHARD - 1, dtype=jnp.int32)[None, :]
    others = others + (others >= full[:, None]).astype(jnp.int32)
    fewest_part = jnp.repeat(others, fewest, axis=1)
    spare_pool = jnp.repeat(others, most - fewest, axis=1)
    pool_keys = jax.random.split(keys[1], devices_all)
    shuffled = jax.vmap(jax.random.permutation)(pool_keys, spare_pool)
    full_part = jnp.broadcast_to(full[:, None], (devices_all, most))
    tickets = jnp.concatenate([full_part, fewest_part, shuffled[:, :extra]], axis=1)
    row_keys = jax.random.split(keys[2], devices_all)
    owner = jax.vmap(jax.random.permutation)(row_keys, tickets).reshape(-1).astype(jnp.int32)
    owner_hot = (owner[:, None] == jnp.arange(N_SHARD, dtype=jnp.int32)[None, :]).astype(jnp.int32)
    ranked = jnp.sum(jnp.cumsum(owner_hot, axis=0) * owner_hot, axis=1) - 1
    rotate = jax.random.randint(keys[3], (N_SHARD,), 0, owned).astype(jnp.int32)
    loose = jnp.minimum(jax.random.randint(keys[4], (ROWS,), 0, owned), jax.random.randint(keys[5], (ROWS,), 0, owned)).astype(jnp.int32)
    within = jnp.where(ranked < owned, ranked, loose)
    within = (within + rotate[owner]) % owned
    return (owner * owned + within).astype(jnp.int32)


def cluster_bases(key):
    key = jax.random.fold_in(key, 202)
    keys = jax.random.split(key, 4)
    gauss = jnp.clip(jax.random.normal(keys[0], (K, D), jnp.float32), -3.5, 3.5)
    order = jax.random.permutation(keys[3], K).astype(jnp.int32)
    return (gauss, order)


def draw_assignment(key, part):
    labels = owner_layout(key)
    return labels[:, None]


def draw_embeddings(key, part):
    labels = owner_layout(key)
    gauss, order = cluster_bases(key)
    key = jax.random.fold_in(key, 5)
    keys = jax.random.split(key, 4)
    stale = jax.random.randint(keys[2], (ROWS,), 0, 100) < 35
    elsewhere = jax.random.randint(keys[3], (ROWS,), 0, K).astype(jnp.int32)
    source = jnp.where(stale, elsewhere, labels).astype(jnp.int32)
    middle = 0.03 * gauss
    spread = jnp.exp(jax.random.uniform(keys[0], (ROWS, 1), jnp.float32, math.log(0.012), math.log(0.036)))
    noise = jnp.clip(jax.random.normal(keys[1], (ROWS, D), jnp.float32), -4.0, 4.0)
    return (middle[source] + spread * noise).astype(jnp.bfloat16)


def draw_centers(key, part):
    gauss, order = cluster_bases(key)
    key = jax.random.fold_in(key, 7)
    keys = jax.random.split(key, 2)
    middle = 0.03 * gauss
    spread = jnp.exp(jax.random.uniform(keys[0], (K, 1), jnp.float32, math.log(0.012), math.log(0.036)))
    noise = jnp.clip(jax.random.normal(keys[1], (K, D), jnp.float32), -4.0, 4.0)
    return (middle[order] + spread * noise).astype(jnp.bfloat16)


def setup_inputs(seed: int = 0) -> dict:
    key_list = jax.random.split(jax.random.key(seed), 4)
    embeddings = draw_embeddings(jax.random.fold_in(key_list[3], 71), 0)
    centers = draw_centers(jax.random.fold_in(key_list[3], 71), 0)
    assignment = draw_assignment(jax.random.fold_in(key_list[3], 71), 0)
    return {"embeddings": embeddings, "centers": centers, "assignment": assignment}


def nearest_old(embeddings, centers_b):
    center_norms = jnp.sum(jnp.square(centers_b.astype(jnp.float32)), 1)
    blocks = embeddings.reshape(-1, ROW_DEV, D)

    def one_block(block_rows):
        row_norms = jnp.sum(jnp.square(block_rows.astype(jnp.float32)), 1)
        products = jnp.dot(block_rows, centers_b.T, preferred_element_type=jnp.float32)
        distance = row_norms[:, None] - 2.0 * products + center_norms[None, :]
        return jnp.min(distance, 1)

    return lax.map(one_block, blocks).reshape(-1)


def nearest_new(embeddings, refined):
    center_norms = jnp.sum(jnp.square(refined), 1)
    blocks = embeddings.reshape(-1, ROW_DEV, D)

    def one_block(block_rows):
        wide_rows = block_rows.astype(jnp.float32)
        row_norms = jnp.sum(jnp.square(wide_rows), 1)
        products = jnp.dot(wide_rows, refined.T, precision=lax.Precision.HIGHEST, preferred_element_type=jnp.float32)
        distance = row_norms[:, None] - 2.0 * products + center_norms[None, :]
        return jnp.min(distance, 1)

    return lax.map(one_block, blocks).reshape(-1)


def reference(embeddings, centers, assignment):
    old_min = nearest_old(embeddings, centers)
    labels = assignment[:, 0].astype(jnp.int32)
    totals = jax.ops.segment_sum(embeddings.astype(jnp.float32), labels, num_segments=K)
    counts = jax.ops.segment_sum(jnp.ones((labels.shape[0],), jnp.float32), labels, num_segments=K)
    refined_centers = totals / counts[:, None]
    new_min = nearest_new(embeddings, refined_centers)
    return old_min, refined_centers, new_min
```

```python
import jax
import jax.numpy as jnp
from jax import lax
from jax.experimental import pallas as pl
from jax.experimental.pallas import tpu as pltpu
from jax.sharding import Mesh, PartitionSpec as P

AXES = ("zh", "core", "y", "x", "zl")
SIZES = (4, 2, 4, 4, 2)
SHARD = ("y", "x", "zl")

D = 768
HALF = 32
CHUNKS = 32
COLS = D // 128
BODY = COLS * HALF
CODED = BODY + 16
LIMIT = 32700.0
VMEM = 48 * 1024 * 1024


def diagonal(rows):
    r = lax.broadcasted_iota(jnp.int32, (rows, 128), 0) % HALF
    c = lax.broadcasted_iota(jnp.int32, (rows, 128), 1)
    return r == c


def to_lanes(column):
    return jnp.sum(jnp.where(diagonal(HALF), column, 0.0), 0, keepdims=True)


def to_column(row):
    return jnp.sum(jnp.where(diagonal(HALF), row, 0.0), 1, keepdims=True)


def code_of(values):
    most = jnp.max(jnp.abs(values), 1, keepdims=True)
    return jnp.ceil(jnp.log2(jnp.maximum(most, 1e-30)) * 256.0)


def quantize(values, code):
    scaled = values * (LIMIT * jnp.exp2(code * (-1.0 / 256.0)))
    return jnp.floor(scaled + 0.5).astype(jnp.int32).astype(jnp.int16)


def scale_of(code):
    return jnp.exp2(code * (1.0 / 256.0)) * (1.0 / LIMIT)


def footer(counts, codes):
    r = lax.broadcasted_iota(jnp.int32, (16, 128), 0)
    both = jnp.where(r == 0, counts, jnp.where(r == 1, codes, 0.0))
    return both.astype(jnp.int32).astype(jnp.int16)


def partial_kernel(base_ref, lab_a, lab_b, rows_a, rows_b, out_ref):
    tile = 128

    def step(t, carry):
        j = t * tile + lax.broadcasted_iota(jnp.int32, (tile, 1), 0)
        k = j + (j // HALF) * HALF + base_ref[0]
        hot_a = jnp.where(k == lab_a[...], 1.0, 0.0)
        hot_b = jnp.where(k == lab_b[...], 1.0, 0.0)
        sums = jnp.dot(
            hot_a.astype(jnp.bfloat16), rows_a[...], preferred_element_type=jnp.float32
        ) + jnp.dot(
            hot_b.astype(jnp.bfloat16), rows_b[...], preferred_element_type=jnp.float32
        )
        counts = jnp.sum(hot_a + hot_b, 1, keepdims=True)
        code = code_of(sums)
        coded = quantize(sums, code)
        for c in range(tile // HALF):
            at = t * (tile // HALF) + c
            part = slice(c * HALF, (c + 1) * HALF)
            for b in range(COLS):
                out_ref[at, b * HALF : (b + 1) * HALF, :] = coded[
                    part, b * 128 : (b + 1) * 128
                ]
            out_ref[at, BODY:CODED, :] = footer(
                to_lanes(counts[part]), to_lanes(code[part])
            )
        return carry

    lax.fori_loop(0, CHUNKS * HALF // tile, step, 0)


def gather_sums_kernel(in_ref, out_ref):
    def step(s, carry):
        blocks, counts = carry
        foot = in_ref[s, BODY:CODED, :].astype(jnp.float32)
        scale = scale_of(to_column(foot[1:2, :]))
        blocks = tuple(
            blocks[b]
            + in_ref[s, b * HALF : (b + 1) * HALF, :].astype(jnp.float32) * scale
            for b in range(COLS)
        )
        return blocks, counts + foot[0:1, :]

    zeros = tuple(jnp.zeros((HALF, 128), jnp.float32) for _ in range(COLS))
    blocks, counts = lax.fori_loop(
        0, CHUNKS, step, (zeros, jnp.zeros((1, 128), jnp.float32))
    )
    for b in range(COLS):
        out_ref[b * HALF : (b + 1) * HALF, :] = blocks[b]
    out_ref[BODY : BODY + 8, :] = jnp.broadcast_to(counts, (8, 128))


def refine_kernel(own, one, two, three, refined_ref, coded_ref):
    total = own[...] + one[...] + two[...] + three[...]
    counts = to_column(total[BODY : BODY + 1, :])
    refined = [total[b * HALF : (b + 1) * HALF, :] / counts for b in range(COLS)]
    for b in range(COLS):
        refined_ref[:, b * 128 : (b + 1) * 128] = refined[b]
    most = refined[0]
    for b in range(COLS):
        most = jnp.maximum(jnp.abs(most), jnp.abs(refined[b]))
    code = code_of(most)
    coded = [quantize(refined[b], code) for b in range(COLS)]
    foot = footer(to_lanes(jnp.zeros_like(code)), to_lanes(code))

    def step(s, carry):
        for b in range(COLS):
            coded_ref[s, b * HALF : (b + 1) * HALF, :] = coded[b]
        coded_ref[s, BODY:CODED, :] = foot
        return carry

    lax.fori_loop(0, CHUNKS, step, 0)


def rows_dot(centers, rows):
    return lax.dot_general(
        centers, rows, (((1,), (1,)), ((), ())), preferred_element_type=jnp.float32
    )


def nearest(value, least):
    n = value.shape[0]
    return jnp.minimum(least, jnp.min(value.reshape(n // 8, 8, value.shape[1]), 0))


def old_kernel(norms_ref, rows_ref, own_ref, other_ref, out_ref):
    tile = 256
    rows = rows_ref[...] * jnp.bfloat16(-2.0)
    least = jnp.full((8, rows.shape[0]), jnp.inf, jnp.float32)
    for ref in (own_ref, other_ref):

        def step(t, least, ref=ref):
            part = ref[pl.ds(pl.multiple_of(t * tile, tile), tile), :]
            wide = part.astype(jnp.float32)
            norm = jnp.sum(wide * wide, 1, keepdims=True)
            return nearest(rows_dot(part, rows) + norm, least)

        least = lax.fori_loop(0, ref.shape[0] // tile, step, least)
    out_ref[...] = norms_ref[...] + jnp.min(least, 0, keepdims=True)


def new_kernel(rows_ref, coded_ref, least_ref, out_ref):
    per = 8
    rows = rows_ref[...] * jnp.bfloat16(-2.0)

    def step(t, least):
        high, low, scale, norm = [], [], [], []
        for c in range(per):
            at = t * per + c
            wide = jnp.concatenate(
                [
                    coded_ref[at, b * HALF : (b + 1) * HALF, :].astype(jnp.float32)
                    for b in range(COLS)
                ],
                1,
            )
            top = wide.astype(jnp.bfloat16)
            high.append(top)
            low.append((wide - top.astype(jnp.float32)).astype(jnp.bfloat16))
            foot = coded_ref[at, BODY:CODED, :].astype(jnp.float32)
            s = scale_of(to_column(foot[1:2, :]))
            scale.append(s)
            norm.append(jnp.sum(wide * wide, 1, keepdims=True) * (s * s))
        product = rows_dot(jnp.concatenate(high, 0), rows) + rows_dot(
            jnp.concatenate(low, 0), rows
        )
        value = product * jnp.concatenate(scale, 0) + jnp.concatenate(norm, 0)
        return nearest(value, least)

    out_ref[...] = lax.fori_loop(0, CHUNKS // per, step, least_ref[...])


def call(kernel, out_shape, *args, flops=0, moved=0, smem=0):
    specs = [
        pl.BlockSpec(memory_space=pltpu.SMEM if i < smem else pltpu.VMEM)
        for i in range(len(args))
    ]
    many = isinstance(out_shape, tuple)
    out_specs = pl.BlockSpec(memory_space=pltpu.VMEM)
    return pl.pallas_call(
        kernel,
        out_shape=out_shape,
        in_specs=specs,
        out_specs=tuple([out_specs] * len(out_shape)) if many else out_specs,
        compiler_params=pltpu.CompilerParams(vmem_limit_bytes=VMEM),
        cost_estimate=pl.CostEstimate(
            flops=flops, bytes_accessed=moved, transcendentals=0
        ),
    )(*args)


def ring(axis, size, k):
    return [(i, (i + k) % size) for i in range(size)]


def swap(value, axis):
    return lax.ppermute(value, axis, [(0, 1), (1, 0)])


def gather_centers(part):
    part = jnp.concatenate([part, swap(part, "zl")])
    for axis in ("x", "y"):
        part = jnp.concatenate(
            [part] + [lax.ppermute(part, axis, ring(axis, 4, k)) for k in (1, 2, 3)]
        )
    return part


def on_device(embeddings, centers, assignment):
    n = embeddings.shape[0]
    core = lax.axis_index("core")
    f32, i16 = jnp.float32, jnp.int16
    labels = assignment.reshape(1, n)
    other_labels = swap(labels, "core")
    other_rows = swap(embeddings, "core")

    mine = lax.dynamic_slice(centers, (core * HALF, 0), (HALF, D))
    old_own = gather_centers(mine)
    old_other = swap(old_own, "core")

    wide = embeddings.astype(f32)
    norms = jnp.sum(wide * wide, 1).reshape(1, n)

    base = (core * HALF).astype(jnp.int32).reshape(1)
    sums = call(
        partial_kernel,
        jax.ShapeDtypeStruct((CHUNKS, CODED, 128), i16),
        base, labels, other_labels, embeddings, other_rows,
        flops=2 * 1024 * 2 * n * D, moved=6 << 20, smem=1,
    )
    sums = lax.all_to_all(sums, SHARD, 0, 0)
    group = call(
        gather_sums_kernel,
        jax.ShapeDtypeStruct((BODY + 8, 128), f32),
        sums,
        flops=1 << 22, moved=2 << 20,
    )
    others = [lax.ppermute(group, "zh", ring("zh", 4, k)) for k in (1, 2, 3)]
    refined, coded = call(
        refine_kernel,
        (
            jax.ShapeDtypeStruct((HALF, D), f32),
            jax.ShapeDtypeStruct((CHUNKS, CODED, 128), i16),
        ),
        group, *others,
        flops=1 << 20, moved=2 << 20,
    )
    refined_other = swap(refined, "core")
    first = core == 0
    refined_centers = jnp.concatenate(
        [
            jnp.where(first, refined, refined_other),
            jnp.where(first, refined_other, refined),
        ]
    )
    new_own = lax.all_to_all(coded, SHARD, 0, 0)
    new_other = swap(new_own, "core")

    old_min = call(
        old_kernel,
        jax.ShapeDtypeStruct((1, n), f32),
        norms, embeddings, old_own, old_other,
        flops=2 * 2048 * n * D, moved=5 << 20,
    )

    least = jnp.full((8, n), jnp.inf, f32)
    for coded in (new_own, new_other):
        least = call(
            new_kernel,
            jax.ShapeDtypeStruct((8, n), f32),
            embeddings, coded, least,
            flops=2 * 2048 * n * D, moved=3 << 20,
        )
    new_min = norms[0] + jnp.min(least, 0)
    return old_min.reshape(n), refined_centers, new_min


def solution(mesh):
    fine = Mesh(mesh.devices.reshape(SIZES), AXES)
    rows = ("zh", "core") + SHARD
    return jax.shard_map(
        on_device,
        mesh=fine,
        in_specs=(P(rows, None), P(SHARD, None), P(rows, None)),
        out_specs=(P(rows), P(SHARD, None), P(rows)),
        check_vma=False,
    )
```

```python
import jax
import jax.numpy as jnp
from jax import lax
from jax.experimental import pallas as pl
from jax.experimental.pallas import tpu as pltpu
from jax.sharding import Mesh, PartitionSpec as P

AXES = ("zh", "core", "y", "x", "zl")
SIZES = (4, 2, 4, 4, 2)
SHARD = ("y", "x", "zl")

D = 768
HALF = 32
CHUNKS = 32
COLS = D // 128
BODY = COLS * HALF
CODED = BODY + 16
LIMIT = 32700.0
VMEM = 16 * 1024 * 1024


def diagonal(rows):
    r = lax.broadcasted_iota(jnp.int32, (rows, 128), 0) % HALF
    c = lax.broadcasted_iota(jnp.int32, (rows, 128), 1)
    return r == c


def to_lanes(column):
    return jnp.sum(jnp.where(diagonal(HALF), column, 0.0), 0, keepdims=True)


def to_column(row):
    return jnp.sum(jnp.where(diagonal(HALF), row, 0.0), 1, keepdims=True)


def code_of(values):
    most = jnp.max(jnp.abs(values), 1, keepdims=True)
    return jnp.ceil(jnp.log2(jnp.maximum(most, 1e-30)) * 256.0)


def quantize(values, code):
    scaled = values * (LIMIT * jnp.exp2(code * (-1.0 / 256.0)))
    return jnp.floor(scaled + 0.5).astype(jnp.int32).astype(jnp.int16)


def scale_of(code):
    return jnp.exp2(code * (1.0 / 256.0)) * (1.0 / LIMIT)


def footer(counts, codes):
    r = lax.broadcasted_iota(jnp.int32, (16, 128), 0)
    both = jnp.where(r == 0, counts, jnp.where(r == 1, codes, 0.0))
    return both.astype(jnp.int32).astype(jnp.int16)


TILE = 256


def is_named(t, base, labels):
    j = t * TILE + lax.broadcasted_iota(jnp.int32, (TILE, 1), 0)
    k = j + (j // HALF) * HALF + base
    return jnp.where(k == labels, 1.0, 0.0)


def own_sums_kernel(base_ref, labels, rows, out_ref):
    for t in range(CHUNKS * HALF // TILE):
        hot = is_named(t, base_ref[0], labels[...]).astype(jnp.bfloat16)
        out_ref[t * TILE : (t + 1) * TILE, :] = jnp.dot(
            hot, rows[...], preferred_element_type=jnp.float32
        )


def chip_sums_kernel(base_ref, own_labels, labels, own_sums, rows, out_ref):
    for t in range(CHUNKS * HALF // TILE):
        hot = is_named(t, base_ref[0], labels[...])
        sums = own_sums[t * TILE : (t + 1) * TILE, :] + jnp.dot(
            hot.astype(jnp.bfloat16), rows[...], preferred_element_type=jnp.float32
        )
        hot = hot + is_named(t, base_ref[0], own_labels[...])
        counts = jnp.sum(hot, 1, keepdims=True)
        code = code_of(sums)
        coded = quantize(sums, code)
        for c in range(TILE // HALF):
            at = t * (TILE // HALF) + c
            part = slice(c * HALF, (c + 1) * HALF)
            for b in range(COLS):
                out_ref[at, b * HALF : (b + 1) * HALF, :] = coded[
                    part, b * 128 : (b + 1) * 128
                ]
            out_ref[at, BODY:CODED, :] = footer(
                to_lanes(counts[part]), to_lanes(code[part])
            )


def block(b):
    return slice(b * HALF, (b + 1) * HALF)


def add_coded(ref, at, blocks, counts):
    foot = ref[at, BODY:CODED, :].astype(jnp.float32)
    scale = scale_of(to_column(foot[1:2, :]))
    blocks = [
        blocks[b] + ref[at, block(b), :].astype(jnp.float32) * scale
        for b in range(COLS)
    ]
    return blocks, counts + foot[0:1, :]


def nothing():
    zeros = [jnp.zeros((HALF, 128), jnp.float32) for _ in range(COLS)]
    return zeros, jnp.zeros((1, 128), jnp.float32)


def code_blocks(blocks):
    most = jnp.abs(blocks[0])
    for b in range(1, COLS):
        most = jnp.maximum(most, jnp.abs(blocks[b]))
    code = code_of(most)
    return [quantize(blocks[b], code) for b in range(COLS)], to_lanes(code)


def group_kernel(in_ref, c0, c1, c2, c3, out_ref, centers_ref):
    together = 8

    def step(t, carry):
        blocks, counts = list(carry[0]), carry[1]
        for i in range(together):
            blocks, counts = add_coded(in_ref, t * together + i, blocks, counts)
        return tuple(blocks), counts

    blocks, counts = nothing()
    blocks, counts = lax.fori_loop(0, CHUNKS // together, step, (tuple(blocks), counts))
    coded, codes = code_blocks(blocks)
    for b in range(COLS):
        out_ref[0, block(b), :] = coded[b]
    out_ref[0, BODY:CODED, :] = footer(counts, codes)
    for i, ref in enumerate((c0, c1, c2, c3)):
        n = ref.shape[0]
        centers_ref[i * n : (i + 1) * n, :] = ref[...]


def refine_kernel(own, one, two, three, refined_ref, coded_ref):
    even = add_coded(two, 0, *add_coded(own, 0, *nothing()))
    odd = add_coded(three, 0, *add_coded(one, 0, *nothing()))
    counts = to_column(even[1] + odd[1])
    refined = [(even[0][b] + odd[0][b]) / counts for b in range(COLS)]
    for b in range(COLS):
        refined_ref[:, b * 128 : (b + 1) * 128] = refined[b]
    coded, codes = code_blocks(refined)
    foot = footer(jnp.zeros_like(codes), codes)

    def step(s, carry):
        for b in range(COLS):
            coded_ref[s, block(b), :] = coded[b]
        coded_ref[s, BODY:CODED, :] = foot
        return carry

    lax.fori_loop(0, CHUNKS, step, 0)


def nearest(value, least):
    n = value.shape[0]
    return jnp.minimum(least, jnp.min(value.reshape(n // 8, 8, value.shape[1]), 0))


def old_kernel(norms_ref, rows_ref, *refs):
    *centers, out_ref, turned_ref = refs
    turned_ref[...] = (rows_ref[...] * jnp.bfloat16(-2.0)).T
    turned = turned_ref[...]
    least = jnp.full((8, turned.shape[1]), jnp.inf, jnp.float32)
    for ref in centers:
        wide = ref[...].astype(jnp.float32)
        norm = jnp.sum(wide * wide, 1, keepdims=True)
        product = jnp.dot(ref[...], turned, preferred_element_type=jnp.float32)
        least = nearest(product + norm, least)
    out_ref[...] = norms_ref[...] + jnp.min(least, 0, keepdims=True)


def new_kernel(turned_ref, coded_ref, norms_ref, least_ref, out_ref):
    per = TILE // HALF
    turned = turned_ref[...]
    least = least_ref[...]
    for t in range(CHUNKS // per):
        high, low, scale, norm = [], [], [], []
        for c in range(per):
            at = t * per + c
            wide = jnp.concatenate(
                [coded_ref[at, block(b), :].astype(jnp.float32) for b in range(COLS)], 1
            )
            top = wide.astype(jnp.bfloat16)
            high.append(top)
            low.append((wide - top.astype(jnp.float32)).astype(jnp.bfloat16))
            foot = coded_ref[at, BODY:CODED, :].astype(jnp.float32)
            s = scale_of(to_column(foot[1:2, :]))
            scale.append(s)
            norm.append(jnp.sum(wide * wide, 1, keepdims=True) * (s * s))
        product = jnp.dot(
            jnp.concatenate(high, 0), turned, preferred_element_type=jnp.float32
        ) + jnp.dot(jnp.concatenate(low, 0), turned, preferred_element_type=jnp.float32)
        value = product * jnp.concatenate(scale, 0) + jnp.concatenate(norm, 0)
        least = nearest(value, least)
    if out_ref.shape == least.shape:
        out_ref[...] = least
    else:
        out_ref[...] = norms_ref[...] + jnp.min(least, 0, keepdims=True)


def call(kernel, out_shape, *args, flops=0, moved=0, smem=0):
    specs = [
        pl.BlockSpec(memory_space=pltpu.SMEM if i < smem else pltpu.VMEM)
        for i in range(len(args))
    ]
    many = isinstance(out_shape, tuple)
    out_specs = pl.BlockSpec(memory_space=pltpu.VMEM)
    return pl.pallas_call(
        kernel,
        out_shape=out_shape,
        in_specs=specs,
        out_specs=tuple([out_specs] * len(out_shape)) if many else out_specs,
        compiler_params=pltpu.CompilerParams(vmem_limit_bytes=VMEM),
        cost_estimate=pl.CostEstimate(
            flops=flops, bytes_accessed=moved, transcendentals=0
        ),
    )(*args)


def ring(axis, size, k):
    return [(i, (i + k) % size) for i in range(size)]


def swap(value, axis):
    return lax.ppermute(value, axis, [(0, 1), (1, 0)])


def around(part, axis):
    return [part] + [lax.ppermute(part, axis, ring(axis, 4, k)) for k in (1, 2, 3)]


def after(first, values):
    return lax.optimization_barrier((first, *values))[1:]


def on_device(embeddings, centers, assignment):
    n = embeddings.shape[0]
    core = lax.axis_index("core")
    f32, bf16, i16 = jnp.float32, jnp.bfloat16, jnp.int16
    shape = jax.ShapeDtypeStruct
    labels = assignment.reshape(1, n)
    other_labels = swap(labels, "core")
    other_rows = swap(embeddings, "core")

    mine = lax.dynamic_slice(centers, (core * HALF, 0), (HALF, D))
    current = around(jnp.concatenate([mine, swap(mine, "zl")]), "x")

    wide = embeddings.astype(f32)
    norms = jnp.sum(wide * wide, 1).reshape(1, n)

    base = (core * HALF).astype(jnp.int32).reshape(1)
    sums = call(
        own_sums_kernel,
        shape((CHUNKS * HALF, D), f32),
        base, labels, embeddings,
        flops=2 * 1024 * n * D, moved=5 << 20, smem=1,
    )
    sums = call(
        chip_sums_kernel,
        shape((CHUNKS, CODED, 128), i16),
        base, labels, other_labels, sums, other_rows,
        flops=2 * 1024 * n * D, moved=6 << 20, smem=1,
    )
    sums = lax.all_to_all(sums, SHARD, 0, 0)
    group, current = call(
        group_kernel,
        (shape((1, CODED, 128), i16), shape((8 * HALF, D), bf16)),
        sums, *current,
        flops=1 << 22, moved=2 << 20,
    )
    current = around(current, "y")
    groups, current[1], current[3] = lax.optimization_barrier(
        (around(group, "zh"), current[1], current[3])
    )
    refined, coded = call(
        refine_kernel,
        (shape((HALF, D), f32), shape((CHUNKS, CODED, 128), i16)),
        *groups,
        flops=1 << 20, moved=2 << 20,
    )
    new_own = lax.all_to_all(coded, SHARD, 0, 0)

    current = after(coded, current)
    current = current + tuple(swap(part, "core") for part in current)
    old_min, turned = call(
        old_kernel,
        (shape((1, n), f32), shape((D, n), bf16)),
        norms, embeddings, *current,
        flops=2 * 2048 * n * D, moved=5 << 20,
    )

    refined_other = swap(refined, "core")
    first = core == 0
    refined_centers = jnp.concatenate(
        [
            jnp.where(first, refined, refined_other),
            jnp.where(first, refined_other, refined),
        ]
    )

    (new_own,) = after(turned, (new_own,))
    new_other = swap(new_own, "core")
    least = jnp.full((8, n), jnp.inf, f32)
    for coded, result in ((new_own, 8), (new_other, 1)):
        least = call(
            new_kernel,
            shape((result, n), f32),
            turned, coded, norms, least,
            flops=2 * 2048 * n * D, moved=3 << 20,
        )
    return old_min.reshape(n), refined_centers, least.reshape(n)


def solution(mesh):
    fine = Mesh(mesh.devices.reshape(SIZES), AXES)
    rows = ("zh", "core") + SHARD
    return jax.shard_map(
        on_device,
        mesh=fine,
        in_specs=(P(rows, None), P(SHARD, None), P(rows, None)),
        out_specs=(P(rows), P(SHARD, None), P(rows)),
        check_vma=False,
    )
```

```python
import jax
import jax.numpy as jnp
from jax import lax
from jax.experimental import pallas as pl
from jax.experimental.pallas import tpu as pltpu
from jax.sharding import Mesh, PartitionSpec as P

AXES = ("zh", "core", "y", "x", "zl")
SIZES = (4, 2, 4, 4, 2)
SHARD = ("y", "x", "zl")

D = 768
HALF = 32
CHUNKS = 32
COLS = D // 128
BODY = COLS * HALF
CODED = BODY + 16
LIMIT = 32700.0
VMEM = 16 * 1024 * 1024


def diagonal(rows):
    r = lax.broadcasted_iota(jnp.int32, (rows, 128), 0) % HALF
    c = lax.broadcasted_iota(jnp.int32, (rows, 128), 1)
    return r == c


def to_lanes(column):
    return jnp.sum(jnp.where(diagonal(HALF), column, 0.0), 0, keepdims=True)


def to_column(row):
    return jnp.sum(jnp.where(diagonal(HALF), row, 0.0), 1, keepdims=True)


def code_of(values):
    most = jnp.max(jnp.abs(values), 1, keepdims=True)
    return jnp.ceil(jnp.log2(jnp.maximum(most, 1e-30)) * 256.0)


def quantize(values, code):
    scaled = values * (LIMIT * jnp.exp2(code * (-1.0 / 256.0)))
    return jnp.floor(scaled + 0.5).astype(jnp.int32).astype(jnp.int16)


def scale_of(code):
    return jnp.exp2(code * (1.0 / 256.0)) * (1.0 / LIMIT)


def footer(counts, codes):
    r = lax.broadcasted_iota(jnp.int32, (16, 128), 0)
    both = jnp.where(r == 0, counts, jnp.where(r == 1, codes, 0.0))
    return both.astype(jnp.int32).astype(jnp.int16)


TILE = 256


def is_named(t, base, labels):
    j = t * TILE + lax.broadcasted_iota(jnp.int32, (TILE, 1), 0)
    k = j + (j // HALF) * HALF + base
    return jnp.where(k == labels, 1.0, 0.0)


def own_sums_kernel(base_ref, labels, rows, out_ref):
    for t in range(CHUNKS * HALF // TILE):
        hot = is_named(t, base_ref[0], labels[...]).astype(jnp.bfloat16)
        out_ref[t * TILE : (t + 1) * TILE, :] = jnp.dot(
            hot, rows[...], preferred_element_type=jnp.float32
        )


def chip_sums_kernel(base_ref, own_labels, labels, own_sums, rows, out_ref):
    for t in range(CHUNKS * HALF // TILE):
        hot = is_named(t, base_ref[0], labels[...])
        sums = own_sums[t * TILE : (t + 1) * TILE, :] + jnp.dot(
            hot.astype(jnp.bfloat16), rows[...], preferred_element_type=jnp.float32
        )
        hot = hot + is_named(t, base_ref[0], own_labels[...])
        counts = jnp.sum(hot, 1, keepdims=True)
        code = code_of(sums)
        coded = quantize(sums, code)
        for c in range(TILE // HALF):
            at = t * (TILE // HALF) + c
            part = slice(c * HALF, (c + 1) * HALF)
            for b in range(COLS):
                out_ref[at, b * HALF : (b + 1) * HALF, :] = coded[
                    part, b * 128 : (b + 1) * 128
                ]
            out_ref[at, BODY:CODED, :] = footer(
                to_lanes(counts[part]), to_lanes(code[part])
            )


def block(b):
    return slice(b * HALF, (b + 1) * HALF)


def add_coded(ref, at, blocks, counts):
    foot = ref[at, BODY:CODED, :].astype(jnp.float32)
    scale = scale_of(to_column(foot[1:2, :]))
    blocks = [
        blocks[b] + ref[at, block(b), :].astype(jnp.float32) * scale
        for b in range(COLS)
    ]
    return blocks, counts + foot[0:1, :]


def nothing():
    zeros = [jnp.zeros((HALF, 128), jnp.float32) for _ in range(COLS)]
    return zeros, jnp.zeros((1, 128), jnp.float32)


def code_blocks(blocks):
    most = jnp.abs(blocks[0])
    for b in range(1, COLS):
        most = jnp.maximum(most, jnp.abs(blocks[b]))
    code = code_of(most)
    return [quantize(blocks[b], code) for b in range(COLS)], to_lanes(code)


def group_kernel(in_ref, c0, c1, c2, c3, out_ref, centers_ref):
    together = 8

    def step(t, carry):
        blocks, counts = list(carry[0]), carry[1]
        for i in range(together):
            blocks, counts = add_coded(in_ref, t * together + i, blocks, counts)
        return tuple(blocks), counts

    blocks, counts = nothing()
    blocks, counts = lax.fori_loop(0, CHUNKS // together, step, (tuple(blocks), counts))
    coded, codes = code_blocks(blocks)
    for b in range(COLS):
        out_ref[0, block(b), :] = coded[b]
    out_ref[0, BODY:CODED, :] = footer(counts, codes)
    for i, ref in enumerate((c0, c1, c2, c3)):
        n = ref.shape[0]
        centers_ref[i * n : (i + 1) * n, :] = ref[...]


def refine_kernel(own, one, two, three, refined_ref, coded_ref):
    even = add_coded(two, 0, *add_coded(own, 0, *nothing()))
    odd = add_coded(three, 0, *add_coded(one, 0, *nothing()))
    counts = to_column(even[1] + odd[1])
    refined = [(even[0][b] + odd[0][b]) / counts for b in range(COLS)]
    for b in range(COLS):
        refined_ref[:, b * 128 : (b + 1) * 128] = refined[b]
    coded, codes = code_blocks(refined)
    foot = footer(jnp.zeros_like(codes), codes)

    def step(s, carry):
        for b in range(COLS):
            coded_ref[s, block(b), :] = coded[b]
        coded_ref[s, BODY:CODED, :] = foot
        return carry

    lax.fori_loop(0, CHUNKS, step, 0)


def nearest(value, least):
    n = value.shape[0]
    return jnp.minimum(least, jnp.min(value.reshape(n // 8, 8, value.shape[1]), 0))


def old_kernel(norms_ref, rows_ref, *refs):
    *centers, out_ref, turned_ref = refs
    turned_ref[...] = (rows_ref[...] * jnp.bfloat16(-2.0)).T
    turned = turned_ref[...]
    least = jnp.full((8, turned.shape[1]), jnp.inf, jnp.float32)
    for ref in centers:
        wide = ref[...].astype(jnp.float32)
        norm = jnp.sum(wide * wide, 1, keepdims=True)
        product = jnp.dot(ref[...], turned, preferred_element_type=jnp.float32)
        least = nearest(product + norm, least)
    out_ref[...] = norms_ref[...] + jnp.min(least, 0, keepdims=True)


def new_kernel(turned_ref, coded_ref, norms_ref, least_ref, out_ref):
    per = TILE // HALF
    turned = turned_ref[...]
    least = least_ref[...]
    for t in range(CHUNKS // per):
        high, low, scale, norm = [], [], [], []
        for c in range(per):
            at = t * per + c
            wide = jnp.concatenate(
                [coded_ref[at, block(b), :].astype(jnp.float32) for b in range(COLS)], 1
            )
            top = wide.astype(jnp.bfloat16)
            high.append(top)
            low.append((wide - top.astype(jnp.float32)).astype(jnp.bfloat16))
            foot = coded_ref[at, BODY:CODED, :].astype(jnp.float32)
            s = scale_of(to_column(foot[1:2, :]))
            scale.append(s)
            norm.append(jnp.sum(wide * wide, 1, keepdims=True) * (s * s))
        product = jnp.dot(
            jnp.concatenate(high, 0), turned, preferred_element_type=jnp.float32
        ) + jnp.dot(jnp.concatenate(low, 0), turned, preferred_element_type=jnp.float32)
        value = product * jnp.concatenate(scale, 0) + jnp.concatenate(norm, 0)
        least = nearest(value, least)
    if out_ref.shape == least.shape:
        out_ref[...] = least
    else:
        out_ref[...] = norms_ref[...] + jnp.min(least, 0, keepdims=True)


def call(kernel, out_shape, *args, flops=0, moved=0, smem=0):
    specs = [
        pl.BlockSpec(memory_space=pltpu.SMEM if i < smem else pltpu.VMEM)
        for i in range(len(args))
    ]
    many = isinstance(out_shape, tuple)
    out_specs = pl.BlockSpec(memory_space=pltpu.VMEM)
    return pl.pallas_call(
        kernel,
        out_shape=out_shape,
        in_specs=specs,
        out_specs=tuple([out_specs] * len(out_shape)) if many else out_specs,
        compiler_params=pltpu.CompilerParams(vmem_limit_bytes=VMEM),
        cost_estimate=pl.CostEstimate(
            flops=flops, bytes_accessed=moved, transcendentals=0
        ),
    )(*args)


def ring(axis, size, k):
    return [(i, (i + k) % size) for i in range(size)]


def swap(value, axis):
    return lax.ppermute(value, axis, [(0, 1), (1, 0)])


def around(part, axis):
    return [part] + [lax.ppermute(part, axis, ring(axis, 4, k)) for k in (1, 2, 3)]


def after(first, values):
    return lax.optimization_barrier((first, *values))[1:]


def on_device(embeddings, centers, assignment):
    n = embeddings.shape[0]
    core = lax.axis_index("core")
    f32, bf16, i16 = jnp.float32, jnp.bfloat16, jnp.int16
    shape = jax.ShapeDtypeStruct
    labels = assignment.reshape(1, n)
    other_labels = swap(labels, "core")
    other_rows = swap(embeddings, "core")

    mine = lax.dynamic_slice(centers, (core * HALF, 0), (HALF, D))
    current = around(jnp.concatenate([mine, swap(mine, "zl")]), "x")

    wide = embeddings.astype(f32)
    norms = jnp.sum(wide * wide, 1).reshape(1, n)

    base = (core * HALF).astype(jnp.int32).reshape(1)
    sums = call(
        own_sums_kernel,
        shape((CHUNKS * HALF, D), f32),
        base, labels, embeddings,
        flops=2 * 1024 * n * D, moved=5 << 20, smem=1,
    )
    sums = call(
        chip_sums_kernel,
        shape((CHUNKS, CODED, 128), i16),
        base, labels, other_labels, sums, other_rows,
        flops=2 * 1024 * n * D, moved=6 << 20, smem=1,
    )
    sums, *current = lax.optimization_barrier((sums, *current))
    sums = lax.all_to_all(sums, SHARD, 0, 0)
    group, current = call(
        group_kernel,
        (shape((1, CODED, 128), i16), shape((8 * HALF, D), bf16)),
        sums, *current,
        flops=1 << 22, moved=2 << 20,
    )
    groups, current = lax.optimization_barrier(
        (around(group, "zh"), around(current, "y"))
    )
    refined, coded = call(
        refine_kernel,
        (shape((HALF, D), f32), shape((CHUNKS, CODED, 128), i16)),
        *groups,
        flops=1 << 20, moved=2 << 20,
    )
    new_own = lax.all_to_all(coded, SHARD, 0, 0)

    current = list(after(coded, current))
    current = current + list(swap(part, "core") for part in current)
    old_min, turned = call(
        old_kernel,
        (shape((1, n), f32), shape((D, n), bf16)),
        norms, embeddings, *current,
        flops=2 * 2048 * n * D, moved=5 << 20,
    )

    refined_other = swap(refined, "core")
    first = core == 0
    refined_centers = jnp.concatenate(
        [
            jnp.where(first, refined, refined_other),
            jnp.where(first, refined_other, refined),
        ]
    )

    new_own, turned, refined_centers = lax.optimization_barrier(
        (new_own, turned, refined_centers)
    )
    new_other = swap(new_own, "core")
    least = jnp.full((8, n), jnp.inf, f32)
    for coded, result in ((new_own, 8), (new_other, 1)):
        least = call(
            new_kernel,
            shape((result, n), f32),
            turned, coded, norms, least,
            flops=2 * 2048 * n * D, moved=3 << 20,
        )
    return old_min.reshape(n), refined_centers, least.reshape(n)


def solution(mesh):
    fine = Mesh(mesh.devices.reshape(SIZES), AXES)
    rows = ("zh", "core") + SHARD
    return jax.shard_map(
        on_device,
        mesh=fine,
        in_specs=(P(rows, None), P(SHARD, None), P(rows, None)),
        out_specs=(P(rows), P(SHARD, None), P(rows)),
        check_vma=False,
    )
```

```python
import jax
import jax.numpy as jnp
from jax import lax
from jax.experimental import pallas as pl
from jax.experimental.pallas import tpu as pltpu
from jax.sharding import Mesh, PartitionSpec as P

AXES = ("zh", "core", "y", "x", "zl")
SIZES = (4, 2, 4, 4, 2)
SHARD = ("y", "x", "zl")

D = 768
HALF = 32
CHUNKS = 32
COLS = D // 128
BODY = COLS * HALF
CODED = BODY + 16
LIMIT = 32700.0
VMEM = 16 * 1024 * 1024


def diagonal(rows):
    r = lax.broadcasted_iota(jnp.int32, (rows, 128), 0) % HALF
    c = lax.broadcasted_iota(jnp.int32, (rows, 128), 1)
    return r == c


def to_lanes(column):
    return jnp.sum(jnp.where(diagonal(HALF), column, 0.0), 0, keepdims=True)


def to_column(row):
    return jnp.sum(jnp.where(diagonal(HALF), row, 0.0), 1, keepdims=True)


def code_of(values):
    most = jnp.max(jnp.abs(values), 1, keepdims=True)
    return jnp.ceil(jnp.log2(jnp.maximum(most, 1e-30)) * 256.0)


def quantize(values, code):
    scaled = values * (LIMIT * jnp.exp2(code * (-1.0 / 256.0)))
    return jnp.floor(scaled + 0.5).astype(jnp.int32).astype(jnp.int16)


def scale_of(code):
    return jnp.exp2(code * (1.0 / 256.0)) * (1.0 / LIMIT)


def footer(counts, codes):
    r = lax.broadcasted_iota(jnp.int32, (16, 128), 0)
    both = jnp.where(r == 0, counts, jnp.where(r == 1, codes, 0.0))
    return both.astype(jnp.int32).astype(jnp.int16)


TILE = 256
EACH = TILE // HALF


def is_named(t, place, labels):
    first, second, at, half = (place[i] for i in range(4))
    j = lax.broadcasted_iota(jnp.int32, (TILE, 1), 0)
    c = j // HALF
    shard = (c // 2) * first + ((at + t) % 4) * second + c % 2
    k = shard * (2 * HALF) + half + j % HALF
    return jnp.where(k == labels, 1.0, 0.0)


def own_sums_kernel(place, labels, rows, out_ref):
    for t in range(4):
        hot = is_named(t, place, labels[...]).astype(jnp.bfloat16)
        out_ref[t * TILE : (t + 1) * TILE, :] = jnp.dot(
            hot, rows[...], preferred_element_type=jnp.float32
        )


def chip_sums_kernel(place, own_labels, labels, own_sums, rows, *out_refs):
    for t in range(4):
        hot = is_named(t, place, labels[...])
        sums = own_sums[t * TILE : (t + 1) * TILE, :] + jnp.dot(
            hot.astype(jnp.bfloat16), rows[...], preferred_element_type=jnp.float32
        )
        hot = hot + is_named(t, place, own_labels[...])
        counts = jnp.sum(hot, 1, keepdims=True)
        code = code_of(sums)
        coded = quantize(sums, code)
        for c in range(EACH):
            part = slice(c * HALF, (c + 1) * HALF)
            for b in range(COLS):
                out_refs[t][c, block(b), :] = coded[part, b * 128 : (b + 1) * 128]
            out_refs[t][c, BODY:CODED, :] = footer(
                to_lanes(counts[part]), to_lanes(code[part])
            )


def block(b):
    return slice(b * HALF, (b + 1) * HALF)


def add_coded(ref, at, blocks, counts):
    foot = ref[at, BODY:CODED, :].astype(jnp.float32)
    scale = scale_of(to_column(foot[1:2, :]))
    blocks = [
        blocks[b] + ref[at, block(b), :].astype(jnp.float32) * scale
        for b in range(COLS)
    ]
    return blocks, counts + foot[0:1, :]


def nothing():
    zeros = [jnp.zeros((HALF, 128), jnp.float32) for _ in range(COLS)]
    return zeros, jnp.zeros((1, 128), jnp.float32)


def code_blocks(blocks):
    most = jnp.abs(blocks[0])
    for b in range(1, COLS):
        most = jnp.maximum(most, jnp.abs(blocks[b]))
    code = code_of(most)
    return [quantize(blocks[b], code) for b in range(COLS)], to_lanes(code)


def add_and_code(refs, at, out_ref, to):
    blocks, counts = nothing()
    for ref in refs:
        blocks, counts = add_coded(ref, at, blocks, counts)
    coded, codes = code_blocks(blocks)
    for b in range(COLS):
        out_ref[to, block(b), :] = coded[b]
    out_ref[to, BODY:CODED, :] = footer(counts, codes)


def join(refs, out_ref):
    n = refs[0].shape[0]
    for i, ref in enumerate(refs):
        out_ref[i * n : (i + 1) * n] = ref[...]


def first_sums_kernel(place, *refs):
    for k in range(4):
        for z in range(2):
            at = ((place[4] + k) % 4) * 2 + z
            add_and_code(refs[:4], at, refs[8 + k], z)
    join(refs[4:8], refs[12])


def second_sums_kernel(place, *refs):
    add_and_code(refs[:4], place[5], refs[4], 0)
    add_and_code(refs[:4], 1 - place[5], refs[5], 0)


def third_sums_kernel(own, other, out_ref):
    add_and_code((own, other), 0, out_ref, 0)


def join_kernel(*refs):
    join(refs[:-1], refs[-1])


def refine_kernel(own, one, two, three, refined_ref, coded_ref):
    even = add_coded(two, 0, *add_coded(own, 0, *nothing()))
    odd = add_coded(three, 0, *add_coded(one, 0, *nothing()))
    counts = to_column(even[1] + odd[1])
    refined = [(even[0][b] + odd[0][b]) / counts for b in range(COLS)]
    for b in range(COLS):
        refined_ref[:, b * 128 : (b + 1) * 128] = refined[b]
    coded, codes = code_blocks(refined)
    for b in range(COLS):
        coded_ref[0, block(b), :] = coded[b]
    coded_ref[0, BODY:CODED, :] = footer(jnp.zeros_like(codes), codes)


def nearest(value, least):
    n = value.shape[0]
    return jnp.minimum(least, jnp.min(value.reshape(n // 8, 8, value.shape[1]), 0))


def old_kernel(norms_ref, rows_ref, *refs):
    *centers, out_ref, turned_ref = refs
    turned_ref[...] = (rows_ref[...] * jnp.bfloat16(-2.0)).T
    turned = turned_ref[...]
    least = jnp.full((8, turned.shape[1]), jnp.inf, jnp.float32)
    for ref in centers:
        wide = ref[...].astype(jnp.float32)
        norm = jnp.sum(wide * wide, 1, keepdims=True)
        product = jnp.dot(ref[...], turned, preferred_element_type=jnp.float32)
        least = nearest(product + norm, least)
    out_ref[...] = norms_ref[...] + jnp.min(least, 0, keepdims=True)


def new_kernel(turned_ref, norms_ref, least_ref, *refs):
    *pieces, out_ref = refs
    turned = turned_ref[...]
    least = least_ref[...]
    for ref in pieces:
        high, low, scale, norm = [], [], [], []
        for c in range(EACH):
            wide = jnp.concatenate(
                [ref[c, block(b), :].astype(jnp.float32) for b in range(COLS)], 1
            )
            top = wide.astype(jnp.bfloat16)
            high.append(top)
            low.append((wide - top.astype(jnp.float32)).astype(jnp.bfloat16))
            foot = ref[c, BODY:CODED, :].astype(jnp.float32)
            s = scale_of(to_column(foot[1:2, :]))
            scale.append(s)
            norm.append(jnp.sum(wide * wide, 1, keepdims=True) * (s * s))
        product = jnp.dot(
            jnp.concatenate(high, 0), turned, preferred_element_type=jnp.float32
        ) + jnp.dot(jnp.concatenate(low, 0), turned, preferred_element_type=jnp.float32)
        value = product * jnp.concatenate(scale, 0) + jnp.concatenate(norm, 0)
        least = nearest(value, least)
    if out_ref.shape == least.shape:
        out_ref[...] = least
    else:
        out_ref[...] = norms_ref[...] + jnp.min(least, 0, keepdims=True)


def call(kernel, out_shape, *args, flops=0, moved=0, smem=0):
    specs = [
        pl.BlockSpec(memory_space=pltpu.SMEM if i < smem else pltpu.VMEM)
        for i in range(len(args))
    ]
    many = isinstance(out_shape, tuple)
    out_specs = pl.BlockSpec(memory_space=pltpu.VMEM)
    return pl.pallas_call(
        kernel,
        out_shape=out_shape,
        in_specs=specs,
        out_specs=tuple([out_specs] * len(out_shape)) if many else out_specs,
        compiler_params=pltpu.CompilerParams(vmem_limit_bytes=VMEM),
        cost_estimate=pl.CostEstimate(
            flops=flops, bytes_accessed=moved, transcendentals=0
        ),
    )(*args)


def swap(value, axis):
    return lax.ppermute(value, axis, [(0, 1), (1, 0)])


def around_z(part):
    return [part] + [
        lax.ppermute(part, "zh", [(i, (i + k) % 4) for i in range(4)])
        for k in (1, 2, 3)
    ]


def onward(k, turn):
    pairs = []
    for core in range(2):
        for y in range(4):
            for x in range(4):
                if core == turn:
                    to = (y, (x + k) % 4)
                else:
                    to = ((y + k) % 4, x)
                pairs.append((core * 16 + y * 4 + x, core * 16 + to[0] * 4 + to[1]))
    return pairs


def send(part, k, turn):
    return lax.ppermute(part, ("core", "y", "x"), onward(k, turn))


def around(part, turn):
    return [part] + [send(part, k, turn) for k in (1, 3, 2)]


def after(first, values):
    return lax.optimization_barrier((first, *values))[1:]


def on_device(embeddings, centers, assignment):
    n = embeddings.shape[0]
    f32, bf16, i16 = jnp.float32, jnp.bfloat16, jnp.int16
    shape = jax.ShapeDtypeStruct

    def coded(chunks):
        return shape((chunks, CODED, 128), i16)

    core, y, x, zl = (lax.axis_index(name) for name in ("core", "y", "x", "zl"))
    first = core == 0
    place = jnp.stack(
        [
            jnp.where(first, 8, 2),
            jnp.where(first, 2, 8),
            jnp.where(first, x, y),
            core * HALF,
            jnp.where(first, y, x),
            zl,
        ]
    ).astype(jnp.int32)

    labels = assignment.reshape(1, n)
    other_labels = swap(labels, "core")
    other_rows = swap(embeddings, "core")

    mine = lax.dynamic_slice(centers, (core * HALF, 0), (HALF, D))
    current = jnp.concatenate([mine, swap(mine, "zl")])
    (other_rows, current) = lax.optimization_barrier((other_rows, current))

    wide = embeddings.astype(f32)
    norms = jnp.sum(wide * wide, 1).reshape(1, n)

    sums = call(
        own_sums_kernel,
        shape((4 * TILE, D), f32),
        place, labels, embeddings,
        flops=2 * 1024 * n * D, moved=5 << 20, smem=1,
    )
    sums = call(
        chip_sums_kernel,
        (coded(EACH),) * 4,
        place, labels, other_labels, sums, other_rows,
        flops=2 * 1024 * n * D, moved=6 << 20, smem=1,
    )

    (current,) = after(sums[0], (current,))
    *sums, current = call(
        first_sums_kernel,
        (coded(2),) * 4 + (shape((8 * HALF, D), bf16),),
        place, sums[0], *(send(sums[k], k, 0) for k in (1, 3, 2)), *around(current, 0),
        flops=1 << 22, moved=3 << 20, smem=1,
    )
    own, other = call(
        second_sums_kernel,
        (coded(1),) * 2,
        place, sums[0], *(send(sums[k], k, 1) for k in (1, 3, 2)),
        flops=1 << 20, moved=1 << 20, smem=1,
    )
    group = call(
        third_sums_kernel, coded(1), own, swap(other, "zl"), flops=1 << 18, moved=1 << 18
    )
    (current,) = after(own, (current,))
    groups, current = lax.optimization_barrier((around_z(group), around(current, 1)))
    refined, code = call(
        refine_kernel,
        (shape((HALF, D), f32), coded(1)),
        *groups,
        flops=1 << 20, moved=1 << 20,
    )

    pair = call(
        join_kernel, coded(2), code, swap(code, "zl"), flops=1 << 10, moved=1 << 18
    )
    new = call(
        join_kernel, coded(EACH), *around(pair, 0), flops=1 << 10, moved=1 << 20
    )
    new = around(new, 1)
    new_other = [swap(part, "core") for part in new]

    current_other = [swap(part, "core") for part in current]
    old_min, turned = call(
        old_kernel,
        (shape((1, n), f32), shape((D, n), bf16)),
        norms, embeddings, *current, *current_other,
        flops=2 * 2048 * n * D, moved=5 << 20,
    )

    refined_other = swap(refined, "core")
    refined_centers = jnp.concatenate(
        [
            jnp.where(first, refined, refined_other),
            jnp.where(first, refined_other, refined),
        ]
    )

    turned, refined_centers = lax.optimization_barrier((turned, refined_centers))
    least = jnp.full((8, n), jnp.inf, f32)
    for pieces in (
        (new[0], new_other[0]),
        (new[1], new[2]),
        (new_other[1], new_other[2], new[3]),
        (new_other[3],),
    ):
        last = pieces[0] is new_other[3]
        least = call(
            new_kernel,
            shape((1 if last else 8, n), f32),
            turned, norms, least, *pieces,
            flops=4 * TILE * n * D * len(pieces), moved=len(pieces) << 19,
        )
    return old_min.reshape(n), refined_centers, least.reshape(n)


def solution(mesh):
    fine = Mesh(mesh.devices.reshape(SIZES), AXES)
    rows = ("zh", "core") + SHARD
    return jax.shard_map(
        on_device,
        mesh=fine,
        in_specs=(P(rows, None), P(SHARD, None), P(rows, None)),
        out_specs=(P(rows), P(SHARD, None), P(rows)),
        check_vma=False,
    )
```

```python
import jax
import jax.numpy as jnp
from jax import lax
from jax.experimental import pallas as pl
from jax.experimental.pallas import tpu as pltpu
from jax.sharding import Mesh, PartitionSpec as P

AXES = ("zh", "core", "y", "x", "zl")
SIZES = (4, 2, 4, 4, 2)
SHARD = ("y", "x", "zl")

D = 768
HALF = 32
CHUNKS = 32
COLS = D // 128
BODY = COLS * HALF
CODED = BODY + 16
LIMIT = 32700.0
VMEM = 16 * 1024 * 1024


def diagonal(rows):
    r = lax.broadcasted_iota(jnp.int32, (rows, 128), 0) % HALF
    c = lax.broadcasted_iota(jnp.int32, (rows, 128), 1)
    return r == c


def to_lanes(column):
    return jnp.sum(jnp.where(diagonal(HALF), column, 0.0), 0, keepdims=True)


def to_column(row):
    return jnp.sum(jnp.where(diagonal(HALF), row, 0.0), 1, keepdims=True)


def code_of(values):
    most = jnp.max(jnp.abs(values), 1, keepdims=True)
    return jnp.ceil(jnp.log2(jnp.maximum(most, 1e-30)) * 256.0)


def quantize(values, code):
    scaled = values * (LIMIT * jnp.exp2(code * (-1.0 / 256.0)))
    return jnp.floor(scaled + 0.5).astype(jnp.int32).astype(jnp.int16)


def scale_of(code):
    return jnp.exp2(code * (1.0 / 256.0)) * (1.0 / LIMIT)


def footer(counts, codes):
    r = lax.broadcasted_iota(jnp.int32, (16, 128), 0)
    both = jnp.where(r == 0, counts, jnp.where(r == 1, codes, 0.0))
    return both.astype(jnp.int32).astype(jnp.int16)


TILE = 256


def is_named(t, base, labels):
    j = t * TILE + lax.broadcasted_iota(jnp.int32, (TILE, 1), 0)
    k = j + (j // HALF) * HALF + base
    return jnp.where(k == labels, 1.0, 0.0)


def own_sums_kernel(base_ref, labels, rows, out_ref):
    for t in range(CHUNKS * HALF // TILE):
        hot = is_named(t, base_ref[0], labels[...]).astype(jnp.bfloat16)
        out_ref[t * TILE : (t + 1) * TILE, :] = jnp.dot(
            hot, rows[...], preferred_element_type=jnp.float32
        )


def chip_sums_kernel(base_ref, own_labels, labels, own_sums, rows, out_ref):
    for t in range(CHUNKS * HALF // TILE):
        hot = is_named(t, base_ref[0], labels[...])
        sums = own_sums[t * TILE : (t + 1) * TILE, :] + jnp.dot(
            hot.astype(jnp.bfloat16), rows[...], preferred_element_type=jnp.float32
        )
        hot = hot + is_named(t, base_ref[0], own_labels[...])
        counts = jnp.sum(hot, 1, keepdims=True)
        code = code_of(sums)
        coded = quantize(sums, code)
        for c in range(TILE // HALF):
            at = t * (TILE // HALF) + c
            part = slice(c * HALF, (c + 1) * HALF)
            for b in range(COLS):
                out_ref[at, b * HALF : (b + 1) * HALF, :] = coded[
                    part, b * 128 : (b + 1) * 128
                ]
            out_ref[at, BODY:CODED, :] = footer(
                to_lanes(counts[part]), to_lanes(code[part])
            )


def block(b):
    return slice(b * HALF, (b + 1) * HALF)


def add_coded(ref, at, blocks, counts):
    foot = ref[at, BODY:CODED, :].astype(jnp.float32)
    scale = scale_of(to_column(foot[1:2, :]))
    blocks = [
        blocks[b] + ref[at, block(b), :].astype(jnp.float32) * scale
        for b in range(COLS)
    ]
    return blocks, counts + foot[0:1, :]


def nothing():
    zeros = [jnp.zeros((HALF, 128), jnp.float32) for _ in range(COLS)]
    return zeros, jnp.zeros((1, 128), jnp.float32)


def code_blocks(blocks):
    most = jnp.abs(blocks[0])
    for b in range(1, COLS):
        most = jnp.maximum(most, jnp.abs(blocks[b]))
    code = code_of(most)
    return [quantize(blocks[b], code) for b in range(COLS)], to_lanes(code)


def group_kernel(in_ref, out_ref):
    together = 8

    def step(t, carry):
        blocks, counts = list(carry[0]), carry[1]
        for i in range(together):
            blocks, counts = add_coded(in_ref, t * together + i, blocks, counts)
        return tuple(blocks), counts

    blocks, counts = nothing()
    blocks, counts = lax.fori_loop(0, CHUNKS // together, step, (tuple(blocks), counts))
    coded, codes = code_blocks(blocks)
    for b in range(COLS):
        out_ref[0, block(b), :] = coded[b]
    out_ref[0, BODY:CODED, :] = footer(counts, codes)


def refine_kernel(groups, refined_ref, coded_ref):
    blocks, counts = nothing()
    for g in range(groups.shape[0]):
        blocks, counts = add_coded(groups, g, blocks, counts)
    counts = to_column(counts)
    refined = [blocks[b] / counts for b in range(COLS)]
    for b in range(COLS):
        refined_ref[:, b * 128 : (b + 1) * 128] = refined[b]
    coded, codes = code_blocks(refined)
    foot = footer(jnp.zeros_like(codes), codes)

    def step(s, carry):
        for b in range(COLS):
            coded_ref[s, block(b), :] = coded[b]
        coded_ref[s, BODY:CODED, :] = foot
        return carry

    lax.fori_loop(0, CHUNKS, step, 0)


def nearest(value, least):
    n = value.shape[0]
    return jnp.minimum(least, jnp.min(value.reshape(n // 8, 8, value.shape[1]), 0))


def old_kernel(norms_ref, rows_ref, *refs):
    *centers, out_ref, turned_ref = refs
    turned_ref[...] = (rows_ref[...] * jnp.bfloat16(-2.0)).T
    turned = turned_ref[...]
    least = jnp.full((8, turned.shape[1]), jnp.inf, jnp.float32)
    for ref in centers:
        wide = ref[...].astype(jnp.float32)
        norm = jnp.sum(wide * wide, 1, keepdims=True)
        product = jnp.dot(ref[...], turned, preferred_element_type=jnp.float32)
        least = nearest(product + norm, least)
    out_ref[...] = norms_ref[...] + jnp.min(least, 0, keepdims=True)


def new_kernel(turned_ref, coded_ref, norms_ref, least_ref, out_ref):
    per = TILE // HALF
    turned = turned_ref[...]
    least = least_ref[...]
    for t in range(CHUNKS // per):
        high, low, scale, norm = [], [], [], []
        for c in range(per):
            at = t * per + c
            wide = jnp.concatenate(
                [coded_ref[at, block(b), :].astype(jnp.float32) for b in range(COLS)], 1
            )
            top = wide.astype(jnp.bfloat16)
            high.append(top)
            low.append((wide - top.astype(jnp.float32)).astype(jnp.bfloat16))
            foot = coded_ref[at, BODY:CODED, :].astype(jnp.float32)
            s = scale_of(to_column(foot[1:2, :]))
            scale.append(s)
            norm.append(jnp.sum(wide * wide, 1, keepdims=True) * (s * s))
        product = jnp.dot(
            jnp.concatenate(high, 0), turned, preferred_element_type=jnp.float32
        ) + jnp.dot(jnp.concatenate(low, 0), turned, preferred_element_type=jnp.float32)
        value = product * jnp.concatenate(scale, 0) + jnp.concatenate(norm, 0)
        least = nearest(value, least)
    if out_ref.shape == least.shape:
        out_ref[...] = least
    else:
        out_ref[...] = norms_ref[...] + jnp.min(least, 0, keepdims=True)


def call(kernel, out_shape, *args, flops=0, moved=0, smem=0):
    specs = [
        pl.BlockSpec(memory_space=pltpu.SMEM if i < smem else pltpu.VMEM)
        for i in range(len(args))
    ]
    many = isinstance(out_shape, tuple)
    out_specs = pl.BlockSpec(memory_space=pltpu.VMEM)
    return pl.pallas_call(
        kernel,
        out_shape=out_shape,
        in_specs=specs,
        out_specs=tuple([out_specs] * len(out_shape)) if many else out_specs,
        compiler_params=pltpu.CompilerParams(vmem_limit_bytes=VMEM),
        cost_estimate=pl.CostEstimate(
            flops=flops, bytes_accessed=moved, transcendentals=0
        ),
    )(*args)


def swap(value, axis):
    return lax.ppermute(value, axis, [(0, 1), (1, 0)])


PLANE = ("core", "y", "x", "zl")


def plane(core, y, x, zl=0):
    return ((core * 4 + y) * 4 + x) * 2 + zl


def along_first():
    both = [(i, z) for i in range(4) for z in range(2)]
    return [[plane(0, a, i, z) for i, z in both] for a in range(4)] + [
        [plane(1, i, a, z) for i, z in both] for a in range(4)
    ]


def along_second(k):
    pairs = []
    for a in range(4):
        for i in range(4):
            to = (i + k) % 4
            pairs.append((plane(0, i, a) // 2, plane(0, to, a) // 2))
            pairs.append((plane(1, a, i) // 2, plane(1, a, to) // 2))
    return pairs


def after(first, values):
    return lax.optimization_barrier((first, *values))[1:]


def on_device(embeddings, centers, assignment):
    n = embeddings.shape[0]
    core = lax.axis_index("core")
    f32, bf16, i16 = jnp.float32, jnp.bfloat16, jnp.int16
    shape = jax.ShapeDtypeStruct
    labels = assignment.reshape(1, n)
    other_labels = swap(labels, "core")
    other_rows = swap(embeddings, "core")

    mine = lax.dynamic_slice(centers, (core * HALF, 0), (HALF, D))
    current = lax.all_to_all(
        jnp.broadcast_to(mine[None], (8, HALF, D)),
        PLANE, 0, 0, axis_index_groups=along_first(),
    ).reshape(8 * HALF, D)

    wide = embeddings.astype(f32)
    norms = jnp.sum(wide * wide, 1).reshape(1, n)

    base = (core * HALF).astype(jnp.int32).reshape(1)
    sums = call(
        own_sums_kernel,
        shape((CHUNKS * HALF, D), f32),
        base, labels, embeddings,
        flops=2 * 1024 * n * D, moved=5 << 20, smem=1,
    )
    sums = call(
        chip_sums_kernel,
        shape((CHUNKS, CODED, 128), i16),
        base, labels, other_labels, sums, other_rows,
        flops=2 * 1024 * n * D, moved=6 << 20, smem=1,
    )
    sums, current = lax.optimization_barrier((sums, current))
    sums = lax.all_to_all(sums, SHARD, 0, 0)
    group = call(
        group_kernel,
        shape((1, CODED, 128), i16),
        sums,
        flops=1 << 22, moved=2 << 20,
    )
    (current,) = after(group, (current,))
    current = [current] + [
        lax.ppermute(current, PLANE[:3], along_second(k)) for k in (1, 3, 2)
    ]
    groups, current = lax.optimization_barrier(
        (lax.all_gather(group, "zh", axis=0, tiled=True), current)
    )
    refined, coded = call(
        refine_kernel,
        (shape((HALF, D), f32), shape((CHUNKS, CODED, 128), i16)),
        groups,
        flops=1 << 20, moved=2 << 20,
    )
    new_own = lax.all_to_all(coded, SHARD, 0, 0)

    current = list(after(coded, current))
    current = current + list(swap(part, "core") for part in current)
    old_min, turned = call(
        old_kernel,
        (shape((1, n), f32), shape((D, n), bf16)),
        norms, embeddings, *current,
        flops=2 * 2048 * n * D, moved=5 << 20,
    )

    refined_other = swap(refined, "core")
    first = core == 0
    refined_centers = jnp.concatenate(
        [
            jnp.where(first, refined, refined_other),
            jnp.where(first, refined_other, refined),
        ]
    )

    new_own, turned, refined_centers = lax.optimization_barrier(
        (new_own, turned, refined_centers)
    )
    new_other = swap(new_own, "core")
    least = jnp.full((8, n), jnp.inf, f32)
    for coded, result in ((new_own, 8), (new_other, 1)):
        least = call(
            new_kernel,
            shape((result, n), f32),
            turned, coded, norms, least,
            flops=2 * 2048 * n * D, moved=3 << 20,
        )
    return old_min.reshape(n), refined_centers, least.reshape(n)


def solution(mesh):
    fine = Mesh(mesh.devices.reshape(SIZES), AXES)
    rows = ("zh", "core") + SHARD
    return jax.shard_map(
        on_device,
        mesh=fine,
        in_specs=(P(rows, None), P(SHARD, None), P(rows, None)),
        out_specs=(P(rows), P(SHARD, None), P(rows)),
        check_vma=False,
    )
```

```python
import jax
import jax.numpy as jnp
from jax import lax
from jax.experimental import pallas as pl
from jax.experimental.pallas import tpu as pltpu
from jax.sharding import Mesh, PartitionSpec as P

AXES = ("zh", "core", "y", "x", "zl")
SIZES = (4, 2, 4, 4, 2)
SHARD = ("y", "x", "zl")

D = 768
HALF = 32
CHUNKS = 32
COLS = D // 128
PART = HALF // 2
BODY = COLS * PART
CODED = BODY + 16
LIMIT = 32700.0
VMEM = 16 * 1024 * 1024


def diagonal(rows):
    r = lax.broadcasted_iota(jnp.int32, (rows, 128), 0) % PART
    c = lax.broadcasted_iota(jnp.int32, (rows, 128), 1)
    return r == c


def to_lanes(column):
    return jnp.sum(jnp.where(diagonal(PART), column, 0.0), 0, keepdims=True)


def to_column(row):
    return jnp.sum(jnp.where(diagonal(PART), row, 0.0), 1, keepdims=True)


def code_of(values):
    most = jnp.max(jnp.abs(values), 1, keepdims=True)
    return jnp.ceil(jnp.log2(jnp.maximum(most, 1e-30)) * 256.0)


def quantize(values, code):
    scaled = values * (LIMIT * jnp.exp2(code * (-1.0 / 256.0)))
    return jnp.floor(scaled + 0.5).astype(jnp.int32).astype(jnp.int16)


def scale_of(code):
    return jnp.exp2(code * (1.0 / 256.0)) * (1.0 / LIMIT)


def footer(counts, codes):
    r = lax.broadcasted_iota(jnp.int32, (16, 128), 0)
    both = jnp.where(r == 0, counts, jnp.where(r == 1, codes, 0.0))
    return both.astype(jnp.int32).astype(jnp.int16)


TILE = 256
EACH = TILE // PART
TILES = CHUNKS * PART // TILE


def is_named(part, t, base, labels):
    j = t * TILE + lax.broadcasted_iota(jnp.int32, (TILE, 1), 0)
    k = (j // PART) * (2 * HALF) + (part * PART + base) + j % PART
    return jnp.where(k == labels, 1.0, 0.0)


def own_sums_kernel(base_ref, labels, rows, out_ref):
    for part in range(2):
        for t in range(TILES):
            hot = is_named(part, t, base_ref[0], labels[...]).astype(jnp.bfloat16)
            at = (part * TILES + t) * TILE
            out_ref[at : at + TILE, :] = jnp.dot(
                hot, rows[...], preferred_element_type=jnp.float32
            )


def chip_sums_kernel(base_ref, own_labels, labels, own_sums, rows, *out_refs):
    for part in range(2):
        for t in range(TILES):
            hot = is_named(part, t, base_ref[0], labels[...])
            at = (part * TILES + t) * TILE
            sums = own_sums[at : at + TILE, :] + jnp.dot(
                hot.astype(jnp.bfloat16), rows[...], preferred_element_type=jnp.float32
            )
            hot = hot + is_named(part, t, base_ref[0], own_labels[...])
            counts = jnp.sum(hot, 1, keepdims=True)
            code = code_of(sums)
            coded = quantize(sums, code)
            for c in range(EACH):
                at = slice(c * PART, (c + 1) * PART)
                for b in range(COLS):
                    out_refs[part][t * EACH + c, block(b), :] = coded[
                        at, b * 128 : (b + 1) * 128
                    ]
                out_refs[part][t * EACH + c, BODY:CODED, :] = footer(
                    to_lanes(counts[at]), to_lanes(code[at])
                )


def block(b):
    return slice(b * PART, (b + 1) * PART)


def add_coded(ref, at, blocks, counts):
    foot = ref[at, BODY:CODED, :].astype(jnp.float32)
    scale = scale_of(to_column(foot[1:2, :]))
    blocks = [
        blocks[b] + ref[at, block(b), :].astype(jnp.float32) * scale
        for b in range(COLS)
    ]
    return blocks, counts + foot[0:1, :]


def nothing():
    zeros = [jnp.zeros((PART, 128), jnp.float32) for _ in range(COLS)]
    return zeros, jnp.zeros((1, 128), jnp.float32)


def code_blocks(blocks):
    most = jnp.abs(blocks[0])
    for b in range(1, COLS):
        most = jnp.maximum(most, jnp.abs(blocks[b]))
    code = code_of(most)
    return [quantize(blocks[b], code) for b in range(COLS)], to_lanes(code)


def group_kernel(in_ref, out_ref):
    together = 8

    def step(t, carry):
        blocks, counts = list(carry[0]), carry[1]
        for i in range(together):
            blocks, counts = add_coded(in_ref, t * together + i, blocks, counts)
        return tuple(blocks), counts

    blocks, counts = nothing()
    blocks, counts = lax.fori_loop(0, CHUNKS // together, step, (tuple(blocks), counts))
    coded, codes = code_blocks(blocks)
    for b in range(COLS):
        out_ref[0, block(b), :] = coded[b]
    out_ref[0, BODY:CODED, :] = footer(counts, codes)


def first_group_kernel(in_ref, c0, c1, c2, c3, out_ref, centers_ref):
    group_kernel(in_ref, out_ref)
    for i, ref in enumerate((c0, c1, c2, c3)):
        n = ref.shape[0]
        centers_ref[i * n : (i + 1) * n, :] = ref[...]


def refine_kernel(own, one, two, three, refined_ref, coded_ref):
    even = add_coded(two, 0, *add_coded(own, 0, *nothing()))
    odd = add_coded(three, 0, *add_coded(one, 0, *nothing()))
    counts = to_column(even[1] + odd[1])
    refined = [(even[0][b] + odd[0][b]) / counts for b in range(COLS)]
    for b in range(COLS):
        refined_ref[:, b * 128 : (b + 1) * 128] = refined[b]
    coded, codes = code_blocks(refined)
    foot = footer(jnp.zeros_like(codes), codes)

    def step(s, carry):
        for b in range(COLS):
            coded_ref[s, block(b), :] = coded[b]
        coded_ref[s, BODY:CODED, :] = foot
        return carry

    lax.fori_loop(0, CHUNKS, step, 0)


def nearest(value, least):
    n = value.shape[0]
    return jnp.minimum(least, jnp.min(value.reshape(n // 8, 8, value.shape[1]), 0))


def old_kernel(norms_ref, rows_ref, *refs):
    *centers, out_ref, turned_ref = refs
    turned_ref[...] = (rows_ref[...] * jnp.bfloat16(-2.0)).T
    turned = turned_ref[...]
    least = jnp.full((8, turned.shape[1]), jnp.inf, jnp.float32)
    for ref in centers:
        wide = ref[...].astype(jnp.float32)
        norm = jnp.sum(wide * wide, 1, keepdims=True)
        product = jnp.dot(ref[...], turned, preferred_element_type=jnp.float32)
        least = nearest(product + norm, least)
    out_ref[...] = norms_ref[...] + jnp.min(least, 0, keepdims=True)


def new_kernel(turned_ref, norms_ref, least_ref, *refs):
    *pieces, out_ref = refs
    turned = turned_ref[...]
    least = least_ref[...]
    for ref, t in [(ref, t) for ref in pieces for t in range(TILES)]:
        high, low, scale, norm = [], [], [], []
        for c in range(t * EACH, (t + 1) * EACH):
            wide = jnp.concatenate(
                [ref[c, block(b), :].astype(jnp.float32) for b in range(COLS)], 1
            )
            top = wide.astype(jnp.bfloat16)
            high.append(top)
            low.append((wide - top.astype(jnp.float32)).astype(jnp.bfloat16))
            foot = ref[c, BODY:CODED, :].astype(jnp.float32)
            s = scale_of(to_column(foot[1:2, :]))
            scale.append(s)
            norm.append(jnp.sum(wide * wide, 1, keepdims=True) * (s * s))
        product = jnp.dot(
            jnp.concatenate(high, 0), turned, preferred_element_type=jnp.float32
        ) + jnp.dot(jnp.concatenate(low, 0), turned, preferred_element_type=jnp.float32)
        value = product * jnp.concatenate(scale, 0) + jnp.concatenate(norm, 0)
        least = nearest(value, least)
    if out_ref.shape == least.shape:
        out_ref[...] = least
    else:
        out_ref[...] = norms_ref[...] + jnp.min(least, 0, keepdims=True)


def call(kernel, out_shape, *args, flops=0, moved=0, smem=0):
    specs = [
        pl.BlockSpec(memory_space=pltpu.SMEM if i < smem else pltpu.VMEM)
        for i in range(len(args))
    ]
    many = isinstance(out_shape, tuple)
    out_specs = pl.BlockSpec(memory_space=pltpu.VMEM)
    return pl.pallas_call(
        kernel,
        out_shape=out_shape,
        in_specs=specs,
        out_specs=tuple([out_specs] * len(out_shape)) if many else out_specs,
        compiler_params=pltpu.CompilerParams(vmem_limit_bytes=VMEM),
        cost_estimate=pl.CostEstimate(
            flops=flops, bytes_accessed=moved, transcendentals=0
        ),
    )(*args)


def swap(value, axis):
    return lax.ppermute(value, axis, [(0, 1), (1, 0)])


def around_z(part):
    return [part] + [
        lax.ppermute(part, "zh", [(i, (i + k) % 4) for i in range(4)])
        for k in (1, 2, 3)
    ]


def onward(k, turn):
    pairs = []
    for core in range(2):
        for y in range(4):
            for x in range(4):
                if core == turn:
                    to = (y, (x + k) % 4)
                else:
                    to = ((y + k) % 4, x)
                pairs.append((core * 16 + y * 4 + x, core * 16 + to[0] * 4 + to[1]))
    return pairs


def send(part, k, turn):
    return lax.ppermute(part, ("core", "y", "x"), onward(k, turn))


def around(part, turn):
    return [part] + [send(part, k, turn) for k in (1, 3, 2)]


def after(first, values):
    return lax.optimization_barrier((first, *values))[1:]


def on_device(embeddings, centers, assignment):
    n = embeddings.shape[0]
    core = lax.axis_index("core")
    f32, bf16, i16 = jnp.float32, jnp.bfloat16, jnp.int16
    shape = jax.ShapeDtypeStruct
    coded = shape((CHUNKS, CODED, 128), i16)
    labels = assignment.reshape(1, n)
    other_labels = swap(labels, "core")
    other_rows = swap(embeddings, "core")

    mine = lax.dynamic_slice(centers, (core * HALF, 0), (HALF, D))
    current = around(jnp.concatenate([mine, swap(mine, "zl")]), 0)

    wide = embeddings.astype(f32)
    norms = jnp.sum(wide * wide, 1).reshape(1, n)

    base = (core * HALF).astype(jnp.int32).reshape(1)
    own_sums = call(
        own_sums_kernel,
        shape((2 * CHUNKS * PART, D), f32),
        base, labels, embeddings,
        flops=2 * 1024 * n * D, moved=5 << 20, smem=1,
    )
    sums = call(
        chip_sums_kernel,
        (coded,) * 2,
        base, labels, other_labels, own_sums, other_rows,
        flops=2 * 1024 * n * D, moved=6 << 20, smem=1,
    )
    first_sums, *current = lax.optimization_barrier((sums[0], *current))
    one = shape((1, CODED, 128), i16)
    first_group, current = call(
        first_group_kernel,
        (one, shape((8 * HALF, D), bf16)),
        lax.all_to_all(first_sums, SHARD, 0, 0), *current,
        flops=1 << 21, moved=2 << 20,
    )
    second_group = call(
        group_kernel,
        one,
        lax.all_to_all(sums[1], SHARD, 0, 0),
        flops=1 << 21, moved=1 << 20,
    )
    groups = [around_z(first_group), around_z(second_group)]
    groups[0], current = lax.optimization_barrier((groups[0], around(current, 1)))
    def refine(parts):
        return call(
            refine_kernel,
            (shape((PART, D), f32), coded),
            *parts,
            flops=1 << 20, moved=1 << 20,
        )

    first_refined, code = refine(groups[0])
    first_new = lax.all_to_all(code, SHARD, 0, 0)

    current = list(after(first_refined, current))
    current = current + [swap(part, "core") for part in current]
    old_min, turned = call(
        old_kernel,
        (shape((1, n), f32), shape((D, n), bf16)),
        norms, embeddings, *current,
        flops=2 * 2048 * n * D, moved=5 << 20,
    )
    groups[1], turned = lax.optimization_barrier((groups[1], turned))
    second_refined, code = refine(groups[1])
    second_new = lax.all_to_all(code, SHARD, 0, 0)

    refined = jnp.concatenate([first_refined, second_refined])
    refined_other = swap(refined, "core")
    first = core == 0
    refined_centers = jnp.concatenate(
        [
            jnp.where(first, refined, refined_other),
            jnp.where(first, refined_other, refined),
        ]
    )

    def nearest_new(result, least, *pieces):
        return call(
            new_kernel,
            shape((result, n), f32),
            turned, norms, least, *pieces,
            flops=4 * 512 * n * D * len(pieces), moved=len(pieces) << 20,
        )

    least = jnp.full((8, n), jnp.inf, f32)
    least = nearest_new(8, least, first_new, swap(first_new, "core"))
    least, second_new, refined_centers = lax.optimization_barrier(
        (least, second_new, refined_centers)
    )
    second_other = swap(second_new, "core")
    least = nearest_new(8, least, second_new)
    least = nearest_new(1, least, second_other)
    return old_min.reshape(n), refined_centers, least.reshape(n)


def solution(mesh):
    fine = Mesh(mesh.devices.reshape(SIZES), AXES)
    rows = ("zh", "core") + SHARD
    return jax.shard_map(
        on_device,
        mesh=fine,
        in_specs=(P(rows, None), P(SHARD, None), P(rows, None)),
        out_specs=(P(rows), P(SHARD, None), P(rows)),
        check_vma=False,
    )
```

```python
import jax
import jax.numpy as jnp
from jax import lax
from jax.experimental import pallas as pl
from jax.experimental.pallas import tpu as pltpu
from jax.sharding import Mesh, PartitionSpec as P

AXES = ("zh", "core", "y", "x", "zl")
SIZES = (4, 2, 4, 4, 2)
SHARD = ("y", "x", "zl")

D = 768
HALF = 32
CHUNKS = 32
COLS = D // 128
BODY = COLS * HALF
CODED = BODY + 16
LIMIT = 32700.0
VMEM = 16 * 1024 * 1024


def diagonal(rows):
    r = lax.broadcasted_iota(jnp.int32, (rows, 128), 0) % HALF
    c = lax.broadcasted_iota(jnp.int32, (rows, 128), 1)
    return r == c


def to_lanes(column):
    return jnp.sum(jnp.where(diagonal(HALF), column, 0.0), 0, keepdims=True)


def to_column(row):
    return jnp.sum(jnp.where(diagonal(HALF), row, 0.0), 1, keepdims=True)


def code_of(values):
    most = jnp.max(jnp.abs(values), 1, keepdims=True)
    return jnp.ceil(jnp.log2(jnp.maximum(most, 1e-30)) * 256.0)


def quantize(values, code):
    scaled = values * (LIMIT * jnp.exp2(code * (-1.0 / 256.0)))
    return jnp.floor(scaled + 0.5).astype(jnp.int32).astype(jnp.int16)


def scale_of(code):
    return jnp.exp2(code * (1.0 / 256.0)) * (1.0 / LIMIT)


def footer(counts, codes):
    r = lax.broadcasted_iota(jnp.int32, (16, 128), 0)
    both = jnp.where(r == 0, counts, jnp.where(r == 1, codes, 0.0))
    return both.astype(jnp.int32).astype(jnp.int16)


TILE = 256
EACH = TILE // HALF


def is_named(t, place, labels):
    first, second, half = (place[i] for i in range(3))
    j = lax.broadcasted_iota(jnp.int32, (TILE, 1), 0)
    c = j // HALF
    shard = (c // 2) * first + t * second + c % 2
    k = shard * (2 * HALF) + half + j % HALF
    return jnp.where(k == labels, 1.0, 0.0)


def own_sums_kernel(place, labels, rows, out_ref):
    for t in range(4):
        hot = is_named(t, place, labels[...]).astype(jnp.bfloat16)
        out_ref[t * TILE : (t + 1) * TILE, :] = jnp.dot(
            hot, rows[...], preferred_element_type=jnp.float32
        )


def chip_sums_kernel(place, own_labels, labels, own_sums, rows, out_ref):
    for t in range(4):
        hot = is_named(t, place, labels[...])
        sums = own_sums[t * TILE : (t + 1) * TILE, :] + jnp.dot(
            hot.astype(jnp.bfloat16), rows[...], preferred_element_type=jnp.float32
        )
        hot = hot + is_named(t, place, own_labels[...])
        counts = jnp.sum(hot, 1, keepdims=True)
        code = code_of(sums)
        coded = quantize(sums, code)
        for c in range(EACH):
            part = slice(c * HALF, (c + 1) * HALF)
            for b in range(COLS):
                out_ref[t * EACH + c, block(b), :] = coded[part, b * 128 : (b + 1) * 128]
            out_ref[t * EACH + c, BODY:CODED, :] = footer(
                to_lanes(counts[part]), to_lanes(code[part])
            )


def block(b):
    return slice(b * HALF, (b + 1) * HALF)


def add_coded(ref, at, blocks, counts):
    foot = ref[at, BODY:CODED, :].astype(jnp.float32)
    scale = scale_of(to_column(foot[1:2, :]))
    blocks = [
        blocks[b] + ref[at, block(b), :].astype(jnp.float32) * scale
        for b in range(COLS)
    ]
    return blocks, counts + foot[0:1, :]


def nothing():
    zeros = [jnp.zeros((HALF, 128), jnp.float32) for _ in range(COLS)]
    return zeros, jnp.zeros((1, 128), jnp.float32)


def code_blocks(blocks):
    most = jnp.abs(blocks[0])
    for b in range(1, COLS):
        most = jnp.maximum(most, jnp.abs(blocks[b]))
    code = code_of(most)
    return [quantize(blocks[b], code) for b in range(COLS)], to_lanes(code)


def add_and_code(ref, sources, out_ref, to):
    blocks, counts = nothing()
    for at in sources:
        blocks, counts = add_coded(ref, at, blocks, counts)
    coded, codes = code_blocks(blocks)
    for b in range(COLS):
        out_ref[to, block(b), :] = coded[b]
    out_ref[to, BODY:CODED, :] = footer(counts, codes)


def first_sums_kernel(in_ref, c0, c1, c2, c3, out_ref, centers_ref):
    for c in range(EACH):
        add_and_code(in_ref, range(c, 4 * EACH, EACH), out_ref, c)
    for i, ref in enumerate((c0, c1, c2, c3)):
        n = ref.shape[0]
        centers_ref[i * n : (i + 1) * n] = ref[...]


def second_sums_kernel(in_ref, out_ref):
    add_and_code(in_ref, range(EACH), out_ref, 0)


def refine_kernel(own, one, two, three, refined_ref, coded_ref):
    even = add_coded(two, 0, *add_coded(own, 0, *nothing()))
    odd = add_coded(three, 0, *add_coded(one, 0, *nothing()))
    counts = to_column(even[1] + odd[1])
    refined = [(even[0][b] + odd[0][b]) / counts for b in range(COLS)]
    for b in range(COLS):
        refined_ref[:, b * 128 : (b + 1) * 128] = refined[b]
    coded, codes = code_blocks(refined)
    foot = footer(jnp.zeros_like(codes), codes)
    for c in range(EACH):
        for b in range(COLS):
            coded_ref[c, block(b), :] = coded[b]
        coded_ref[c, BODY:CODED, :] = foot


def nearest(value, least):
    n = value.shape[0]
    return jnp.minimum(least, jnp.min(value.reshape(n // 8, 8, value.shape[1]), 0))


def old_kernel(norms_ref, rows_ref, *refs):
    *centers, out_ref, turned_ref = refs
    turned_ref[...] = (rows_ref[...] * jnp.bfloat16(-2.0)).T
    turned = turned_ref[...]
    least = jnp.full((8, turned.shape[1]), jnp.inf, jnp.float32)
    for ref in centers:
        wide = ref[...].astype(jnp.float32)
        norm = jnp.sum(wide * wide, 1, keepdims=True)
        product = jnp.dot(ref[...], turned, preferred_element_type=jnp.float32)
        least = nearest(product + norm, least)
    out_ref[...] = norms_ref[...] + jnp.min(least, 0, keepdims=True)


def new_kernel(turned_ref, norms_ref, least_ref, *refs):
    *pieces, out_ref = refs
    turned = turned_ref[...]
    least = least_ref[...]
    for ref, t in [(ref, t) for ref in pieces for t in range(CHUNKS // EACH)]:
        high, low, scale, norm = [], [], [], []
        for c in range(t * EACH, (t + 1) * EACH):
            wide = jnp.concatenate(
                [ref[c, block(b), :].astype(jnp.float32) for b in range(COLS)], 1
            )
            top = wide.astype(jnp.bfloat16)
            high.append(top)
            low.append((wide - top.astype(jnp.float32)).astype(jnp.bfloat16))
            foot = ref[c, BODY:CODED, :].astype(jnp.float32)
            s = scale_of(to_column(foot[1:2, :]))
            scale.append(s)
            norm.append(jnp.sum(wide * wide, 1, keepdims=True) * (s * s))
        product = jnp.dot(
            jnp.concatenate(high, 0), turned, preferred_element_type=jnp.float32
        ) + jnp.dot(jnp.concatenate(low, 0), turned, preferred_element_type=jnp.float32)
        value = product * jnp.concatenate(scale, 0) + jnp.concatenate(norm, 0)
        least = nearest(value, least)
    if out_ref.shape == least.shape:
        out_ref[...] = least
    else:
        out_ref[...] = norms_ref[...] + jnp.min(least, 0, keepdims=True)


def call(kernel, out_shape, *args, flops=0, moved=0, smem=0):
    specs = [
        pl.BlockSpec(memory_space=pltpu.SMEM if i < smem else pltpu.VMEM)
        for i in range(len(args))
    ]
    many = isinstance(out_shape, tuple)
    out_specs = pl.BlockSpec(memory_space=pltpu.VMEM)
    return pl.pallas_call(
        kernel,
        out_shape=out_shape,
        in_specs=specs,
        out_specs=tuple([out_specs] * len(out_shape)) if many else out_specs,
        compiler_params=pltpu.CompilerParams(vmem_limit_bytes=VMEM),
        cost_estimate=pl.CostEstimate(
            flops=flops, bytes_accessed=moved, transcendentals=0
        ),
    )(*args)


def swap(value, axis):
    return lax.ppermute(value, axis, [(0, 1), (1, 0)])


def around_z(part):
    return [part] + [
        lax.ppermute(part, "zh", [(i, (i + k) % 4) for i in range(4)])
        for k in (1, 2, 3)
    ]


def spot(core, a, b, zl):
    y, x = (b, a) if core == 0 else (a, b)
    return ((core * 4 + y) * 4 + x) * 2 + zl


def fours():
    return [
        [spot(core, a, b, 0) // 2 for a in range(4)]
        for core in range(2)
        for b in range(4)
    ]


def eights():
    return [
        [spot(core, a, b, z) for b in range(4) for z in range(2)]
        for core in range(2)
        for a in range(4)
    ]


def exchange_four(value):
    return lax.all_to_all(
        value.reshape(4, -1, 128), ("core", "y", "x"), 0, 0, axis_index_groups=fours()
    ).reshape(value.shape)


def exchange_eight(value):
    return lax.all_to_all(
        value, ("core", "y", "x", "zl"), 0, 0, axis_index_groups=eights()
    )


def around(part, turn):
    parts = [part]
    for k in (1, 3, 2):
        pairs = []
        for core in range(2):
            for a in range(4):
                for b in range(4):
                    to = ((a + k) % 4, b) if turn == 0 else (a, (b + k) % 4)
                    pairs.append((spot(core, a, b, 0) // 2, spot(core, *to, 0) // 2))
        parts.append(lax.ppermute(part, ("core", "y", "x"), pairs))
    return parts


def after(first, values):
    return lax.optimization_barrier((first, *values))[1:]


def on_device(embeddings, centers, assignment):
    n = embeddings.shape[0]
    f32, bf16, i16 = jnp.float32, jnp.bfloat16, jnp.int16
    shape = jax.ShapeDtypeStruct

    def coded(chunks):
        return shape((chunks, CODED, 128), i16)

    core = lax.axis_index("core")
    first = core == 0
    place = jnp.stack(
        [jnp.where(first, 8, 2), jnp.where(first, 2, 8), core * HALF]
    ).astype(jnp.int32)

    labels = assignment.reshape(1, n)
    other_labels = swap(labels, "core")
    other_rows = swap(embeddings, "core")

    mine = lax.dynamic_slice(centers, (core * HALF, 0), (HALF, D))
    current = jnp.concatenate([mine, swap(mine, "zl")])
    (other_rows, current) = lax.optimization_barrier((other_rows, current))

    wide = embeddings.astype(f32)
    norms = jnp.sum(wide * wide, 1).reshape(1, n)

    sums = call(
        own_sums_kernel,
        shape((4 * TILE, D), f32),
        place, labels, embeddings,
        flops=2 * 1024 * n * D, moved=5 << 20, smem=1,
    )
    sums = call(
        chip_sums_kernel,
        coded(CHUNKS),
        place, labels, other_labels, sums, other_rows,
        flops=2 * 1024 * n * D, moved=6 << 20, smem=1,
    )

    (current,) = after(sums, (current,))
    sums, current = call(
        first_sums_kernel,
        (coded(EACH), shape((8 * HALF, D), bf16)),
        exchange_four(sums), *around(current, 0),
        flops=1 << 22, moved=3 << 20,
    )
    group = call(
        second_sums_kernel,
        coded(1),
        exchange_eight(sums),
        flops=1 << 20, moved=1 << 20,
    )
    (current,) = after(group, (current,))
    groups, current = lax.optimization_barrier((around_z(group), around(current, 1)))
    refined, code = call(
        refine_kernel,
        (shape((HALF, D), f32), coded(EACH)),
        *groups,
        flops=1 << 20, moved=1 << 20,
    )

    new = exchange_eight(code)
    new = exchange_four(
        jnp.broadcast_to(new[None], (4, *new.shape)).reshape(CHUNKS, CODED, 128)
    )

    current = list(after(refined, current))
    current_other = [swap(part, "core") for part in current]
    old_min, turned = call(
        old_kernel,
        (shape((1, n), f32), shape((D, n), bf16)),
        norms, embeddings, *current, *current_other,
        flops=2 * 2048 * n * D, moved=5 << 20,
    )

    refined_other = swap(refined, "core")
    refined_centers = jnp.concatenate(
        [
            jnp.where(first, refined, refined_other),
            jnp.where(first, refined_other, refined),
        ]
    )

    new, turned, refined_centers = lax.optimization_barrier(
        (new, turned, refined_centers)
    )
    new_other = swap(new, "core")
    least = jnp.full((8, n), jnp.inf, f32)
    for piece, result in ((new, 8), (new_other, 1)):
        least = call(
            new_kernel,
            shape((result, n), f32),
            turned, norms, least, piece,
            flops=4 * 1024 * n * D, moved=3 << 20,
        )
    return old_min.reshape(n), refined_centers, least.reshape(n)


def solution(mesh):
    fine = Mesh(mesh.devices.reshape(SIZES), AXES)
    rows = ("zh", "core") + SHARD
    return jax.shard_map(
        on_device,
        mesh=fine,
        in_specs=(P(rows, None), P(SHARD, None), P(rows, None)),
        out_specs=(P(rows), P(SHARD, None), P(rows)),
        check_vma=False,
    )
```

```python
import jax
import jax.numpy as jnp
from jax import lax
from jax.experimental import pallas as pl
from jax.experimental.pallas import tpu as pltpu
from jax.sharding import Mesh, PartitionSpec as P

AXES = ("zh", "core", "y", "x", "zl")
SIZES = (4, 2, 4, 4, 2)
SHARD = ("y", "x", "zl")

D = 768
HALF = 32
CHUNKS = 32
COLS = D // 128
BODY = COLS * HALF
CODED = BODY + 16
LIMIT = 32700.0
VMEM = 16 * 1024 * 1024


def diagonal(rows):
    r = lax.broadcasted_iota(jnp.int32, (rows, 128), 0) % HALF
    c = lax.broadcasted_iota(jnp.int32, (rows, 128), 1)
    return r == c


def to_lanes(column):
    return jnp.sum(jnp.where(diagonal(HALF), column, 0.0), 0, keepdims=True)


def to_column(row):
    return jnp.sum(jnp.where(diagonal(HALF), row, 0.0), 1, keepdims=True)


def code_of(values):
    most = jnp.max(jnp.abs(values), 1, keepdims=True)
    return jnp.ceil(jnp.log2(jnp.maximum(most, 1e-30)) * 256.0)


def quantize(values, code):
    scaled = values * (LIMIT * jnp.exp2(code * (-1.0 / 256.0)))
    return jnp.floor(scaled + 0.5).astype(jnp.int32).astype(jnp.int16)


def scale_of(code):
    return jnp.exp2(code * (1.0 / 256.0)) * (1.0 / LIMIT)


def footer(counts, codes):
    r = lax.broadcasted_iota(jnp.int32, (16, 128), 0)
    both = jnp.where(r == 0, counts, jnp.where(r == 1, codes, 0.0))
    return both.astype(jnp.int32).astype(jnp.int16)


TILE = 256
EACH = TILE // HALF


def is_named(t, place, labels):
    first, second, half = (place[i] for i in range(3))
    j = lax.broadcasted_iota(jnp.int32, (TILE, 1), 0)
    c = j // HALF
    shard = (c // 2) * first + t * second + c % 2
    k = shard * (2 * HALF) + half + j % HALF
    return jnp.where(k == labels, 1.0, 0.0)


def own_sums_kernel(place, labels, rows, out_ref):
    for t in range(4):
        hot = is_named(t, place, labels[...]).astype(jnp.bfloat16)
        out_ref[t * TILE : (t + 1) * TILE, :] = jnp.dot(
            hot, rows[...], preferred_element_type=jnp.float32
        )


def chip_sums_kernel(place, own_labels, labels, own_sums, rows, out_ref):
    for t in range(4):
        hot = is_named(t, place, labels[...])
        sums = own_sums[t * TILE : (t + 1) * TILE, :] + jnp.dot(
            hot.astype(jnp.bfloat16), rows[...], preferred_element_type=jnp.float32
        )
        hot = hot + is_named(t, place, own_labels[...])
        counts = jnp.sum(hot, 1, keepdims=True)
        code = code_of(sums)
        coded = quantize(sums, code)
        for c in range(EACH):
            part = slice(c * HALF, (c + 1) * HALF)
            for b in range(COLS):
                out_ref[t * EACH + c, block(b), :] = coded[part, b * 128 : (b + 1) * 128]
            out_ref[t * EACH + c, BODY:CODED, :] = footer(
                to_lanes(counts[part]), to_lanes(code[part])
            )


def block(b):
    return slice(b * HALF, (b + 1) * HALF)


def add_coded(ref, at, blocks, counts):
    foot = ref[at, BODY:CODED, :].astype(jnp.float32)
    scale = scale_of(to_column(foot[1:2, :]))
    blocks = [
        blocks[b] + ref[at, block(b), :].astype(jnp.float32) * scale
        for b in range(COLS)
    ]
    return blocks, counts + foot[0:1, :]


def nothing():
    zeros = [jnp.zeros((HALF, 128), jnp.float32) for _ in range(COLS)]
    return zeros, jnp.zeros((1, 128), jnp.float32)


def code_blocks(blocks):
    most = jnp.abs(blocks[0])
    for b in range(1, COLS):
        most = jnp.maximum(most, jnp.abs(blocks[b]))
    code = code_of(most)
    return [quantize(blocks[b], code) for b in range(COLS)], to_lanes(code)


def add_and_code(ref, sources, out_ref, to):
    blocks, counts = nothing()
    for at in sources:
        blocks, counts = add_coded(ref, at, blocks, counts)
    coded, codes = code_blocks(blocks)
    for b in range(COLS):
        out_ref[to, block(b), :] = coded[b]
    out_ref[to, BODY:CODED, :] = footer(counts, codes)


def first_sums_kernel(in_ref, out_ref):
    for c in range(EACH):
        add_and_code(in_ref, range(c, 4 * EACH, EACH), out_ref, c)


def second_sums_kernel(in_ref, c0, c1, c2, c3, out_ref, centers_ref):
    add_and_code(in_ref, range(EACH), out_ref, 0)
    for i, ref in enumerate((c0, c1, c2, c3)):
        n = ref.shape[0]
        centers_ref[i * n : (i + 1) * n] = ref[...]


def refine_kernel(own, one, two, three, refined_ref, coded_ref):
    even = add_coded(two, 0, *add_coded(own, 0, *nothing()))
    odd = add_coded(three, 0, *add_coded(one, 0, *nothing()))
    counts = to_column(even[1] + odd[1])
    refined = [(even[0][b] + odd[0][b]) / counts for b in range(COLS)]
    for b in range(COLS):
        refined_ref[:, b * 128 : (b + 1) * 128] = refined[b]
    coded, codes = code_blocks(refined)
    foot = footer(jnp.zeros_like(codes), codes)
    for c in range(EACH):
        for b in range(COLS):
            coded_ref[c, block(b), :] = coded[b]
        coded_ref[c, BODY:CODED, :] = foot


def nearest(value, least):
    n = value.shape[0]
    return jnp.minimum(least, jnp.min(value.reshape(n // 8, 8, value.shape[1]), 0))


def old_kernel(norms_ref, rows_ref, *refs):
    *centers, out_ref, turned_ref = refs
    turned_ref[...] = (rows_ref[...] * jnp.bfloat16(-2.0)).T
    turned = turned_ref[...]
    least = jnp.full((8, turned.shape[1]), jnp.inf, jnp.float32)
    for ref in centers:
        wide = ref[...].astype(jnp.float32)
        norm = jnp.sum(wide * wide, 1, keepdims=True)
        product = jnp.dot(ref[...], turned, preferred_element_type=jnp.float32)
        least = nearest(product + norm, least)
    out_ref[...] = norms_ref[...] + jnp.min(least, 0, keepdims=True)


def new_kernel(turned_ref, norms_ref, least_ref, *refs):
    *pieces, out_ref = refs
    turned = turned_ref[...]
    least = least_ref[...]
    for ref, t in [(ref, t) for ref in pieces for t in range(CHUNKS // EACH)]:
        high, low, scale, norm = [], [], [], []
        for c in range(t * EACH, (t + 1) * EACH):
            wide = jnp.concatenate(
                [ref[c, block(b), :].astype(jnp.float32) for b in range(COLS)], 1
            )
            top = wide.astype(jnp.bfloat16)
            high.append(top)
            low.append((wide - top.astype(jnp.float32)).astype(jnp.bfloat16))
            foot = ref[c, BODY:CODED, :].astype(jnp.float32)
            s = scale_of(to_column(foot[1:2, :]))
            scale.append(s)
            norm.append(jnp.sum(wide * wide, 1, keepdims=True) * (s * s))
        product = jnp.dot(
            jnp.concatenate(high, 0), turned, preferred_element_type=jnp.float32
        ) + jnp.dot(jnp.concatenate(low, 0), turned, preferred_element_type=jnp.float32)
        value = product * jnp.concatenate(scale, 0) + jnp.concatenate(norm, 0)
        least = nearest(value, least)
    if out_ref.shape == least.shape:
        out_ref[...] = least
    else:
        out_ref[...] = norms_ref[...] + jnp.min(least, 0, keepdims=True)


def call(kernel, out_shape, *args, flops=0, moved=0, smem=0):
    specs = [
        pl.BlockSpec(memory_space=pltpu.SMEM if i < smem else pltpu.VMEM)
        for i in range(len(args))
    ]
    many = isinstance(out_shape, tuple)
    out_specs = pl.BlockSpec(memory_space=pltpu.VMEM)
    return pl.pallas_call(
        kernel,
        out_shape=out_shape,
        in_specs=specs,
        out_specs=tuple([out_specs] * len(out_shape)) if many else out_specs,
        compiler_params=pltpu.CompilerParams(vmem_limit_bytes=VMEM),
        cost_estimate=pl.CostEstimate(
            flops=flops, bytes_accessed=moved, transcendentals=0
        ),
    )(*args)


def swap(value, axis):
    return lax.ppermute(value, axis, [(0, 1), (1, 0)])


def around_z(part):
    return [part] + [
        lax.ppermute(part, "zh", [(i, (i + k) % 4) for i in range(4)])
        for k in (1, 2, 3)
    ]


def spot(core, a, b, zl):
    y, x = (b, a) if core == 0 else (a, b)
    return ((core * 4 + y) * 4 + x) * 2 + zl


def fours():
    return [
        [spot(core, a, b, 0) // 2 for a in range(4)]
        for core in range(2)
        for b in range(4)
    ]


def eights():
    return [
        [spot(core, a, b, z) for b in range(4) for z in range(2)]
        for core in range(2)
        for a in range(4)
    ]


def exchange_four(value):
    return lax.all_to_all(
        value.reshape(4, -1, 128), ("core", "y", "x"), 0, 0, axis_index_groups=fours()
    ).reshape(value.shape)


def exchange_eight(value):
    return lax.all_to_all(
        value, ("core", "y", "x", "zl"), 0, 0, axis_index_groups=eights()
    )


def around(part, turn):
    parts = [part]
    for k in (1, 3, 2):
        pairs = []
        for core in range(2):
            for a in range(4):
                for b in range(4):
                    to = ((a + k) % 4, b) if turn == 0 else (a, (b + k) % 4)
                    pairs.append((spot(core, a, b, 0) // 2, spot(core, *to, 0) // 2))
        parts.append(lax.ppermute(part, ("core", "y", "x"), pairs))
    return parts


def after(first, values):
    return lax.optimization_barrier((first, *values))[1:]


def on_device(embeddings, centers, assignment):
    n = embeddings.shape[0]
    f32, bf16, i16 = jnp.float32, jnp.bfloat16, jnp.int16
    shape = jax.ShapeDtypeStruct

    def coded(chunks):
        return shape((chunks, CODED, 128), i16)

    core = lax.axis_index("core")
    first = core == 0
    place = jnp.stack(
        [jnp.where(first, 8, 2), jnp.where(first, 2, 8), core * HALF]
    ).astype(jnp.int32)

    labels = assignment.reshape(1, n)
    other_labels = swap(labels, "core")
    other_rows = swap(embeddings, "core")

    mine = lax.dynamic_slice(centers, (core * HALF, 0), (HALF, D))
    current = jnp.concatenate([mine, swap(mine, "zl")])
    (other_rows, current) = lax.optimization_barrier((other_rows, current))

    wide = embeddings.astype(f32)
    norms = jnp.sum(wide * wide, 1).reshape(1, n)

    sums = call(
        own_sums_kernel,
        shape((4 * TILE, D), f32),
        place, labels, embeddings,
        flops=2 * 1024 * n * D, moved=5 << 20, smem=1,
    )
    sums = call(
        chip_sums_kernel,
        coded(CHUNKS),
        place, labels, other_labels, sums, other_rows,
        flops=2 * 1024 * n * D, moved=6 << 20, smem=1,
    )

    sums = call(
        first_sums_kernel,
        coded(EACH),
        exchange_four(sums),
        flops=1 << 22, moved=3 << 20,
    )
    (current,) = after(sums, (current,))
    group, current = call(
        second_sums_kernel,
        (coded(1), shape((8 * HALF, D), bf16)),
        exchange_eight(sums), *around(current, 0),
        flops=1 << 20, moved=1 << 20,
    )
    (current,) = after(group, (current,))
    groups, current = lax.optimization_barrier((around_z(group), around(current, 1)))
    refined, code = call(
        refine_kernel,
        (shape((HALF, D), f32), coded(EACH)),
        *groups,
        flops=1 << 20, moved=1 << 20,
    )

    new = exchange_eight(code)

    current = list(after(refined, current))
    current_other = [swap(part, "core") for part in current]
    old_min, turned = call(
        old_kernel,
        (shape((1, n), f32), shape((D, n), bf16)),
        norms, embeddings, *current, *current_other,
        flops=2 * 2048 * n * D, moved=5 << 20,
    )

    refined_other = swap(refined, "core")
    refined_centers = jnp.concatenate(
        [
            jnp.where(first, refined, refined_other),
            jnp.where(first, refined_other, refined),
        ]
    )

    new, turned, refined_centers = lax.optimization_barrier(
        (new, turned, refined_centers)
    )
    new = exchange_four(
        jnp.broadcast_to(new[None], (4, *new.shape)).reshape(CHUNKS, CODED, 128)
    )
    new_other = swap(new, "core")
    least = jnp.full((8, n), jnp.inf, f32)
    for piece, result in ((new, 8), (new_other, 1)):
        least = call(
            new_kernel,
            shape((result, n), f32),
            turned, norms, least, piece,
            flops=4 * 1024 * n * D, moved=3 << 20,
        )
    return old_min.reshape(n), refined_centers, least.reshape(n)


def solution(mesh):
    fine = Mesh(mesh.devices.reshape(SIZES), AXES)
    rows = ("zh", "core") + SHARD
    return jax.shard_map(
        on_device,
        mesh=fine,
        in_specs=(P(rows, None), P(SHARD, None), P(rows, None)),
        out_specs=(P(rows), P(SHARD, None), P(rows)),
        check_vma=False,
    )
```

```python
import jax
import jax.numpy as jnp
from jax import lax
from jax.experimental import pallas as pl
from jax.experimental.pallas import tpu as pltpu
from jax.sharding import Mesh, PartitionSpec as P

AXES = ("zh", "core", "y", "x", "zl")
SIZES = (4, 2, 4, 4, 2)
SHARD = ("y", "x", "zl")

D = 768
HALF = 32
CHUNKS = 32
COLS = D // 128
BODY = COLS * HALF
CODED = BODY + 16
EIGHTH = 8
SMALL = COLS * EIGHTH + 16
LIMIT = 32700.0
VMEM = 16 * 1024 * 1024


def diagonal(rows):
    r = lax.broadcasted_iota(jnp.int32, (rows, 128), 0) % HALF
    c = lax.broadcasted_iota(jnp.int32, (rows, 128), 1)
    return r == c


def to_lanes(column):
    return jnp.sum(jnp.where(diagonal(HALF), column, 0.0), 0, keepdims=True)


def to_column(row):
    return jnp.sum(jnp.where(diagonal(HALF), row, 0.0), 1, keepdims=True)


def code_of(values):
    most = jnp.max(jnp.abs(values), 1, keepdims=True)
    return jnp.ceil(jnp.log2(jnp.maximum(most, 1e-30)) * 256.0)


def scaled(values, code):
    return jnp.floor(values * (LIMIT * jnp.exp2(code * (-1.0 / 256.0))) + 0.5)


def whole(values):
    return values.astype(jnp.int32).astype(jnp.int16)


def quantize(values, code):
    return whole(scaled(values, code))


def scale_of(code):
    return jnp.exp2(code * (1.0 / 256.0)) * (1.0 / LIMIT)


def footer(counts, codes):
    r = lax.broadcasted_iota(jnp.int32, (16, 128), 0)
    both = jnp.where(r == 0, counts, jnp.where(r == 1, codes, 0.0))
    return both.astype(jnp.int32).astype(jnp.int16)


TILE = 256
EACH = TILE // HALF


def is_named(t, place, labels):
    first, second, half = (place[i] for i in range(3))
    j = lax.broadcasted_iota(jnp.int32, (TILE, 1), 0)
    c = j // HALF
    shard = (c // 2) * first + t * second + c % 2
    k = shard * (2 * HALF) + half + j % HALF
    return jnp.where(k == labels, 1.0, 0.0)


def own_sums_kernel(place, labels, rows, out_ref):
    for t in range(4):
        hot = is_named(t, place, labels[...]).astype(jnp.bfloat16)
        out_ref[t * TILE : (t + 1) * TILE, :] = jnp.dot(
            hot, rows[...], preferred_element_type=jnp.float32
        )


def chip_sums_kernel(place, own_labels, labels, own_sums, rows, out_ref):
    for t in range(4):
        hot = is_named(t, place, labels[...])
        sums = own_sums[t * TILE : (t + 1) * TILE, :] + jnp.dot(
            hot.astype(jnp.bfloat16), rows[...], preferred_element_type=jnp.float32
        )
        hot = hot + is_named(t, place, own_labels[...])
        counts = jnp.sum(hot, 1, keepdims=True)
        code = code_of(sums)
        coded = quantize(sums, code)
        for c in range(EACH):
            part = slice(c * HALF, (c + 1) * HALF)
            for b in range(COLS):
                out_ref[t * EACH + c, block(b), :] = coded[part, b * 128 : (b + 1) * 128]
            out_ref[t * EACH + c, BODY:CODED, :] = footer(
                to_lanes(counts[part]), to_lanes(code[part])
            )


def block(b):
    return slice(b * HALF, (b + 1) * HALF)


def add_coded(ref, at, blocks, counts):
    foot = ref[at, BODY:CODED, :].astype(jnp.float32)
    scale = scale_of(to_column(foot[1:2, :]))
    blocks = [
        blocks[b] + ref[at, block(b), :].astype(jnp.float32) * scale
        for b in range(COLS)
    ]
    return blocks, counts + foot[0:1, :]


def nothing():
    zeros = [jnp.zeros((HALF, 128), jnp.float32) for _ in range(COLS)]
    return zeros, jnp.zeros((1, 128), jnp.float32)


def first_sums_kernel(in_ref, out_ref):
    for c in range(EACH):
        blocks, counts = nothing()
        for at in range(c, 4 * EACH, EACH):
            blocks, counts = add_coded(in_ref, at, blocks, counts)
        most = jnp.abs(blocks[0])
        for b in range(1, COLS):
            most = jnp.maximum(most, jnp.abs(blocks[b]))
        code = code_of(most)
        values = [scaled(blocks[b], code) for b in range(COLS)]
        last = [jnp.broadcast_to(v, (HALF, 128)) for v in (code, to_column(counts))]
        for z in range(4):
            part = slice(z * EIGHTH, (z + 1) * EIGHTH)
            for t, pair in enumerate(
                (values[0:2], values[2:4], values[4:6], last)
            ):
                both = jnp.concatenate([v[part] for v in pair], 0)
                out_ref[z * EACH + c, tile_of(t), :] = whole(both)


def tile_of(t):
    return slice(t * 16, (t + 1) * 16)


def refine_kernel(place, in_ref, c0, c1, c2, c3, out_ref, centers_ref):
    total = [jnp.zeros((16, 128), jnp.float32) for _ in range(3)]
    counts = jnp.zeros((EIGHTH, 128), jnp.float32)
    for at in range(CHUNKS):
        foot = in_ref[at, tile_of(3), :].astype(jnp.float32)
        scale = scale_of(foot[:EIGHTH])
        scale = jnp.concatenate([scale, scale], 0)
        for t in range(3):
            total[t] += in_ref[at, tile_of(t), :].astype(jnp.float32) * scale
        counts = counts + foot[EIGHTH:]
    counts = jnp.concatenate([counts, counts], 0)
    lane = lax.broadcasted_iota(jnp.int32, (16, 128), 1)
    foot = jnp.zeros((16, 128), jnp.float32)
    coded = []
    for t in range(3):
        refined = total[t] / counts
        code = code_of(refined)
        coded.append(whole(scaled(refined, code)))
        foot = jnp.where(lane == place[3] * 3 + t, code, foot)
    coded.append(whole(foot))
    for at in range(CHUNKS):
        for t in range(4):
            out_ref[at, tile_of(t), :] = coded[t]
    for i, ref in enumerate((c0, c1, c2, c3)):
        n = ref.shape[0]
        centers_ref[i * n : (i + 1) * n] = ref[...]


def decode(load, scales):
    rows = []
    for z in range(4):
        tiles = [
            load(z, t).astype(jnp.float32) * scales[:, z * 3 + t : z * 3 + t + 1]
            for t in range(3)
        ]
        rows.append(
            jnp.concatenate(
                [tile[h * EIGHTH : (h + 1) * EIGHTH] for tile in tiles for h in range(2)],
                1,
            )
        )
    return jnp.concatenate(rows, 0)


def merged_foot(ref, c):
    foot = ref[c, tile_of(3), :].astype(jnp.float32)
    for z in range(1, 4):
        foot = foot + ref[z * EACH + c, tile_of(3), :].astype(jnp.float32)
    return foot


def repack_kernel(place, in_ref, out_ref, refined_ref):
    for c in range(EACH):
        foot = whole(merged_foot(in_ref, c))
        for k in range(4):
            for z in range(4):
                out_ref[k * EACH + c, z * 48 : (z + 1) * 48, :] = in_ref[
                    z * EACH + c, 0:48, :
                ]
            out_ref[k * EACH + c, BODY:CODED, :] = foot
    own = place[4]
    refined_ref[...] = decode(
        lambda z, t: in_ref[z * EACH + own, tile_of(t), :],
        scale_of(merged_foot(in_ref, own)),
    )


def nearest(value, least):
    n = value.shape[0]
    return jnp.minimum(least, jnp.min(value.reshape(n // 8, 8, value.shape[1]), 0))


def old_kernel(norms_ref, rows_ref, *refs):
    *centers, out_ref, turned_ref = refs
    turned_ref[...] = (rows_ref[...] * jnp.bfloat16(-2.0)).T
    turned = turned_ref[...]
    least = jnp.full((8, turned.shape[1]), jnp.inf, jnp.float32)
    for ref in centers:
        wide = ref[...].astype(jnp.float32)
        norm = jnp.sum(wide * wide, 1, keepdims=True)
        product = jnp.dot(ref[...], turned, preferred_element_type=jnp.float32)
        least = nearest(product + norm, least)
    out_ref[...] = norms_ref[...] + jnp.min(least, 0, keepdims=True)


def new_min(turned_ref, piece, least_ref):
    turned = turned_ref[...]
    least = least_ref[...]
    for t in range(CHUNKS // EACH):
        high, low, norm = [], [], []
        for c in range(t * EACH, (t + 1) * EACH):
            wide = decode(
                lambda z, i, c=c: piece[c, z * 48 + i * 16 : z * 48 + i * 16 + 16, :],
                scale_of(piece[c, BODY:CODED, :].astype(jnp.float32)),
            )
            top = wide.astype(jnp.bfloat16)
            high.append(top)
            low.append((wide - top.astype(jnp.float32)).astype(jnp.bfloat16))
            norm.append(jnp.sum(wide * wide, 1, keepdims=True))
        product = jnp.dot(
            jnp.concatenate(high, 0), turned, preferred_element_type=jnp.float32
        ) + jnp.dot(jnp.concatenate(low, 0), turned, preferred_element_type=jnp.float32)
        least = nearest(product + jnp.concatenate(norm, 0), least)
    return least


def new_own_kernel(turned_ref, piece, least_ref, out_ref):
    out_ref[...] = new_min(turned_ref, piece, least_ref)


def new_other_kernel(
    place, turned_ref, piece, least_ref, norms_ref, own, other, out_ref, refined_ref
):
    least = new_min(turned_ref, piece, least_ref)
    out_ref[...] = norms_ref[...] + jnp.min(least, 0, keepdims=True)
    half = place[2]
    refined_ref[pl.ds(pl.multiple_of(half, HALF), HALF), :] = own[...]
    refined_ref[pl.ds(pl.multiple_of(HALF - half, HALF), HALF), :] = other[...]


def call(kernel, out_shape, *args, flops=0, moved=0, smem=0):
    specs = [
        pl.BlockSpec(memory_space=pltpu.SMEM if i < smem else pltpu.VMEM)
        for i in range(len(args))
    ]
    many = isinstance(out_shape, tuple)
    out_specs = pl.BlockSpec(memory_space=pltpu.VMEM)
    return pl.pallas_call(
        kernel,
        out_shape=out_shape,
        in_specs=specs,
        out_specs=tuple([out_specs] * len(out_shape)) if many else out_specs,
        compiler_params=pltpu.CompilerParams(vmem_limit_bytes=VMEM),
        cost_estimate=pl.CostEstimate(
            flops=flops, bytes_accessed=moved, transcendentals=0
        ),
    )(*args)


def swap(value, axis):
    return lax.ppermute(value, axis, [(0, 1), (1, 0)])


def spot(core, a, b, zl):
    y, x = (b, a) if core == 0 else (a, b)
    return ((core * 4 + y) * 4 + x) * 2 + zl


def fours():
    return [
        [spot(core, a, b, 0) // 2 for a in range(4)]
        for core in range(2)
        for b in range(4)
    ]


def many():
    return [
        [zh * 64 + spot(core, a, b, z) for zh in range(4) for b in range(4) for z in range(2)]
        for core in range(2)
        for a in range(4)
    ]


def exchange_four(value):
    return lax.all_to_all(
        value.reshape(4, -1, 128), ("core", "y", "x"), 0, 0, axis_index_groups=fours()
    ).reshape(value.shape)


def exchange_many(value):
    return lax.all_to_all(value, AXES, 0, 0, axis_index_groups=many())


def around(part, turn):
    parts = [part]
    for k in (1, 3, 2):
        pairs = []
        for core in range(2):
            for a in range(4):
                for b in range(4):
                    to = ((a + k) % 4, b) if turn == 0 else (a, (b + k) % 4)
                    pairs.append((spot(core, a, b, 0) // 2, spot(core, *to, 0) // 2))
        parts.append(lax.ppermute(part, ("core", "y", "x"), pairs))
    return parts


def after(first, values):
    return lax.optimization_barrier((first, *values))[1:]


def on_device(embeddings, centers, assignment):
    n = embeddings.shape[0]
    f32, bf16, i16 = jnp.float32, jnp.bfloat16, jnp.int16
    shape = jax.ShapeDtypeStruct

    def coded(chunks):
        return shape((chunks, CODED, 128), i16)

    zh, core, y, x, zl = (lax.axis_index(name) for name in AXES)
    first = core == 0
    place = jnp.stack(
        [
            jnp.where(first, 8, 2),
            jnp.where(first, 2, 8),
            core * HALF,
            zh,
            jnp.where(first, y, x) * 2 + zl,
        ]
    ).astype(jnp.int32)

    labels = assignment.reshape(1, n)
    other_labels = swap(labels, "core")
    other_rows = swap(embeddings, "core")

    mine = lax.dynamic_slice(centers, (core * HALF, 0), (HALF, D))
    current = jnp.concatenate([mine, swap(mine, "zl")])
    (other_rows, current) = lax.optimization_barrier((other_rows, current))

    wide = embeddings.astype(f32)
    norms = jnp.sum(wide * wide, 1).reshape(1, n)

    sums = call(
        own_sums_kernel,
        shape((4 * TILE, D), f32),
        place, labels, embeddings,
        flops=2 * 1024 * n * D, moved=5 << 20, smem=1,
    )
    sums = call(
        chip_sums_kernel,
        coded(CHUNKS),
        place, labels, other_labels, sums, other_rows,
        flops=2 * 1024 * n * D, moved=6 << 20, smem=1,
    )

    small = shape((CHUNKS, SMALL, 128), i16)
    sums = call(
        first_sums_kernel,
        small,
        exchange_four(sums),
        flops=1 << 22, moved=3 << 20,
    )
    (current,) = after(sums, (current,))
    code, current = call(
        refine_kernel,
        (small, shape((8 * HALF, D), bf16)),
        place, exchange_many(sums), *around(current, 0),
        flops=1 << 20, moved=2 << 20, smem=1,
    )

    code, current = lax.optimization_barrier((exchange_many(code), around(current, 1)))
    code, refined = call(
        repack_kernel,
        (coded(CHUNKS), shape((HALF, D), f32)),
        place, code,
        flops=1 << 20, moved=3 << 20, smem=1,
    )
    new = exchange_four(code)
    current = list(after(refined, current))
    current_other = [swap(part, "core") for part in current]
    old_min, turned = call(
        old_kernel,
        (shape((1, n), f32), shape((D, n), bf16)),
        norms, embeddings, *current, *current_other,
        flops=2 * 2048 * n * D, moved=5 << 20,
    )
    refined_other = swap(refined, "core")
    new, turned, refined_other = lax.optimization_barrier((new, turned, refined_other))
    new_other = swap(new, "core")
    least = call(
        new_own_kernel,
        shape((8, n), f32),
        turned, new, jnp.full((8, n), jnp.inf, f32),
        flops=4 * 1024 * n * D, moved=3 << 20,
    )
    new_min, refined_centers = call(
        new_other_kernel,
        (shape((1, n), f32), shape((2 * HALF, D), f32)),
        place, turned, new_other, least, norms, refined, refined_other,
        flops=4 * 1024 * n * D, moved=3 << 20, smem=1,
    )
    return old_min.reshape(n), refined_centers, new_min.reshape(n)


def solution(mesh):
    fine = Mesh(mesh.devices.reshape(SIZES), AXES)
    rows = ("zh", "core") + SHARD
    return jax.shard_map(
        on_device,
        mesh=fine,
        in_specs=(P(rows, None), P(SHARD, None), P(rows, None)),
        out_specs=(P(rows), P(SHARD, None), P(rows)),
        check_vma=False,
    )
```

```python
import jax
import jax.numpy as jnp
from jax import lax
from jax.experimental import pallas as pl
from jax.experimental.pallas import tpu as pltpu
from jax.sharding import Mesh, PartitionSpec as P

AXES = ("zh", "core", "y", "x", "zl")
SIZES = (4, 2, 4, 4, 2)
SHARD = ("y", "x", "zl")

D = 768
HALF = 32
CHUNKS = 32
COLS = D // 128
BODY = COLS * HALF
CODED = BODY + 16
LIMIT = 32700.0
VMEM = 16 * 1024 * 1024


def diagonal(rows):
    r = lax.broadcasted_iota(jnp.int32, (rows, 128), 0) % HALF
    c = lax.broadcasted_iota(jnp.int32, (rows, 128), 1)
    return r == c


def to_lanes(column):
    return jnp.sum(jnp.where(diagonal(HALF), column, 0.0), 0, keepdims=True)


def to_column(row):
    return jnp.sum(jnp.where(diagonal(HALF), row, 0.0), 1, keepdims=True)


def code_of(values):
    most = jnp.max(jnp.abs(values), 1, keepdims=True)
    return jnp.ceil(jnp.log2(jnp.maximum(most, 1e-30)) * 256.0)


def quantize(values, code):
    scaled = values * (LIMIT * jnp.exp2(code * (-1.0 / 256.0)))
    return jnp.floor(scaled + 0.5).astype(jnp.int32).astype(jnp.int16)


def scale_of(code):
    return jnp.exp2(code * (1.0 / 256.0)) * (1.0 / LIMIT)


def footer(counts, codes):
    r = lax.broadcasted_iota(jnp.int32, (16, 128), 0)
    both = jnp.where(r == 0, counts, jnp.where(r == 1, codes, 0.0))
    return both.astype(jnp.int32).astype(jnp.int16)


TILE = 256
EACH = TILE // HALF


def is_named(t, place, labels):
    first, second, half = (place[i] for i in range(3))
    within = lax.broadcasted_iota(jnp.int32, (HALF, 1), 0) + half
    k = jnp.concatenate(
        [
            within + ((c // 2) * first + t * second + c % 2) * (2 * HALF)
            for c in range(EACH)
        ],
        0,
    )
    return jnp.where(k == labels, 1.0, 0.0)


def own_sums_kernel(place, labels, rows, out_ref):
    for t in range(4):
        hot = is_named(t, place, labels[...]).astype(jnp.bfloat16)
        out_ref[t * TILE : (t + 1) * TILE, :] = jnp.dot(
            hot, rows[...], preferred_element_type=jnp.float32
        )


def chip_sums_kernel(place, own_labels, labels, own_sums, rows, out_ref):
    for t in range(4):
        hot = is_named(t, place, labels[...])
        sums = own_sums[t * TILE : (t + 1) * TILE, :] + jnp.dot(
            hot.astype(jnp.bfloat16), rows[...], preferred_element_type=jnp.float32
        )
        hot = hot + is_named(t, place, own_labels[...])
        counts = jnp.sum(hot, 1, keepdims=True)
        code = code_of(sums)
        coded = quantize(sums, code)
        for c in range(EACH):
            part = slice(c * HALF, (c + 1) * HALF)
            for b in range(COLS):
                out_ref[t * EACH + c, block(b), :] = coded[part, b * 128 : (b + 1) * 128]
            out_ref[t * EACH + c, BODY:CODED, :] = footer(
                to_lanes(counts[part]), to_lanes(code[part])
            )


def block(b):
    return slice(b * HALF, (b + 1) * HALF)


def add_coded(ref, at, blocks, counts):
    foot = ref[at, BODY:CODED, :].astype(jnp.float32)
    scale = scale_of(to_column(foot[1:2, :]))
    blocks = [
        blocks[b] + ref[at, block(b), :].astype(jnp.float32) * scale
        for b in range(COLS)
    ]
    return blocks, counts + foot[0:1, :]


def nothing():
    zeros = [jnp.zeros((HALF, 128), jnp.float32) for _ in range(COLS)]
    return zeros, jnp.zeros((1, 128), jnp.float32)


def code_blocks(blocks):
    most = jnp.abs(blocks[0])
    for b in range(1, COLS):
        most = jnp.maximum(most, jnp.abs(blocks[b]))
    code = code_of(most)
    return [quantize(blocks[b], code) for b in range(COLS)], to_lanes(code)


def add_and_code(ref, sources, out_ref, to):
    blocks, counts = nothing()
    for at in sources:
        blocks, counts = add_coded(ref, at, blocks, counts)
    coded, codes = code_blocks(blocks)
    for b in range(COLS):
        out_ref[to, block(b), :] = coded[b]
    out_ref[to, BODY:CODED, :] = footer(counts, codes)


def first_sums_kernel(in_ref, out_ref):
    for c in range(EACH):
        add_and_code(in_ref, range(c, 4 * EACH, EACH), out_ref, c)


def second_sums_kernel(in_ref, c0, c1, c2, c3, out_ref, centers_ref):
    add_and_code(in_ref, range(EACH), out_ref, 0)
    for i, ref in enumerate((c0, c1, c2, c3)):
        n = ref.shape[0]
        centers_ref[i * n : (i + 1) * n] = ref[...]


def refine_kernel(own, one, two, three, refined_ref, coded_ref):
    even = add_coded(two, 0, *add_coded(own, 0, *nothing()))
    odd = add_coded(three, 0, *add_coded(one, 0, *nothing()))
    counts = to_column(even[1] + odd[1])
    refined = [(even[0][b] + odd[0][b]) / counts for b in range(COLS)]
    for b in range(COLS):
        refined_ref[:, b * 128 : (b + 1) * 128] = refined[b]
    coded, codes = code_blocks(refined)
    foot = footer(jnp.zeros_like(codes), codes)
    for c in range(EACH):
        for b in range(COLS):
            coded_ref[c, block(b), :] = coded[b]
        coded_ref[c, BODY:CODED, :] = foot


def nearest(value, least):
    n = value.shape[0]
    return jnp.minimum(least, jnp.min(value.reshape(n // 8, 8, value.shape[1]), 0))


def turn_kernel(rows_ref, turned_ref, norms_ref):
    turned_ref[...] = (rows_ref[...] * jnp.bfloat16(-2.0)).T
    total = jnp.zeros((8, turned_ref.shape[1]), jnp.float32)
    for i in range(D // 16):
        wide = turned_ref[i * 16 : (i + 1) * 16, :].astype(jnp.float32)
        wide = wide * wide
        total = total + (wide[:8] + wide[8:])
    norms_ref[...] = jnp.sum(total, 0, keepdims=True) * 0.25


def old_kernel(norms_ref, turned_ref, *refs):
    *centers, out_ref = refs
    turned = turned_ref[...]
    least = jnp.full((8, turned.shape[1]), jnp.inf, jnp.float32)
    for ref in centers:
        wide = ref[...].astype(jnp.float32)
        norm = jnp.sum(wide * wide, 1, keepdims=True)
        product = jnp.dot(ref[...], turned, preferred_element_type=jnp.float32)
        least = nearest(product + norm, least)
    out_ref[...] = norms_ref[...] + jnp.min(least, 0, keepdims=True)


def new_min(turned_ref, piece, least_ref):
    turned = turned_ref[...]
    least = least_ref[...]
    for t in range(CHUNKS // EACH):
        high, low, scale, norm = [], [], [], []
        for c in range(t * EACH, (t + 1) * EACH):
            wide = jnp.concatenate(
                [piece[c, block(b), :].astype(jnp.float32) for b in range(COLS)], 1
            )
            top = wide.astype(jnp.bfloat16)
            high.append(top)
            low.append((wide - top.astype(jnp.float32)).astype(jnp.bfloat16))
            foot = piece[c, BODY:CODED, :].astype(jnp.float32)
            s = scale_of(to_column(foot[1:2, :]))
            scale.append(s)
            norm.append(jnp.sum(wide * wide, 1, keepdims=True) * (s * s))
        product = jnp.dot(
            jnp.concatenate(high, 0), turned, preferred_element_type=jnp.float32
        ) + jnp.dot(jnp.concatenate(low, 0), turned, preferred_element_type=jnp.float32)
        value = product * jnp.concatenate(scale, 0) + jnp.concatenate(norm, 0)
        least = nearest(value, least)
    return least


def new_own_kernel(turned_ref, piece, least_ref, out_ref):
    out_ref[...] = new_min(turned_ref, piece, least_ref)


def new_other_kernel(
    place, turned_ref, piece, least_ref, norms_ref, own, other, out_ref, refined_ref
):
    least = new_min(turned_ref, piece, least_ref)
    out_ref[...] = norms_ref[...] + jnp.min(least, 0, keepdims=True)
    half = place[2]
    refined_ref[pl.ds(pl.multiple_of(half, HALF), HALF), :] = own[...]
    refined_ref[pl.ds(pl.multiple_of(HALF - half, HALF), HALF), :] = other[...]


def call(kernel, out_shape, *args, flops=0, moved=0, smem=0):
    specs = [
        pl.BlockSpec(memory_space=pltpu.SMEM if i < smem else pltpu.VMEM)
        for i in range(len(args))
    ]
    many = isinstance(out_shape, tuple)
    out_specs = pl.BlockSpec(memory_space=pltpu.VMEM)
    return pl.pallas_call(
        kernel,
        out_shape=out_shape,
        in_specs=specs,
        out_specs=tuple([out_specs] * len(out_shape)) if many else out_specs,
        compiler_params=pltpu.CompilerParams(vmem_limit_bytes=VMEM),
        cost_estimate=pl.CostEstimate(
            flops=flops, bytes_accessed=moved, transcendentals=0
        ),
    )(*args)


def swap(value, axis):
    return lax.ppermute(value, axis, [(0, 1), (1, 0)])


def around_z(part):
    return [part] + [
        lax.ppermute(part, "zh", [(i, (i + k) % 4) for i in range(4)])
        for k in (1, 2, 3)
    ]


def spot(core, a, b, zl):
    y, x = (b, a) if core == 0 else (a, b)
    return ((core * 4 + y) * 4 + x) * 2 + zl


def fours():
    return [
        [spot(core, a, b, 0) // 2 for a in range(4)]
        for core in range(2)
        for b in range(4)
    ]


def eights():
    return [
        [spot(core, a, b, z) for b in range(4) for z in range(2)]
        for core in range(2)
        for a in range(4)
    ]


def exchange_four(value):
    return lax.all_to_all(
        value.reshape(4, -1, 128), ("core", "y", "x"), 0, 0, axis_index_groups=fours()
    ).reshape(value.shape)


def exchange_eight(value):
    return lax.all_to_all(
        value, ("core", "y", "x", "zl"), 0, 0, axis_index_groups=eights()
    )


def around(part, turn):
    parts = [part]
    for k in (1, 3, 2):
        pairs = []
        for core in range(2):
            for a in range(4):
                for b in range(4):
                    to = ((a + k) % 4, b) if turn == 0 else (a, (b + k) % 4)
                    pairs.append((spot(core, a, b, 0) // 2, spot(core, *to, 0) // 2))
        parts.append(lax.ppermute(part, ("core", "y", "x"), pairs))
    return parts


def after(first, values):
    return lax.optimization_barrier((first, *values))[1:]


def on_device(embeddings, centers, assignment):
    n = embeddings.shape[0]
    f32, bf16, i16 = jnp.float32, jnp.bfloat16, jnp.int16
    shape = jax.ShapeDtypeStruct

    def coded(chunks):
        return shape((chunks, CODED, 128), i16)

    core = lax.axis_index("core")
    first = core == 0
    place = jnp.stack(
        [jnp.where(first, 8, 2), jnp.where(first, 2, 8), core * HALF]
    ).astype(jnp.int32)

    labels = assignment.reshape(1, n)
    other_labels = swap(labels, "core")
    other_rows = swap(embeddings, "core")

    mine = lax.dynamic_slice(centers, (core * HALF, 0), (HALF, D))
    current = jnp.concatenate([mine, swap(mine, "zl")])
    (other_rows, current) = lax.optimization_barrier((other_rows, current))

    sums = call(
        own_sums_kernel,
        shape((4 * TILE, D), f32),
        place, labels, embeddings,
        flops=2 * 1024 * n * D, moved=5 << 20, smem=1,
    )
    sums = call(
        chip_sums_kernel,
        coded(CHUNKS),
        place, labels, other_labels, sums, other_rows,
        flops=2 * 1024 * n * D, moved=6 << 20, smem=1,
    )

    sums = call(
        first_sums_kernel,
        coded(EACH),
        exchange_four(sums),
        flops=1 << 22, moved=3 << 20,
    )
    current, rows = after(sums, (current, embeddings))
    turned, norms = call(
        turn_kernel,
        (shape((D, n), bf16), shape((1, n), f32)),
        rows,
        flops=4 * n * D, moved=4 << 20,
    )
    sums, turned = lax.optimization_barrier((exchange_eight(sums), turned))
    group, current = call(
        second_sums_kernel,
        (coded(1), shape((8 * HALF, D), bf16)),
        sums, *around(current, 0),
        flops=1 << 20, moved=1 << 20,
    )
    (current,) = after(group, (current,))
    groups, current = lax.optimization_barrier((around_z(group), around(current, 1)))
    refined, code = call(
        refine_kernel,
        (shape((HALF, D), f32), coded(EACH)),
        *groups,
        flops=1 << 20, moved=1 << 20,
    )

    new = exchange_eight(code)

    current = list(after(refined, current))
    current_other = [swap(part, "core") for part in current]
    old_min = call(
        old_kernel,
        shape((1, n), f32),
        norms, turned, *current, *current_other,
        flops=2 * 2048 * n * D, moved=5 << 20,
    )
    refined_other = swap(refined, "core")
    new, old_min, refined_other = lax.optimization_barrier((new, old_min, refined_other))
    new = exchange_four(
        jnp.broadcast_to(new[None], (4, *new.shape)).reshape(CHUNKS, CODED, 128)
    )
    new_other = swap(new, "core")
    least = call(
        new_own_kernel,
        shape((8, n), f32),
        turned, new, jnp.full((8, n), jnp.inf, f32),
        flops=4 * 1024 * n * D, moved=3 << 20,
    )
    new_min, refined_centers = call(
        new_other_kernel,
        (shape((1, n), f32), shape((2 * HALF, D), f32)),
        place, turned, new_other, least, norms, refined, refined_other,
        flops=4 * 1024 * n * D, moved=3 << 20, smem=1,
    )
    return old_min.reshape(n), refined_centers, new_min.reshape(n)


def solution(mesh):
    fine = Mesh(mesh.devices.reshape(SIZES), AXES)
    rows = ("zh", "core") + SHARD
    return jax.shard_map(
        on_device,
        mesh=fine,
        in_specs=(P(rows, None), P(SHARD, None), P(rows, None)),
        out_specs=(P(rows), P(SHARD, None), P(rows)),
        check_vma=False,
    )
```

```python
import jax
import jax.numpy as jnp
from jax import lax
from jax.experimental import pallas as pl
from jax.experimental.pallas import tpu as pltpu
from jax.sharding import Mesh, PartitionSpec as P

AXES = ("zh", "core", "y", "x", "zl")
SIZES = (4, 2, 4, 4, 2)
SHARD = ("y", "x", "zl")

D = 768
HALF = 32
CHUNKS = 32
COLS = D // 128
BODY = COLS * HALF
CODED = BODY + 16
LIMIT = 32700.0
VMEM = 16 * 1024 * 1024


def diagonal(rows):
    r = lax.broadcasted_iota(jnp.int32, (rows, 128), 0) % HALF
    c = lax.broadcasted_iota(jnp.int32, (rows, 128), 1)
    return r == c


def to_lanes(column):
    return jnp.sum(jnp.where(diagonal(HALF), column, 0.0), 0, keepdims=True)


def to_column(row):
    return jnp.sum(jnp.where(diagonal(HALF), row, 0.0), 1, keepdims=True)


def code_of(values):
    most = jnp.max(jnp.abs(values), 1, keepdims=True)
    return jnp.ceil(jnp.log2(jnp.maximum(most, 1e-30)) * 256.0)


def quantize(values, code):
    scaled = values * (LIMIT * jnp.exp2(code * (-1.0 / 256.0)))
    return jnp.floor(scaled + 0.5).astype(jnp.int32).astype(jnp.int16)


def scale_of(code):
    return jnp.exp2(code * (1.0 / 256.0)) * (1.0 / LIMIT)


def footer(counts, codes):
    r = lax.broadcasted_iota(jnp.int32, (16, 128), 0)
    both = jnp.where(r == 0, counts, jnp.where(r == 1, codes, 0.0))
    return both.astype(jnp.int32).astype(jnp.int16)


TILE = 256
EACH = TILE // HALF


def is_named(t, place, labels):
    first, second, half = (place[i] for i in range(3))
    within = lax.broadcasted_iota(jnp.int32, (HALF, 1), 0) + half
    k = jnp.concatenate(
        [
            within + ((c // 2) * first + t * second + c % 2) * (2 * HALF)
            for c in range(EACH)
        ],
        0,
    )
    return jnp.where(k == labels, 1.0, 0.0)


def own_sums_kernel(place, labels, rows, out_ref):
    for t in range(4):
        hot = is_named(t, place, labels[...]).astype(jnp.bfloat16)
        out_ref[t * TILE : (t + 1) * TILE, :] = jnp.dot(
            hot, rows[...], preferred_element_type=jnp.float32
        )


def chip_sums_kernel(place, own_labels, labels, own_sums, rows, out_ref):
    for t in range(4):
        hot = is_named(t, place, labels[...])
        sums = own_sums[t * TILE : (t + 1) * TILE, :] + jnp.dot(
            hot.astype(jnp.bfloat16), rows[...], preferred_element_type=jnp.float32
        )
        hot = hot + is_named(t, place, own_labels[...])
        counts = jnp.sum(hot, 1, keepdims=True)
        code = code_of(sums)
        coded = quantize(sums, code)
        for c in range(EACH):
            part = slice(c * HALF, (c + 1) * HALF)
            for b in range(COLS):
                out_ref[t * EACH + c, block(b), :] = coded[part, b * 128 : (b + 1) * 128]
            out_ref[t * EACH + c, BODY:CODED, :] = footer(
                to_lanes(counts[part]), to_lanes(code[part])
            )


def block(b):
    return slice(b * HALF, (b + 1) * HALF)


def add_coded(ref, at, blocks, counts):
    foot = ref[at, BODY:CODED, :].astype(jnp.float32)
    scale = scale_of(to_column(foot[1:2, :]))
    blocks = [
        blocks[b] + ref[at, block(b), :].astype(jnp.float32) * scale
        for b in range(COLS)
    ]
    return blocks, counts + foot[0:1, :]


def nothing():
    zeros = [jnp.zeros((HALF, 128), jnp.float32) for _ in range(COLS)]
    return zeros, jnp.zeros((1, 128), jnp.float32)


def code_blocks(blocks):
    most = jnp.abs(blocks[0])
    for b in range(1, COLS):
        most = jnp.maximum(most, jnp.abs(blocks[b]))
    code = code_of(most)
    return [quantize(blocks[b], code) for b in range(COLS)], to_lanes(code)


def add_and_code(ref, sources, out_ref, to):
    blocks, counts = nothing()
    for at in sources:
        blocks, counts = add_coded(ref, at, blocks, counts)
    coded, codes = code_blocks(blocks)
    for b in range(COLS):
        out_ref[to, block(b), :] = coded[b]
    out_ref[to, BODY:CODED, :] = footer(counts, codes)


def first_sums_kernel(in_ref, out_ref):
    for c in range(EACH):
        add_and_code(in_ref, range(c, 4 * EACH, EACH), out_ref, c)


def second_sums_kernel(in_ref, c0, c1, c2, c3, out_ref, centers_ref):
    add_and_code(in_ref, range(EACH), out_ref, 0)
    for i, ref in enumerate((c0, c1, c2, c3)):
        n = ref.shape[0]
        centers_ref[i * n : (i + 1) * n] = ref[...]


def refine_kernel(own, one, two, three, refined_ref, coded_ref):
    even = add_coded(two, 0, *add_coded(own, 0, *nothing()))
    odd = add_coded(three, 0, *add_coded(one, 0, *nothing()))
    counts = to_column(even[1] + odd[1])
    refined = [(even[0][b] + odd[0][b]) / counts for b in range(COLS)]
    for b in range(COLS):
        refined_ref[:, b * 128 : (b + 1) * 128] = refined[b]
    coded, codes = code_blocks(refined)
    foot = footer(jnp.zeros_like(codes), codes)
    for c in range(EACH):
        for b in range(COLS):
            coded_ref[c, block(b), :] = coded[b]
        coded_ref[c, BODY:CODED, :] = foot


def nearest(value, least):
    n = value.shape[0]
    return jnp.minimum(least, jnp.min(value.reshape(n // 8, 8, value.shape[1]), 0))


def turn_kernel(rows_ref, turned_ref, norms_ref):
    turned_ref[...] = (rows_ref[...] * jnp.bfloat16(-2.0)).T
    total = jnp.zeros((8, turned_ref.shape[1]), jnp.float32)
    for i in range(D // 16):
        wide = turned_ref[i * 16 : (i + 1) * 16, :].astype(jnp.float32)
        wide = wide * wide
        total = total + (wide[:8] + wide[8:])
    norms_ref[...] = jnp.sum(total, 0, keepdims=True) * 0.25


def old_least(turned_ref, centers, least):
    turned = turned_ref[...]
    for ref in centers:
        wide = ref[...].astype(jnp.float32)
        norm = jnp.sum(wide * wide, 1, keepdims=True)
        product = jnp.dot(ref[...], turned, preferred_element_type=jnp.float32)
        least = nearest(product + norm, least)
    return least


def old_own_kernel(turned_ref, *refs):
    *centers, out_ref = refs
    least = jnp.full(out_ref.shape, jnp.inf, jnp.float32)
    out_ref[...] = old_least(turned_ref, centers, least)


def old_other_kernel(norms_ref, turned_ref, least_ref, *refs):
    *centers, out_ref = refs
    least = old_least(turned_ref, centers, least_ref[...])
    out_ref[...] = norms_ref[...] + jnp.min(least, 0, keepdims=True)


def spread_kernel(in_ref, out_ref):
    for k in range(4):
        out_ref[k * EACH : (k + 1) * EACH] = in_ref[...]


def new_min(turned_ref, piece, least_ref):
    turned = turned_ref[...]
    least = least_ref[...]
    for t in range(CHUNKS // EACH):
        high, low, scale, norm = [], [], [], []
        for c in range(t * EACH, (t + 1) * EACH):
            wide = jnp.concatenate(
                [piece[c, block(b), :].astype(jnp.float32) for b in range(COLS)], 1
            )
            top = wide.astype(jnp.bfloat16)
            high.append(top)
            low.append((wide - top.astype(jnp.float32)).astype(jnp.bfloat16))
            foot = piece[c, BODY:CODED, :].astype(jnp.float32)
            s = scale_of(to_column(foot[1:2, :]))
            scale.append(s)
            norm.append(jnp.sum(wide * wide, 1, keepdims=True) * (s * s))
        product = jnp.dot(
            jnp.concatenate(high, 0), turned, preferred_element_type=jnp.float32
        ) + jnp.dot(jnp.concatenate(low, 0), turned, preferred_element_type=jnp.float32)
        value = product * jnp.concatenate(scale, 0) + jnp.concatenate(norm, 0)
        least = nearest(value, least)
    return least


def new_own_kernel(turned_ref, piece, least_ref, out_ref):
    out_ref[...] = new_min(turned_ref, piece, least_ref)


def new_other_kernel(
    place, turned_ref, piece, least_ref, norms_ref, own, other, out_ref, refined_ref
):
    least = new_min(turned_ref, piece, least_ref)
    out_ref[...] = norms_ref[...] + jnp.min(least, 0, keepdims=True)
    half = place[2]
    refined_ref[pl.ds(pl.multiple_of(half, HALF), HALF), :] = own[...]
    refined_ref[pl.ds(pl.multiple_of(HALF - half, HALF), HALF), :] = other[...]


def call(kernel, out_shape, *args, flops=0, moved=0, smem=0):
    specs = [
        pl.BlockSpec(memory_space=pltpu.SMEM if i < smem else pltpu.VMEM)
        for i in range(len(args))
    ]
    many = isinstance(out_shape, tuple)
    out_specs = pl.BlockSpec(memory_space=pltpu.VMEM)
    return pl.pallas_call(
        kernel,
        out_shape=out_shape,
        in_specs=specs,
        out_specs=tuple([out_specs] * len(out_shape)) if many else out_specs,
        compiler_params=pltpu.CompilerParams(vmem_limit_bytes=VMEM),
        cost_estimate=pl.CostEstimate(
            flops=flops, bytes_accessed=moved, transcendentals=0
        ),
    )(*args)


def swap(value, axis):
    return lax.ppermute(value, axis, [(0, 1), (1, 0)])


def around_z(part):
    return [part] + [
        lax.ppermute(part, "zh", [(i, (i + k) % 4) for i in range(4)])
        for k in (1, 2, 3)
    ]


def spot(core, a, b, zl):
    y, x = (b, a) if core == 0 else (a, b)
    return ((core * 4 + y) * 4 + x) * 2 + zl


def fours():
    return [
        [spot(core, a, b, 0) // 2 for a in range(4)]
        for core in range(2)
        for b in range(4)
    ]


def eights():
    return [
        [spot(core, a, b, z) for b in range(4) for z in range(2)]
        for core in range(2)
        for a in range(4)
    ]


def exchange_four(value):
    return lax.all_to_all(
        value.reshape(4, -1, 128), ("core", "y", "x"), 0, 0, axis_index_groups=fours()
    ).reshape(value.shape)


def exchange_eight(value):
    return lax.all_to_all(
        value, ("core", "y", "x", "zl"), 0, 0, axis_index_groups=eights()
    )


def around(part, turn):
    parts = [part]
    for k in (1, 3, 2):
        pairs = []
        for core in range(2):
            for a in range(4):
                for b in range(4):
                    to = ((a + k) % 4, b) if turn == 0 else (a, (b + k) % 4)
                    pairs.append((spot(core, a, b, 0) // 2, spot(core, *to, 0) // 2))
        parts.append(lax.ppermute(part, ("core", "y", "x"), pairs))
    return parts


def after(first, values):
    return lax.optimization_barrier((first, *values))[1:]


def on_device(embeddings, centers, assignment):
    n = embeddings.shape[0]
    f32, bf16, i16 = jnp.float32, jnp.bfloat16, jnp.int16
    shape = jax.ShapeDtypeStruct

    def coded(chunks):
        return shape((chunks, CODED, 128), i16)

    core = lax.axis_index("core")
    first = core == 0
    place = jnp.stack(
        [jnp.where(first, 8, 2), jnp.where(first, 2, 8), core * HALF]
    ).astype(jnp.int32)

    labels = assignment.reshape(1, n)
    other_labels = swap(labels, "core")
    other_rows = swap(embeddings, "core")

    mine = lax.dynamic_slice(centers, (core * HALF, 0), (HALF, D))
    current = jnp.concatenate([mine, swap(mine, "zl")])
    (other_rows, current) = lax.optimization_barrier((other_rows, current))

    sums = call(
        own_sums_kernel,
        shape((4 * TILE, D), f32),
        place, labels, embeddings,
        flops=2 * 1024 * n * D, moved=5 << 20, smem=1,
    )
    sums = call(
        chip_sums_kernel,
        coded(CHUNKS),
        place, labels, other_labels, sums, other_rows,
        flops=2 * 1024 * n * D, moved=6 << 20, smem=1,
    )

    sums = call(
        first_sums_kernel,
        coded(EACH),
        exchange_four(sums),
        flops=1 << 22, moved=3 << 20,
    )
    current, rows = after(sums, (current, embeddings))
    turned, norms = call(
        turn_kernel,
        (shape((D, n), bf16), shape((1, n), f32)),
        rows,
        flops=4 * n * D, moved=4 << 20,
    )
    sums, turned = lax.optimization_barrier((exchange_eight(sums), turned))
    group, current = call(
        second_sums_kernel,
        (coded(1), shape((8 * HALF, D), bf16)),
        sums, *around(current, 0),
        flops=1 << 20, moved=1 << 20,
    )
    (current,) = after(group, (current,))
    groups, current = lax.optimization_barrier((around_z(group), around(current, 1)))
    refined, code = call(
        refine_kernel,
        (shape((HALF, D), f32), coded(EACH)),
        *groups,
        flops=1 << 20, moved=1 << 20,
    )

    new = exchange_eight(code)

    current = list(after(refined, current))
    current_other = [swap(part, "core") for part in current]
    least = call(
        old_own_kernel,
        shape((8, n), f32),
        turned, *current,
        flops=2 * 1024 * n * D, moved=3 << 20,
    )
    old_min = call(
        old_other_kernel,
        shape((1, n), f32),
        norms, turned, least, *current_other,
        flops=2 * 1024 * n * D, moved=3 << 20,
    )
    refined_other = swap(refined, "core")
    new, old_min, refined_other = lax.optimization_barrier((new, old_min, refined_other))
    new = exchange_four(
        call(spread_kernel, coded(CHUNKS), new, flops=1 << 10, moved=2 << 20)
    )
    new_other = swap(new, "core")
    least = call(
        new_own_kernel,
        shape((8, n), f32),
        turned, new, jnp.full((8, n), jnp.inf, f32),
        flops=4 * 1024 * n * D, moved=3 << 20,
    )
    new_min, refined_centers = call(
        new_other_kernel,
        (shape((1, n), f32), shape((2 * HALF, D), f32)),
        place, turned, new_other, least, norms, refined, refined_other,
        flops=4 * 1024 * n * D, moved=3 << 20, smem=1,
    )
    return old_min.reshape(n), refined_centers, new_min.reshape(n)


def solution(mesh):
    fine = Mesh(mesh.devices.reshape(SIZES), AXES)
    rows = ("zh", "core") + SHARD
    return jax.shard_map(
        on_device,
        mesh=fine,
        in_specs=(P(rows, None), P(SHARD, None), P(rows, None)),
        out_specs=(P(rows), P(SHARD, None), P(rows)),
        check_vma=False,
    )
```

```python
import jax
import jax.numpy as jnp
from jax import lax
from jax.experimental import pallas as pl
from jax.experimental.pallas import tpu as pltpu
from jax.sharding import Mesh, PartitionSpec as P

AXES = ("zh", "core", "y", "x", "zl")
SIZES = (4, 2, 4, 4, 2)
SHARD = ("y", "x", "zl")

D = 768
HALF = 32
CHUNKS = 32
COLS = D // 128
BODY = COLS * HALF
CODED = BODY + 16
LIMIT = 32700.0
VMEM = 16 * 1024 * 1024


def diagonal(rows):
    r = lax.broadcasted_iota(jnp.int32, (rows, 128), 0) % HALF
    c = lax.broadcasted_iota(jnp.int32, (rows, 128), 1)
    return r == c


def to_lanes(column):
    return jnp.sum(jnp.where(diagonal(HALF), column, 0.0), 0, keepdims=True)


def to_column(row):
    return jnp.sum(jnp.where(diagonal(HALF), row, 0.0), 1, keepdims=True)


def code_of(values):
    most = jnp.max(jnp.abs(values), 1, keepdims=True)
    return jnp.ceil(jnp.log2(jnp.maximum(most, 1e-30)) * 256.0)


def quantize(values, code):
    scaled = values * (LIMIT * jnp.exp2(code * (-1.0 / 256.0)))
    return jnp.floor(scaled + 0.5).astype(jnp.int32).astype(jnp.int16)


def scale_of(code):
    return jnp.exp2(code * (1.0 / 256.0)) * (1.0 / LIMIT)


def footer(counts, codes):
    r = lax.broadcasted_iota(jnp.int32, (16, 128), 0)
    both = jnp.where(r == 0, counts, jnp.where(r == 1, codes, 0.0))
    return both.astype(jnp.int32).astype(jnp.int16)


TILE = 256
EACH = TILE // HALF


def is_named(t, place, labels):
    first, second, half = (place[i] for i in range(3))
    within = lax.broadcasted_iota(jnp.int32, (HALF, 1), 0) + half
    k = jnp.concatenate(
        [
            within + ((c // 2) * first + t * second + c % 2) * (2 * HALF)
            for c in range(EACH)
        ],
        0,
    )
    return jnp.where(k == labels, 1.0, 0.0)


def own_sums_kernel(place, labels, rows, out_ref):
    for t in range(4):
        hot = is_named(t, place, labels[...]).astype(jnp.bfloat16)
        out_ref[t * TILE : (t + 1) * TILE, :] = jnp.dot(
            hot, rows[...], preferred_element_type=jnp.float32
        )


def chip_sums_kernel(place, own_labels, labels, own_sums, rows, out_ref):
    for t in range(4):
        hot = is_named(t, place, labels[...])
        sums = own_sums[t * TILE : (t + 1) * TILE, :] + jnp.dot(
            hot.astype(jnp.bfloat16), rows[...], preferred_element_type=jnp.float32
        )
        hot = hot + is_named(t, place, own_labels[...])
        counts = jnp.sum(hot, 1, keepdims=True)
        code = code_of(sums)
        coded = quantize(sums, code)
        for c in range(EACH):
            part = slice(c * HALF, (c + 1) * HALF)
            for b in range(COLS):
                out_ref[t * EACH + c, block(b), :] = coded[part, b * 128 : (b + 1) * 128]
            out_ref[t * EACH + c, BODY:CODED, :] = footer(
                to_lanes(counts[part]), to_lanes(code[part])
            )


def block(b):
    return slice(b * HALF, (b + 1) * HALF)


def add_coded(ref, at, blocks, counts):
    foot = ref[at, BODY:CODED, :].astype(jnp.float32)
    scale = scale_of(to_column(foot[1:2, :]))
    blocks = [
        blocks[b] + ref[at, block(b), :].astype(jnp.float32) * scale
        for b in range(COLS)
    ]
    return blocks, counts + foot[0:1, :]


def nothing():
    zeros = [jnp.zeros((HALF, 128), jnp.float32) for _ in range(COLS)]
    return zeros, jnp.zeros((1, 128), jnp.float32)


def code_blocks(blocks):
    most = jnp.abs(blocks[0])
    for b in range(1, COLS):
        most = jnp.maximum(most, jnp.abs(blocks[b]))
    code = code_of(most)
    return [quantize(blocks[b], code) for b in range(COLS)], to_lanes(code)


def add_and_code(ref, sources, out_ref, to):
    blocks, counts = nothing()
    for at in sources:
        blocks, counts = add_coded(ref, at, blocks, counts)
    coded, codes = code_blocks(blocks)
    for b in range(COLS):
        out_ref[to, block(b), :] = coded[b]
    out_ref[to, BODY:CODED, :] = footer(counts, codes)


def first_sums_kernel(in_ref, out_ref):
    for c in range(EACH):
        add_and_code(in_ref, range(c, 4 * EACH, EACH), out_ref, c)


def second_sums_kernel(in_ref, c0, c1, c2, c3, out_ref, centers_ref):
    add_and_code(in_ref, range(EACH), out_ref, 0)
    for i, ref in enumerate((c0, c1, c2, c3)):
        n = ref.shape[0]
        centers_ref[i * n : (i + 1) * n] = ref[...]


def refine_kernel(own, one, two, three, refined_ref, coded_ref):
    even = add_coded(two, 0, *add_coded(own, 0, *nothing()))
    odd = add_coded(three, 0, *add_coded(one, 0, *nothing()))
    counts = to_column(even[1] + odd[1])
    refined = [(even[0][b] + odd[0][b]) / counts for b in range(COLS)]
    for b in range(COLS):
        refined_ref[:, b * 128 : (b + 1) * 128] = refined[b]
    coded, codes = code_blocks(refined)
    foot = footer(jnp.zeros_like(codes), codes)
    for c in range(EACH):
        for b in range(COLS):
            coded_ref[c, block(b), :] = coded[b]
        coded_ref[c, BODY:CODED, :] = foot


def nearest(value, least):
    n = value.shape[0]
    return jnp.minimum(least, jnp.min(value.reshape(n // 8, 8, value.shape[1]), 0))


def turn_kernel(rows_ref, turned_ref, norms_ref):
    turned_ref[...] = (rows_ref[...] * jnp.bfloat16(-2.0)).T
    total = jnp.zeros((8, turned_ref.shape[1]), jnp.float32)
    for i in range(D // 16):
        wide = turned_ref[i * 16 : (i + 1) * 16, :].astype(jnp.float32)
        wide = wide * wide
        total = total + (wide[:8] + wide[8:])
    norms_ref[...] = jnp.sum(total, 0, keepdims=True) * 0.25


def old_least(turned_ref, centers, least):
    turned = turned_ref[...]
    for ref in centers:
        wide = ref[...].astype(jnp.float32)
        norm = jnp.sum(wide * wide, 1, keepdims=True)
        product = jnp.dot(ref[...], turned, preferred_element_type=jnp.float32)
        least = nearest(product + norm, least)
    return least


def old_own_kernel(turned_ref, *refs):
    *centers, out_ref = refs
    least = jnp.full(out_ref.shape, jnp.inf, jnp.float32)
    out_ref[...] = old_least(turned_ref, centers, least)


def old_other_kernel(place, norms_ref, turned_ref, least_ref, own, other, *refs):
    *centers, out_ref, refined_ref = refs
    least = old_least(turned_ref, centers, least_ref[...])
    out_ref[...] = norms_ref[...] + jnp.min(least, 0, keepdims=True)
    half = place[2]
    refined_ref[pl.ds(pl.multiple_of(half, HALF), HALF), :] = own[...]
    refined_ref[pl.ds(pl.multiple_of(HALF - half, HALF), HALF), :] = other[...]


def new_least(turned_ref, pieces, least):
    turned = turned_ref[...]
    for piece in pieces:
        high, low, scale, norm = [], [], [], []
        for c in range(EACH):
            wide = jnp.concatenate(
                [piece[c, block(b), :].astype(jnp.float32) for b in range(COLS)], 1
            )
            top = wide.astype(jnp.bfloat16)
            high.append(top)
            low.append((wide - top.astype(jnp.float32)).astype(jnp.bfloat16))
            foot = piece[c, BODY:CODED, :].astype(jnp.float32)
            s = scale_of(to_column(foot[1:2, :]))
            scale.append(s)
            norm.append(jnp.sum(wide * wide, 1, keepdims=True) * (s * s))
        product = jnp.dot(
            jnp.concatenate(high, 0), turned, preferred_element_type=jnp.float32
        ) + jnp.dot(jnp.concatenate(low, 0), turned, preferred_element_type=jnp.float32)
        value = product * jnp.concatenate(scale, 0) + jnp.concatenate(norm, 0)
        least = nearest(value, least)
    return least


def new_kernel(turned_ref, least_ref, *refs):
    *pieces, out_ref = refs
    out_ref[...] = new_least(turned_ref, pieces, least_ref[...])


def last_kernel(turned_ref, least_ref, norms_ref, piece, out_ref):
    least = new_least(turned_ref, [piece], least_ref[...])
    out_ref[...] = norms_ref[...] + jnp.min(least, 0, keepdims=True)


def call(kernel, out_shape, *args, flops=0, moved=0, smem=0):
    specs = [
        pl.BlockSpec(memory_space=pltpu.SMEM if i < smem else pltpu.VMEM)
        for i in range(len(args))
    ]
    many = isinstance(out_shape, tuple)
    out_specs = pl.BlockSpec(memory_space=pltpu.VMEM)
    return pl.pallas_call(
        kernel,
        out_shape=out_shape,
        in_specs=specs,
        out_specs=tuple([out_specs] * len(out_shape)) if many else out_specs,
        compiler_params=pltpu.CompilerParams(vmem_limit_bytes=VMEM),
        cost_estimate=pl.CostEstimate(
            flops=flops, bytes_accessed=moved, transcendentals=0
        ),
    )(*args)


def swap(value, axis):
    return lax.ppermute(value, axis, [(0, 1), (1, 0)])


def around_z(part):
    return [part] + [
        lax.ppermute(part, "zh", [(i, (i + k) % 4) for i in range(4)])
        for k in (1, 2, 3)
    ]


def spot(core, a, b, zl):
    y, x = (b, a) if core == 0 else (a, b)
    return ((core * 4 + y) * 4 + x) * 2 + zl


def fours():
    return [
        [spot(core, a, b, 0) // 2 for a in range(4)]
        for core in range(2)
        for b in range(4)
    ]


def eights():
    return [
        [spot(core, a, b, z) for b in range(4) for z in range(2)]
        for core in range(2)
        for a in range(4)
    ]


def exchange_four(value):
    return lax.all_to_all(
        value.reshape(4, -1, 128), ("core", "y", "x"), 0, 0, axis_index_groups=fours()
    ).reshape(value.shape)


def exchange_eight(value):
    return lax.all_to_all(
        value, ("core", "y", "x", "zl"), 0, 0, axis_index_groups=eights()
    )


def around(part, turn):
    parts = [part]
    for k in (1, 3, 2):
        pairs = []
        for core in range(2):
            for a in range(4):
                for b in range(4):
                    to = ((a + k) % 4, b) if turn == 0 else (a, (b + k) % 4)
                    pairs.append((spot(core, a, b, 0) // 2, spot(core, *to, 0) // 2))
        parts.append(lax.ppermute(part, ("core", "y", "x"), pairs))
    return parts


def after(first, values):
    return lax.optimization_barrier((first, *values))[1:]


def on_device(embeddings, centers, assignment):
    n = embeddings.shape[0]
    f32, bf16, i16 = jnp.float32, jnp.bfloat16, jnp.int16
    shape = jax.ShapeDtypeStruct

    def coded(chunks):
        return shape((chunks, CODED, 128), i16)

    core = lax.axis_index("core")
    first = core == 0
    place = jnp.stack(
        [jnp.where(first, 8, 2), jnp.where(first, 2, 8), core * HALF]
    ).astype(jnp.int32)

    labels = assignment.reshape(1, n)
    other_labels = swap(labels, "core")
    other_rows = swap(embeddings, "core")

    mine = lax.dynamic_slice(centers, (core * HALF, 0), (HALF, D))
    current = jnp.concatenate([mine, swap(mine, "zl")])
    (other_rows, current) = lax.optimization_barrier((other_rows, current))

    sums = call(
        own_sums_kernel,
        shape((4 * TILE, D), f32),
        place, labels, embeddings,
        flops=2 * 1024 * n * D, moved=5 << 20, smem=1,
    )
    sums = call(
        chip_sums_kernel,
        coded(CHUNKS),
        place, labels, other_labels, sums, other_rows,
        flops=2 * 1024 * n * D, moved=6 << 20, smem=1,
    )

    sums = call(
        first_sums_kernel,
        coded(EACH),
        exchange_four(sums),
        flops=1 << 22, moved=3 << 20,
    )
    current, rows = after(sums, (current, embeddings))
    turned, norms = call(
        turn_kernel,
        (shape((D, n), bf16), shape((1, n), f32)),
        rows,
        flops=4 * n * D, moved=4 << 20,
    )
    sums, turned = lax.optimization_barrier((exchange_eight(sums), turned))
    group, current = call(
        second_sums_kernel,
        (coded(1), shape((8 * HALF, D), bf16)),
        sums, *around(current, 0),
        flops=1 << 20, moved=1 << 20,
    )
    (current,) = after(group, (current,))
    groups, current = lax.optimization_barrier((around_z(group), around(current, 1)))
    refined, code = call(
        refine_kernel,
        (shape((HALF, D), f32), coded(EACH)),
        *groups,
        flops=1 << 20, moved=1 << 20,
    )

    new = exchange_eight(code)

    current = list(after(refined, current))
    current_other = [swap(part, "core") for part in current]
    least = call(
        old_own_kernel,
        shape((8, n), f32),
        turned, *current,
        flops=2 * 1024 * n * D, moved=3 << 20,
    )
    old_min, refined_centers = call(
        old_other_kernel,
        (shape((1, n), f32), shape((2 * HALF, D), f32)),
        place, norms, turned, least, refined, swap(refined, "core"), *current_other,
        flops=2 * 1024 * n * D, moved=3 << 20, smem=1,
    )
    new, old_min = lax.optimization_barrier((new, old_min))
    new = around(new, 0)

    def take(least, *pieces):
        return call(
            new_kernel,
            shape((8, n), f32),
            turned, least, *pieces,
            flops=4 * TILE * n * D * len(pieces), moved=len(pieces) << 19,
        )

    least = jnp.full((8, n), jnp.inf, f32)
    least = take(least, new[0], swap(new[0], "core"))
    least, new[1], new[2] = lax.optimization_barrier((least, new[1], new[2]))
    swapped = [swap(new[1], "core"), swap(new[2], "core")]
    least = take(least, new[1], new[2])
    least, new[3] = lax.optimization_barrier((least, new[3]))
    last = swap(new[3], "core")
    least = take(least, *swapped, new[3])
    new_min = call(
        last_kernel,
        shape((1, n), f32),
        turned, least, norms, last,
        flops=4 * TILE * n * D, moved=1 << 19,
    )
    return old_min.reshape(n), refined_centers, new_min.reshape(n)


def solution(mesh):
    fine = Mesh(mesh.devices.reshape(SIZES), AXES)
    rows = ("zh", "core") + SHARD
    return jax.shard_map(
        on_device,
        mesh=fine,
        in_specs=(P(rows, None), P(SHARD, None), P(rows, None)),
        out_specs=(P(rows), P(SHARD, None), P(rows)),
        check_vma=False,
    )
```

```python
import jax
import jax.numpy as jnp
from jax import lax
from jax.experimental import pallas as pl
from jax.experimental.pallas import tpu as pltpu
from jax.sharding import Mesh, PartitionSpec as P

AXES = ("zh", "core", "y", "x", "zl")
SIZES = (4, 2, 4, 4, 2)
SHARD = ("y", "x", "zl")

D = 768
HALF = 32
CHUNKS = 32
COLS = D // 128
BODY = COLS * HALF
CODED = BODY + 16
LIMIT = 32700.0
VMEM = 16 * 1024 * 1024


def diagonal(rows):
    r = lax.broadcasted_iota(jnp.int32, (rows, 128), 0) % HALF
    c = lax.broadcasted_iota(jnp.int32, (rows, 128), 1)
    return r == c


def to_lanes(column):
    return jnp.sum(jnp.where(diagonal(HALF), column, 0.0), 0, keepdims=True)


def to_column(row):
    return jnp.sum(jnp.where(diagonal(HALF), row, 0.0), 1, keepdims=True)


def code_of(values):
    most = jnp.max(jnp.abs(values), 1, keepdims=True)
    return jnp.ceil(jnp.log2(jnp.maximum(most, 1e-30)) * 256.0)


def quantize(values, code):
    scaled = values * (LIMIT * jnp.exp2(code * (-1.0 / 256.0)))
    return jnp.floor(scaled + 0.5).astype(jnp.int32).astype(jnp.int16)


def scale_of(code):
    return jnp.exp2(code * (1.0 / 256.0)) * (1.0 / LIMIT)


def footer(counts, codes):
    r = lax.broadcasted_iota(jnp.int32, (16, 128), 0)
    both = jnp.where(r == 0, counts, jnp.where(r == 1, codes, 0.0))
    return both.astype(jnp.int32).astype(jnp.int16)


TILE = 256
EACH = TILE // HALF


def is_named(t, place, labels):
    first, second, half = (place[i] for i in range(3))
    within = lax.broadcasted_iota(jnp.int32, (HALF, 1), 0) + half
    k = jnp.concatenate(
        [
            within + ((c // 2) * first + t * second + c % 2) * (2 * HALF)
            for c in range(EACH)
        ],
        0,
    )
    return jnp.where(k == labels, 1.0, 0.0)


def own_sums_kernel(place, labels, rows, out_ref):
    for t in range(4):
        hot = is_named(t, place, labels[...]).astype(jnp.bfloat16)
        out_ref[t * TILE : (t + 1) * TILE, :] = jnp.dot(
            hot, rows[...], preferred_element_type=jnp.float32
        )


def chip_sums_kernel(place, own_labels, labels, own_sums, rows, out_ref):
    for t in range(4):
        hot = is_named(t, place, labels[...])
        sums = own_sums[t * TILE : (t + 1) * TILE, :] + jnp.dot(
            hot.astype(jnp.bfloat16), rows[...], preferred_element_type=jnp.float32
        )
        hot = hot + is_named(t, place, own_labels[...])
        counts = jnp.sum(hot, 1, keepdims=True)
        code = code_of(sums)
        coded = quantize(sums, code)
        for c in range(EACH):
            part = slice(c * HALF, (c + 1) * HALF)
            for b in range(COLS):
                out_ref[t * EACH + c, block(b), :] = coded[part, b * 128 : (b + 1) * 128]
            out_ref[t * EACH + c, BODY:CODED, :] = footer(
                to_lanes(counts[part]), to_lanes(code[part])
            )


def block(b):
    return slice(b * HALF, (b + 1) * HALF)


def add_coded(ref, at, blocks, counts):
    foot = ref[at, BODY:CODED, :].astype(jnp.float32)
    scale = scale_of(to_column(foot[1:2, :]))
    blocks = [
        blocks[b] + ref[at, block(b), :].astype(jnp.float32) * scale
        for b in range(COLS)
    ]
    return blocks, counts + foot[0:1, :]


def nothing():
    zeros = [jnp.zeros((HALF, 128), jnp.float32) for _ in range(COLS)]
    return zeros, jnp.zeros((1, 128), jnp.float32)


def code_blocks(blocks):
    most = jnp.abs(blocks[0])
    for b in range(1, COLS):
        most = jnp.maximum(most, jnp.abs(blocks[b]))
    code = code_of(most)
    return [quantize(blocks[b], code) for b in range(COLS)], to_lanes(code)


def add_and_code(ref, sources, out_ref, to):
    blocks, counts = nothing()
    for at in sources:
        blocks, counts = add_coded(ref, at, blocks, counts)
    coded, codes = code_blocks(blocks)
    for b in range(COLS):
        out_ref[to, block(b), :] = coded[b]
    out_ref[to, BODY:CODED, :] = footer(counts, codes)


def first_sums_kernel(in_ref, out_ref):
    for c in range(EACH):
        add_and_code(in_ref, range(c, 4 * EACH, EACH), out_ref, c)


def second_sums_kernel(in_ref, c0, c1, c2, c3, out_ref, centers_ref):
    add_and_code(in_ref, range(EACH), out_ref, 0)
    for i, ref in enumerate((c0, c1, c2, c3)):
        n = ref.shape[0]
        centers_ref[i * n : (i + 1) * n] = ref[...]


def refine_kernel(own, one, two, three, refined_ref, coded_ref):
    even = add_coded(two, 0, *add_coded(own, 0, *nothing()))
    odd = add_coded(three, 0, *add_coded(one, 0, *nothing()))
    counts = to_column(even[1] + odd[1])
    refined = [(even[0][b] + odd[0][b]) / counts for b in range(COLS)]
    for b in range(COLS):
        refined_ref[:, b * 128 : (b + 1) * 128] = refined[b]
    coded, codes = code_blocks(refined)
    foot = footer(jnp.zeros_like(codes), codes)
    for c in range(EACH):
        for b in range(COLS):
            coded_ref[c, block(b), :] = coded[b]
        coded_ref[c, BODY:CODED, :] = foot


def nearest(value, least):
    n = value.shape[0]
    return jnp.minimum(least, jnp.min(value.reshape(n // 8, 8, value.shape[1]), 0))


def turn_kernel(rows_ref, turned_ref, norms_ref):
    turned_ref[...] = (rows_ref[...] * jnp.bfloat16(-2.0)).T
    total = jnp.zeros((8, turned_ref.shape[1]), jnp.float32)
    for i in range(D // 16):
        wide = turned_ref[i * 16 : (i + 1) * 16, :].astype(jnp.float32)
        wide = wide * wide
        total = total + (wide[:8] + wide[8:])
    norms_ref[...] = jnp.sum(total, 0, keepdims=True) * 0.25


def old_least(turned_ref, centers, least):
    turned = turned_ref[...]
    for ref in centers:
        wide = ref[...].astype(jnp.float32)
        norm = jnp.sum(wide * wide, 1, keepdims=True)
        product = jnp.dot(ref[...], turned, preferred_element_type=jnp.float32)
        least = nearest(product + norm, least)
    return least


def old_own_kernel(turned_ref, *refs):
    *centers, out_ref = refs
    least = jnp.full(out_ref.shape, jnp.inf, jnp.float32)
    out_ref[...] = old_least(turned_ref, centers, least)


def old_other_kernel(place, norms_ref, turned_ref, least_ref, own, other, *refs):
    *centers, out_ref, refined_ref = refs
    least = old_least(turned_ref, centers, least_ref[...])
    out_ref[...] = norms_ref[...] + jnp.min(least, 0, keepdims=True)
    half = place[2]
    refined_ref[pl.ds(pl.multiple_of(half, HALF), HALF), :] = own[...]
    refined_ref[pl.ds(pl.multiple_of(HALF - half, HALF), HALF), :] = other[...]


def new_least(turned_ref, pieces, least):
    turned = turned_ref[...]
    for piece in pieces:
        high, low, scale, norm = [], [], [], []
        for c in range(EACH):
            wide = jnp.concatenate(
                [piece[c, block(b), :].astype(jnp.float32) for b in range(COLS)], 1
            )
            top = wide.astype(jnp.bfloat16)
            high.append(top)
            low.append((wide - top.astype(jnp.float32)).astype(jnp.bfloat16))
            foot = piece[c, BODY:CODED, :].astype(jnp.float32)
            s = scale_of(to_column(foot[1:2, :]))
            scale.append(s)
            norm.append(jnp.sum(wide * wide, 1, keepdims=True) * (s * s))
        product = jnp.dot(
            jnp.concatenate(high, 0), turned, preferred_element_type=jnp.float32
        ) + jnp.dot(jnp.concatenate(low, 0), turned, preferred_element_type=jnp.float32)
        value = product * jnp.concatenate(scale, 0) + jnp.concatenate(norm, 0)
        least = nearest(value, least)
    return least


def new_kernel(turned_ref, least_ref, *refs):
    *pieces, out_ref = refs
    out_ref[...] = new_least(turned_ref, pieces, least_ref[...])


def last_kernel(turned_ref, least_ref, norms_ref, piece, out_ref):
    least = new_least(turned_ref, [piece], least_ref[...])
    out_ref[...] = norms_ref[...] + jnp.min(least, 0, keepdims=True)


def call(kernel, out_shape, *args, flops=0, moved=0, smem=0):
    specs = [
        pl.BlockSpec(memory_space=pltpu.SMEM if i < smem else pltpu.VMEM)
        for i in range(len(args))
    ]
    many = isinstance(out_shape, tuple)
    out_specs = pl.BlockSpec(memory_space=pltpu.VMEM)
    return pl.pallas_call(
        kernel,
        out_shape=out_shape,
        in_specs=specs,
        out_specs=tuple([out_specs] * len(out_shape)) if many else out_specs,
        compiler_params=pltpu.CompilerParams(vmem_limit_bytes=VMEM),
        cost_estimate=pl.CostEstimate(
            flops=flops, bytes_accessed=moved, transcendentals=0
        ),
    )(*args)


def swap(value, axis):
    return lax.ppermute(value, axis, [(0, 1), (1, 0)])


def around_z(part):
    return [part] + [
        lax.ppermute(part, "zh", [(i, (i + k) % 4) for i in range(4)])
        for k in (1, 2, 3)
    ]


def spot(core, a, b, zl):
    y, x = (b, a) if core == 0 else (a, b)
    return ((core * 4 + y) * 4 + x) * 2 + zl


def fours():
    return [
        [spot(core, a, b, 0) // 2 for a in range(4)]
        for core in range(2)
        for b in range(4)
    ]


def eights():
    return [
        [spot(core, a, b, z) for b in range(4) for z in range(2)]
        for core in range(2)
        for a in range(4)
    ]


def exchange_four(value):
    return lax.all_to_all(
        value.reshape(4, -1, 128), ("core", "y", "x"), 0, 0, axis_index_groups=fours()
    ).reshape(value.shape)


def exchange_eight(value):
    return lax.all_to_all(
        value, ("core", "y", "x", "zl"), 0, 0, axis_index_groups=eights()
    )


def around(part, turn):
    parts = [part]
    for k in (1, 3, 2):
        pairs = []
        for core in range(2):
            for a in range(4):
                for b in range(4):
                    to = ((a + k) % 4, b) if turn == 0 else (a, (b + k) % 4)
                    pairs.append((spot(core, a, b, 0) // 2, spot(core, *to, 0) // 2))
        parts.append(lax.ppermute(part, ("core", "y", "x"), pairs))
    return parts


def after(first, values):
    return lax.optimization_barrier((first, *values))[1:]


def on_device(embeddings, centers, assignment):
    n = embeddings.shape[0]
    f32, bf16, i16 = jnp.float32, jnp.bfloat16, jnp.int16
    shape = jax.ShapeDtypeStruct

    def coded(chunks):
        return shape((chunks, CODED, 128), i16)

    core = lax.axis_index("core")
    first = core == 0
    place = jnp.stack(
        [jnp.where(first, 8, 2), jnp.where(first, 2, 8), core * HALF]
    ).astype(jnp.int32)

    labels = assignment.reshape(1, n)
    other_labels = swap(labels, "core")
    other_rows = swap(embeddings, "core")

    mine = lax.dynamic_slice(centers, (core * HALF, 0), (HALF, D))
    current = jnp.concatenate([mine, swap(mine, "zl")])
    (other_rows, current) = lax.optimization_barrier((other_rows, current))

    sums = call(
        own_sums_kernel,
        shape((4 * TILE, D), f32),
        place, labels, embeddings,
        flops=2 * 1024 * n * D, moved=5 << 20, smem=1,
    )
    sums = call(
        chip_sums_kernel,
        coded(CHUNKS),
        place, labels, other_labels, sums, other_rows,
        flops=2 * 1024 * n * D, moved=6 << 20, smem=1,
    )

    sums = call(
        first_sums_kernel,
        coded(EACH),
        exchange_four(sums),
        flops=1 << 22, moved=3 << 20,
    )
    current, rows = after(sums, (current, embeddings))
    turned, norms = call(
        turn_kernel,
        (shape((D, n), bf16), shape((1, n), f32)),
        rows,
        flops=4 * n * D, moved=4 << 20,
    )
    sums, turned = lax.optimization_barrier((exchange_eight(sums), turned))
    group, current = call(
        second_sums_kernel,
        (coded(1), shape((8 * HALF, D), bf16)),
        sums, *around(current, 0),
        flops=1 << 20, moved=1 << 20,
    )
    (current,) = after(group, (current,))
    groups, current = lax.optimization_barrier((around_z(group), around(current, 1)))
    refined, code = call(
        refine_kernel,
        (shape((HALF, D), f32), coded(EACH)),
        *groups,
        flops=1 << 20, moved=1 << 20,
    )

    new = exchange_eight(code)

    current = list(after(refined, current))
    current_other = [swap(part, "core") for part in current]
    least = call(
        old_own_kernel,
        shape((8, n), f32),
        turned, *current,
        flops=2 * 1024 * n * D, moved=3 << 20,
    )
    new, least = lax.optimization_barrier((new, least))
    old_min, refined_centers = call(
        old_other_kernel,
        (shape((1, n), f32), shape((2 * HALF, D), f32)),
        place, norms, turned, least, refined, swap(refined, "core"), *current_other,
        flops=2 * 1024 * n * D, moved=3 << 20, smem=1,
    )
    new = around(new, 0)

    def take(least, *pieces):
        return call(
            new_kernel,
            shape((8, n), f32),
            turned, least, *pieces,
            flops=4 * TILE * n * D * len(pieces), moved=len(pieces) << 19,
        )

    least = jnp.full((8, n), jnp.inf, f32)
    least = take(least, new[0], swap(new[0], "core"))
    least, old_min, new[1], new[2] = lax.optimization_barrier(
        (least, old_min, new[1], new[2])
    )
    swapped = [swap(new[1], "core"), swap(new[2], "core")]
    least = take(least, new[1], new[2])
    least, new[3] = lax.optimization_barrier((least, new[3]))
    last = swap(new[3], "core")
    least = take(least, *swapped, new[3])
    new_min = call(
        last_kernel,
        shape((1, n), f32),
        turned, least, norms, last,
        flops=4 * TILE * n * D, moved=1 << 19,
    )
    return old_min.reshape(n), refined_centers, new_min.reshape(n)


def solution(mesh):
    fine = Mesh(mesh.devices.reshape(SIZES), AXES)
    rows = ("zh", "core") + SHARD
    return jax.shard_map(
        on_device,
        mesh=fine,
        in_specs=(P(rows, None), P(SHARD, None), P(rows, None)),
        out_specs=(P(rows), P(SHARD, None), P(rows)),
        check_vma=False,
    )
```

```python
import jax
import jax.numpy as jnp
from jax import lax
from jax.experimental import pallas as pl
from jax.experimental.pallas import tpu as pltpu
from jax.sharding import Mesh, PartitionSpec as P

AXES = ("zh", "core", "y", "x", "zl")
SIZES = (4, 2, 4, 4, 2)
SHARD = ("y", "x", "zl")

D = 768
HALF = 32
CHUNKS = 32
COLS = D // 128
BODY = COLS * HALF
CODED = BODY + 16
LIMIT = 32700.0
VMEM = 16 * 1024 * 1024


def diagonal(rows):
    r = lax.broadcasted_iota(jnp.int32, (rows, 128), 0) % HALF
    c = lax.broadcasted_iota(jnp.int32, (rows, 128), 1)
    return r == c


def to_lanes(column):
    return jnp.sum(jnp.where(diagonal(HALF), column, 0.0), 0, keepdims=True)


def to_column(row):
    return jnp.sum(jnp.where(diagonal(HALF), row, 0.0), 1, keepdims=True)


def code_of(values):
    most = jnp.max(jnp.abs(values), 1, keepdims=True)
    return jnp.ceil(jnp.log2(jnp.maximum(most, 1e-30)) * 256.0)


def quantize(values, code):
    scaled = values * (LIMIT * jnp.exp2(code * (-1.0 / 256.0)))
    return jnp.floor(scaled + 0.5).astype(jnp.int32).astype(jnp.int16)


def scale_of(code):
    return jnp.exp2(code * (1.0 / 256.0)) * (1.0 / LIMIT)


def footer(counts, codes):
    r = lax.broadcasted_iota(jnp.int32, (16, 128), 0)
    both = jnp.where(r == 0, counts, jnp.where(r == 1, codes, 0.0))
    return both.astype(jnp.int32).astype(jnp.int16)


TILE = 256
EACH = TILE // HALF


def is_named(t, place, labels):
    first, second, half = (place[i] for i in range(3))
    within = lax.broadcasted_iota(jnp.int32, (HALF, 1), 0) + half
    k = jnp.concatenate(
        [
            within + ((c // 2) * first + t * second + c % 2) * (2 * HALF)
            for c in range(EACH)
        ],
        0,
    )
    return jnp.where(k == labels, 1.0, 0.0)


def own_sums_kernel(place, labels, rows, out_ref):
    for t in range(4):
        hot = is_named(t, place, labels[...]).astype(jnp.bfloat16)
        out_ref[t * TILE : (t + 1) * TILE, :] = jnp.dot(
            hot, rows[...], preferred_element_type=jnp.float32
        )


def chip_sums_kernel(place, own_labels, labels, own_sums, rows, out_ref):
    for t in range(4):
        hot = is_named(t, place, labels[...])
        sums = own_sums[t * TILE : (t + 1) * TILE, :] + jnp.dot(
            hot.astype(jnp.bfloat16), rows[...], preferred_element_type=jnp.float32
        )
        hot = hot + is_named(t, place, own_labels[...])
        counts = jnp.sum(hot, 1, keepdims=True)
        code = code_of(sums)
        coded = quantize(sums, code)
        for c in range(EACH):
            part = slice(c * HALF, (c + 1) * HALF)
            for b in range(COLS):
                out_ref[t * EACH + c, block(b), :] = coded[part, b * 128 : (b + 1) * 128]
            out_ref[t * EACH + c, BODY:CODED, :] = footer(
                to_lanes(counts[part]), to_lanes(code[part])
            )


def block(b):
    return slice(b * HALF, (b + 1) * HALF)


def add_coded(ref, at, blocks, counts):
    foot = ref[at, BODY:CODED, :].astype(jnp.float32)
    scale = scale_of(to_column(foot[1:2, :]))
    blocks = [
        blocks[b] + ref[at, block(b), :].astype(jnp.float32) * scale
        for b in range(COLS)
    ]
    return blocks, counts + foot[0:1, :]


def nothing():
    zeros = [jnp.zeros((HALF, 128), jnp.float32) for _ in range(COLS)]
    return zeros, jnp.zeros((1, 128), jnp.float32)


def code_blocks(blocks):
    most = jnp.abs(blocks[0])
    for b in range(1, COLS):
        most = jnp.maximum(most, jnp.abs(blocks[b]))
    code = code_of(most)
    return [quantize(blocks[b], code) for b in range(COLS)], to_lanes(code)


def add_and_code(ref, sources, out_ref, to):
    blocks, counts = nothing()
    for at in sources:
        blocks, counts = add_coded(ref, at, blocks, counts)
    coded, codes = code_blocks(blocks)
    for b in range(COLS):
        out_ref[to, block(b), :] = coded[b]
    out_ref[to, BODY:CODED, :] = footer(counts, codes)


def first_sums_kernel(in_ref, out_ref):
    for c in range(EACH):
        add_and_code(in_ref, range(c, 4 * EACH, EACH), out_ref, c)


def second_sums_kernel(in_ref, c0, c1, c2, c3, out_ref, centers_ref):
    add_and_code(in_ref, range(EACH), out_ref, 0)
    for i, ref in enumerate((c0, c1, c2, c3)):
        n = ref.shape[0]
        centers_ref[i * n : (i + 1) * n] = ref[...]


def refine_kernel(own, one, two, three, refined_ref, coded_ref):
    even = add_coded(two, 0, *add_coded(own, 0, *nothing()))
    odd = add_coded(three, 0, *add_coded(one, 0, *nothing()))
    counts = to_column(even[1] + odd[1])
    refined = [(even[0][b] + odd[0][b]) / counts for b in range(COLS)]
    for b in range(COLS):
        refined_ref[:, b * 128 : (b + 1) * 128] = refined[b]
    coded, codes = code_blocks(refined)
    foot = footer(jnp.zeros_like(codes), codes)
    for c in range(EACH):
        for b in range(COLS):
            coded_ref[c, block(b), :] = coded[b]
        coded_ref[c, BODY:CODED, :] = foot


def nearest(value, least):
    n = value.shape[0]
    return jnp.minimum(least, jnp.min(value.reshape(n // 8, 8, value.shape[1]), 0))


def turn_kernel(rows_ref, turned_ref, norms_ref):
    turned_ref[...] = (rows_ref[...] * jnp.bfloat16(-2.0)).T
    total = jnp.zeros((8, turned_ref.shape[1]), jnp.float32)
    for i in range(D // 16):
        wide = turned_ref[i * 16 : (i + 1) * 16, :].astype(jnp.float32)
        wide = wide * wide
        total = total + (wide[:8] + wide[8:])
    norms_ref[...] = jnp.sum(total, 0, keepdims=True) * 0.25


def old_least(turned_ref, centers, least):
    turned = turned_ref[...]
    for ref in centers:
        wide = ref[...].astype(jnp.float32)
        norm = jnp.sum(wide * wide, 1, keepdims=True)
        product = jnp.dot(ref[...], turned, preferred_element_type=jnp.float32)
        least = nearest(product + norm, least)
    return least


def old_own_kernel(turned_ref, *refs):
    *centers, out_ref = refs
    least = jnp.full(out_ref.shape, jnp.inf, jnp.float32)
    out_ref[...] = old_least(turned_ref, centers, least)


def old_other_kernel(place, norms_ref, turned_ref, least_ref, own, other, *refs):
    *centers, out_ref, refined_ref = refs
    least = old_least(turned_ref, centers, least_ref[...])
    out_ref[...] = norms_ref[...] + jnp.min(least, 0, keepdims=True)
    half = place[2]
    refined_ref[pl.ds(pl.multiple_of(half, HALF), HALF), :] = own[...]
    refined_ref[pl.ds(pl.multiple_of(HALF - half, HALF), HALF), :] = other[...]


def new_least(turned_ref, pieces, least):
    turned = turned_ref[...]
    for piece in pieces:
        high, low, scale, norm = [], [], [], []
        for c in range(EACH):
            wide = jnp.concatenate(
                [piece[c, block(b), :].astype(jnp.float32) for b in range(COLS)], 1
            )
            top = wide.astype(jnp.bfloat16)
            high.append(top)
            low.append((wide - top.astype(jnp.float32)).astype(jnp.bfloat16))
            foot = piece[c, BODY:CODED, :].astype(jnp.float32)
            s = scale_of(to_column(foot[1:2, :]))
            scale.append(s)
            norm.append(jnp.sum(wide * wide, 1, keepdims=True) * (s * s))
        product = jnp.dot(
            jnp.concatenate(high, 0), turned, preferred_element_type=jnp.float32
        ) + jnp.dot(jnp.concatenate(low, 0), turned, preferred_element_type=jnp.float32)
        value = product * jnp.concatenate(scale, 0) + jnp.concatenate(norm, 0)
        least = nearest(value, least)
    return least


def new_kernel(turned_ref, least_ref, *refs):
    *pieces, out_ref = refs
    out_ref[...] = new_least(turned_ref, pieces, least_ref[...])


def last_kernel(turned_ref, least_ref, norms_ref, piece, out_ref):
    least = new_least(turned_ref, [piece], least_ref[...])
    out_ref[...] = norms_ref[...] + jnp.min(least, 0, keepdims=True)


def call(kernel, out_shape, *args, flops=0, moved=0, smem=0):
    specs = [
        pl.BlockSpec(memory_space=pltpu.SMEM if i < smem else pltpu.VMEM)
        for i in range(len(args))
    ]
    many = isinstance(out_shape, tuple)
    out_specs = pl.BlockSpec(memory_space=pltpu.VMEM)
    return pl.pallas_call(
        kernel,
        out_shape=out_shape,
        in_specs=specs,
        out_specs=tuple([out_specs] * len(out_shape)) if many else out_specs,
        compiler_params=pltpu.CompilerParams(vmem_limit_bytes=VMEM),
        cost_estimate=pl.CostEstimate(
            flops=flops, bytes_accessed=moved, transcendentals=0
        ),
    )(*args)


def swap(value, axis):
    return lax.ppermute(value, axis, [(0, 1), (1, 0)])


def around_z(part):
    return [part] + [
        lax.ppermute(part, "zh", [(i, (i + k) % 4) for i in range(4)])
        for k in (1, 2, 3)
    ]


def spot(core, a, b, zl):
    y, x = (b, a) if core == 0 else (a, b)
    return ((core * 4 + y) * 4 + x) * 2 + zl


def fours():
    return [
        [spot(core, a, b, 0) // 2 for a in range(4)]
        for core in range(2)
        for b in range(4)
    ]


def eights():
    return [
        [spot(core, a, b, z) for b in range(4) for z in range(2)]
        for core in range(2)
        for a in range(4)
    ]


def exchange_four(value):
    return lax.all_to_all(
        value.reshape(4, -1, 128), ("core", "y", "x"), 0, 0, axis_index_groups=fours()
    ).reshape(value.shape)


def exchange_eight(value):
    return lax.all_to_all(
        value, ("core", "y", "x", "zl"), 0, 0, axis_index_groups=eights()
    )


def send(part, turn, k):
    pairs = []
    for core in range(2):
        for a in range(4):
            for b in range(4):
                to = ((a + k) % 4, b) if turn == 0 else (a, (b + k) % 4)
                pairs.append((spot(core, a, b, 0) // 2, spot(core, *to, 0) // 2))
    return lax.ppermute(part, ("core", "y", "x"), pairs)


def around(part, turn):
    return [part] + [send(part, turn, k) for k in (1, 3, 2)]


def after(first, values):
    return lax.optimization_barrier((first, *values))[1:]


def on_device(embeddings, centers, assignment):
    n = embeddings.shape[0]
    f32, bf16, i16 = jnp.float32, jnp.bfloat16, jnp.int16
    shape = jax.ShapeDtypeStruct

    def coded(chunks):
        return shape((chunks, CODED, 128), i16)

    core = lax.axis_index("core")
    first = core == 0
    place = jnp.stack(
        [jnp.where(first, 8, 2), jnp.where(first, 2, 8), core * HALF]
    ).astype(jnp.int32)

    labels = assignment.reshape(1, n)
    other_labels = swap(labels, "core")
    other_rows = swap(embeddings, "core")

    mine = lax.dynamic_slice(centers, (core * HALF, 0), (HALF, D))
    current = jnp.concatenate([mine, swap(mine, "zl")])
    (other_rows, current) = lax.optimization_barrier((other_rows, current))

    sums = call(
        own_sums_kernel,
        shape((4 * TILE, D), f32),
        place, labels, embeddings,
        flops=2 * 1024 * n * D, moved=5 << 20, smem=1,
    )
    sums = call(
        chip_sums_kernel,
        coded(CHUNKS),
        place, labels, other_labels, sums, other_rows,
        flops=2 * 1024 * n * D, moved=6 << 20, smem=1,
    )

    sums = call(
        first_sums_kernel,
        coded(EACH),
        exchange_four(sums),
        flops=1 << 22, moved=3 << 20,
    )
    current, rows = after(sums, (current, embeddings))
    turned, norms = call(
        turn_kernel,
        (shape((D, n), bf16), shape((1, n), f32)),
        rows,
        flops=4 * n * D, moved=4 << 20,
    )
    sums, turned = lax.optimization_barrier((exchange_eight(sums), turned))
    group, current = call(
        second_sums_kernel,
        (coded(1), shape((8 * HALF, D), bf16)),
        sums, *around(current, 0),
        flops=1 << 20, moved=1 << 20,
    )
    (current,) = after(group, (current,))
    groups, current = lax.optimization_barrier((around_z(group), around(current, 1)))
    refined, code = call(
        refine_kernel,
        (shape((HALF, D), f32), coded(EACH)),
        *groups,
        flops=1 << 20, moved=1 << 20,
    )

    new = exchange_eight(code)

    current = list(after(refined, current))
    current_other = [swap(part, "core") for part in current]
    least = call(
        old_own_kernel,
        shape((8, n), f32),
        turned, *current,
        flops=2 * 1024 * n * D, moved=3 << 20,
    )
    new, least = lax.optimization_barrier((new, least))
    old_min, refined_centers = call(
        old_other_kernel,
        (shape((1, n), f32), shape((2 * HALF, D), f32)),
        place, norms, turned, least, refined, swap(refined, "core"), *current_other,
        flops=2 * 1024 * n * D, moved=3 << 20, smem=1,
    )
    def take(least, *pieces):
        return call(
            new_kernel,
            shape((8, n), f32),
            turned, least, *pieces,
            flops=4 * TILE * n * D * len(pieces), moved=len(pieces) << 19,
        )

    near = [send(new, 0, 1), send(new, 0, 3)]
    (far,) = after(old_min, (new,))
    far = send(far, 0, 2)
    least = jnp.full((8, n), jnp.inf, f32)
    least = take(least, new, swap(new, "core"))
    least, old_min, *near = lax.optimization_barrier((least, old_min, *near))
    swapped = [swap(part, "core") for part in near]
    least = take(least, *near)
    least = take(least, *swapped)
    least, far = lax.optimization_barrier((least, far))
    last = swap(far, "core")
    least = take(least, far)
    new_min = call(
        last_kernel,
        shape((1, n), f32),
        turned, least, norms, last,
        flops=4 * TILE * n * D, moved=1 << 19,
    )
    return old_min.reshape(n), refined_centers, new_min.reshape(n)


def solution(mesh):
    fine = Mesh(mesh.devices.reshape(SIZES), AXES)
    rows = ("zh", "core") + SHARD
    return jax.shard_map(
        on_device,
        mesh=fine,
        in_specs=(P(rows, None), P(SHARD, None), P(rows, None)),
        out_specs=(P(rows), P(SHARD, None), P(rows)),
        check_vma=False,
    )
```

```python
import jax
import jax.numpy as jnp
from jax import lax
from jax.experimental import pallas as pl
from jax.experimental.pallas import tpu as pltpu
from jax.sharding import Mesh, PartitionSpec as P

AXES = ("zh", "core", "y", "x", "zl")
SIZES = (4, 2, 4, 4, 2)
SHARD = ("y", "x", "zl")

D = 768
HALF = 32
CHUNKS = 32
COLS = D // 128
BODY = COLS * HALF
CODED = BODY + 16
LIMIT = 32700.0
VMEM = 16 * 1024 * 1024


def diagonal(rows):
    r = lax.broadcasted_iota(jnp.int32, (rows, 128), 0) % HALF
    c = lax.broadcasted_iota(jnp.int32, (rows, 128), 1)
    return r == c


def to_lanes(column):
    return jnp.sum(jnp.where(diagonal(HALF), column, 0.0), 0, keepdims=True)


def to_column(row):
    return jnp.sum(jnp.where(diagonal(HALF), row, 0.0), 1, keepdims=True)


def code_of(values):
    most = jnp.max(jnp.abs(values), 1, keepdims=True)
    return jnp.ceil(jnp.log2(jnp.maximum(most, 1e-30)) * 256.0)


def quantize(values, code):
    scaled = values * (LIMIT * jnp.exp2(code * (-1.0 / 256.0)))
    return jnp.floor(scaled + 0.5).astype(jnp.int32).astype(jnp.int16)


def scale_of(code):
    return jnp.exp2(code * (1.0 / 256.0)) * (1.0 / LIMIT)


def footer(counts, codes):
    r = lax.broadcasted_iota(jnp.int32, (16, 128), 0)
    both = jnp.where(r == 0, counts, jnp.where(r == 1, codes, 0.0))
    return both.astype(jnp.int32).astype(jnp.int16)


TILE = 256
EACH = TILE // HALF


def is_named(t, place, labels):
    first, second, half = (place[i] for i in range(3))
    within = lax.broadcasted_iota(jnp.int32, (HALF, 1), 0) + half
    k = jnp.concatenate(
        [
            within + ((c // 2) * first + t * second + c % 2) * (2 * HALF)
            for c in range(EACH)
        ],
        0,
    )
    return jnp.where(k == labels, 1.0, 0.0)


def own_sums_kernel(place, labels, rows, out_ref):
    for t in range(4):
        hot = is_named(t, place, labels[...]).astype(jnp.bfloat16)
        out_ref[t * TILE : (t + 1) * TILE, :] = jnp.dot(
            hot, rows[...], preferred_element_type=jnp.float32
        )


def chip_sums_kernel(place, own_labels, labels, own_sums, rows, out_ref):
    for t in range(4):
        hot = is_named(t, place, labels[...])
        sums = own_sums[t * TILE : (t + 1) * TILE, :] + jnp.dot(
            hot.astype(jnp.bfloat16), rows[...], preferred_element_type=jnp.float32
        )
        hot = hot + is_named(t, place, own_labels[...])
        counts = jnp.sum(hot, 1, keepdims=True)
        code = code_of(sums)
        coded = quantize(sums, code)
        for c in range(EACH):
            part = slice(c * HALF, (c + 1) * HALF)
            for b in range(COLS):
                out_ref[t * EACH + c, block(b), :] = coded[part, b * 128 : (b + 1) * 128]
            out_ref[t * EACH + c, BODY:CODED, :] = footer(
                to_lanes(counts[part]), to_lanes(code[part])
            )


def block(b):
    return slice(b * HALF, (b + 1) * HALF)


def add_coded(ref, at, blocks, counts):
    foot = ref[at, BODY:CODED, :].astype(jnp.float32)
    scale = scale_of(to_column(foot[1:2, :]))
    blocks = [
        blocks[b] + ref[at, block(b), :].astype(jnp.float32) * scale
        for b in range(COLS)
    ]
    return blocks, counts + foot[0:1, :]


def nothing():
    zeros = [jnp.zeros((HALF, 128), jnp.float32) for _ in range(COLS)]
    return zeros, jnp.zeros((1, 128), jnp.float32)


def code_blocks(blocks):
    most = jnp.abs(blocks[0])
    for b in range(1, COLS):
        most = jnp.maximum(most, jnp.abs(blocks[b]))
    code = code_of(most)
    return [quantize(blocks[b], code) for b in range(COLS)], to_lanes(code)


def add_and_code(ref, sources, out_ref, to):
    blocks, counts = nothing()
    for at in sources:
        blocks, counts = add_coded(ref, at, blocks, counts)
    coded, codes = code_blocks(blocks)
    for b in range(COLS):
        out_ref[to, block(b), :] = coded[b]
    out_ref[to, BODY:CODED, :] = footer(counts, codes)


def first_sums_kernel(in_ref, out_ref):
    for c in range(EACH):
        add_and_code(in_ref, range(c, 4 * EACH, EACH), out_ref, c)


def second_sums_kernel(in_ref, c0, c1, c2, c3, out_ref, centers_ref):
    add_and_code(in_ref, range(EACH), out_ref, 0)
    for i, ref in enumerate((c0, c1, c2, c3)):
        n = ref.shape[0]
        centers_ref[i * n : (i + 1) * n] = ref[...]


def refine_kernel(groups, refined_ref, coded_ref):
    blocks, counts = nothing()
    for g in range(groups.shape[0]):
        blocks, counts = add_coded(groups, g, blocks, counts)
    counts = to_column(counts)
    refined = [blocks[b] / counts for b in range(COLS)]
    for b in range(COLS):
        refined_ref[:, b * 128 : (b + 1) * 128] = refined[b]
    coded, codes = code_blocks(refined)
    foot = footer(jnp.zeros_like(codes), codes)
    for c in range(EACH):
        for b in range(COLS):
            coded_ref[c, block(b), :] = coded[b]
        coded_ref[c, BODY:CODED, :] = foot


def nearest(value, least):
    n = value.shape[0]
    return jnp.minimum(least, jnp.min(value.reshape(n // 8, 8, value.shape[1]), 0))


def turn_kernel(rows_ref, turned_ref, norms_ref):
    turned_ref[...] = (rows_ref[...] * jnp.bfloat16(-2.0)).T
    total = jnp.zeros((8, turned_ref.shape[1]), jnp.float32)
    for i in range(D // 16):
        wide = turned_ref[i * 16 : (i + 1) * 16, :].astype(jnp.float32)
        wide = wide * wide
        total = total + (wide[:8] + wide[8:])
    norms_ref[...] = jnp.sum(total, 0, keepdims=True) * 0.25


def old_least(turned_ref, centers, least):
    turned = turned_ref[...]
    for ref in centers:
        wide = ref[...].astype(jnp.float32)
        norm = jnp.sum(wide * wide, 1, keepdims=True)
        product = jnp.dot(ref[...], turned, preferred_element_type=jnp.float32)
        least = nearest(product + norm, least)
    return least


def old_own_kernel(turned_ref, *refs):
    *centers, out_ref = refs
    least = jnp.full(out_ref.shape, jnp.inf, jnp.float32)
    out_ref[...] = old_least(turned_ref, centers, least)


def old_other_kernel(place, norms_ref, turned_ref, least_ref, own, other, *refs):
    *centers, out_ref, refined_ref = refs
    least = old_least(turned_ref, centers, least_ref[...])
    out_ref[...] = norms_ref[...] + jnp.min(least, 0, keepdims=True)
    half = place[2]
    refined_ref[pl.ds(pl.multiple_of(half, HALF), HALF), :] = own[...]
    refined_ref[pl.ds(pl.multiple_of(HALF - half, HALF), HALF), :] = other[...]


def new_least(turned_ref, pieces, least):
    turned = turned_ref[...]
    for piece in pieces:
        high, low, scale, norm = [], [], [], []
        for c in range(EACH):
            wide = jnp.concatenate(
                [piece[c, block(b), :].astype(jnp.float32) for b in range(COLS)], 1
            )
            top = wide.astype(jnp.bfloat16)
            high.append(top)
            low.append((wide - top.astype(jnp.float32)).astype(jnp.bfloat16))
            foot = piece[c, BODY:CODED, :].astype(jnp.float32)
            s = scale_of(to_column(foot[1:2, :]))
            scale.append(s)
            norm.append(jnp.sum(wide * wide, 1, keepdims=True) * (s * s))
        product = jnp.dot(
            jnp.concatenate(high, 0), turned, preferred_element_type=jnp.float32
        ) + jnp.dot(jnp.concatenate(low, 0), turned, preferred_element_type=jnp.float32)
        value = product * jnp.concatenate(scale, 0) + jnp.concatenate(norm, 0)
        least = nearest(value, least)
    return least


def new_kernel(turned_ref, least_ref, *refs):
    *pieces, out_ref = refs
    out_ref[...] = new_least(turned_ref, pieces, least_ref[...])


def last_kernel(turned_ref, least_ref, norms_ref, piece, out_ref):
    least = new_least(turned_ref, [piece], least_ref[...])
    out_ref[...] = norms_ref[...] + jnp.min(least, 0, keepdims=True)


def call(kernel, out_shape, *args, flops=0, moved=0, smem=0):
    specs = [
        pl.BlockSpec(memory_space=pltpu.SMEM if i < smem else pltpu.VMEM)
        for i in range(len(args))
    ]
    many = isinstance(out_shape, tuple)
    out_specs = pl.BlockSpec(memory_space=pltpu.VMEM)
    return pl.pallas_call(
        kernel,
        out_shape=out_shape,
        in_specs=specs,
        out_specs=tuple([out_specs] * len(out_shape)) if many else out_specs,
        compiler_params=pltpu.CompilerParams(vmem_limit_bytes=VMEM),
        cost_estimate=pl.CostEstimate(
            flops=flops, bytes_accessed=moved, transcendentals=0
        ),
    )(*args)


def swap(value, axis):
    return lax.ppermute(value, axis, [(0, 1), (1, 0)])


def all_of_z(part):
    return lax.all_to_all(jnp.broadcast_to(part, (4, *part.shape[1:])), "zh", 0, 0)


def spot(core, a, b, zl):
    y, x = (b, a) if core == 0 else (a, b)
    return ((core * 4 + y) * 4 + x) * 2 + zl


def fours():
    return [
        [spot(core, a, b, 0) // 2 for a in range(4)]
        for core in range(2)
        for b in range(4)
    ]


def eights():
    return [
        [spot(core, a, b, z) for b in range(4) for z in range(2)]
        for core in range(2)
        for a in range(4)
    ]


def exchange_four(value):
    return lax.all_to_all(
        value.reshape(4, -1, 128), ("core", "y", "x"), 0, 0, axis_index_groups=fours()
    ).reshape(value.shape)


def exchange_eight(value):
    return lax.all_to_all(
        value, ("core", "y", "x", "zl"), 0, 0, axis_index_groups=eights()
    )


def around(part, turn):
    parts = [part]
    for k in (1, 3, 2):
        pairs = []
        for core in range(2):
            for a in range(4):
                for b in range(4):
                    to = ((a + k) % 4, b) if turn == 0 else (a, (b + k) % 4)
                    pairs.append((spot(core, a, b, 0) // 2, spot(core, *to, 0) // 2))
        parts.append(lax.ppermute(part, ("core", "y", "x"), pairs))
    return parts


def after(first, values):
    return lax.optimization_barrier((first, *values))[1:]


def on_device(embeddings, centers, assignment):
    n = embeddings.shape[0]
    f32, bf16, i16 = jnp.float32, jnp.bfloat16, jnp.int16
    shape = jax.ShapeDtypeStruct

    def coded(chunks):
        return shape((chunks, CODED, 128), i16)

    core = lax.axis_index("core")
    first = core == 0
    place = jnp.stack(
        [jnp.where(first, 8, 2), jnp.where(first, 2, 8), core * HALF]
    ).astype(jnp.int32)

    labels = assignment.reshape(1, n)
    other_labels = swap(labels, "core")
    other_rows = swap(embeddings, "core")

    mine = lax.dynamic_slice(centers, (core * HALF, 0), (HALF, D))
    current = jnp.concatenate([mine, swap(mine, "zl")])
    (other_rows, current) = lax.optimization_barrier((other_rows, current))

    sums = call(
        own_sums_kernel,
        shape((4 * TILE, D), f32),
        place, labels, embeddings,
        flops=2 * 1024 * n * D, moved=5 << 20, smem=1,
    )
    sums = call(
        chip_sums_kernel,
        coded(CHUNKS),
        place, labels, other_labels, sums, other_rows,
        flops=2 * 1024 * n * D, moved=6 << 20, smem=1,
    )

    sums = call(
        first_sums_kernel,
        coded(EACH),
        exchange_four(sums),
        flops=1 << 22, moved=3 << 20,
    )
    current, rows = after(sums, (current, embeddings))
    turned, norms = call(
        turn_kernel,
        (shape((D, n), bf16), shape((1, n), f32)),
        rows,
        flops=4 * n * D, moved=4 << 20,
    )
    sums, turned = lax.optimization_barrier((exchange_eight(sums), turned))
    group, current = call(
        second_sums_kernel,
        (coded(1), shape((8 * HALF, D), bf16)),
        sums, *around(current, 0),
        flops=1 << 20, moved=1 << 20,
    )
    (current,) = after(group, (current,))
    groups, current = lax.optimization_barrier((all_of_z(group), around(current, 1)))
    refined, code = call(
        refine_kernel,
        (shape((HALF, D), f32), coded(EACH)),
        groups,
        flops=1 << 20, moved=1 << 20,
    )

    new = exchange_eight(code)

    current = list(after(refined, current))
    current_other = [swap(part, "core") for part in current]
    least = call(
        old_own_kernel,
        shape((8, n), f32),
        turned, *current,
        flops=2 * 1024 * n * D, moved=3 << 20,
    )
    new, least = lax.optimization_barrier((new, least))
    old_min, refined_centers = call(
        old_other_kernel,
        (shape((1, n), f32), shape((2 * HALF, D), f32)),
        place, norms, turned, least, refined, swap(refined, "core"), *current_other,
        flops=2 * 1024 * n * D, moved=3 << 20, smem=1,
    )
    new = around(new, 0)

    def take(least, *pieces):
        return call(
            new_kernel,
            shape((8, n), f32),
            turned, least, *pieces,
            flops=4 * TILE * n * D * len(pieces), moved=len(pieces) << 19,
        )

    least = jnp.full((8, n), jnp.inf, f32)
    least = take(least, new[0], swap(new[0], "core"))
    least, old_min, new[1], new[2] = lax.optimization_barrier(
        (least, old_min, new[1], new[2])
    )
    swapped = [swap(new[1], "core"), swap(new[2], "core")]
    least = take(least, new[1], new[2])
    least, new[3] = lax.optimization_barrier((least, new[3]))
    last = swap(new[3], "core")
    least = take(least, *swapped, new[3])
    new_min = call(
        last_kernel,
        shape((1, n), f32),
        turned, least, norms, last,
        flops=4 * TILE * n * D, moved=1 << 19,
    )
    return old_min.reshape(n), refined_centers, new_min.reshape(n)


def solution(mesh):
    fine = Mesh(mesh.devices.reshape(SIZES), AXES)
    rows = ("zh", "core") + SHARD
    return jax.shard_map(
        on_device,
        mesh=fine,
        in_specs=(P(rows, None), P(SHARD, None), P(rows, None)),
        out_specs=(P(rows), P(SHARD, None), P(rows)),
        check_vma=False,
    )
```
